32 devices in a mesh: dp: 16 (over z, x, core), tensor: 2 (over y).
Axes of the slice: x: 2, y: 2, z: 4, core: 2. Of those that a mesh axis runs over, the one named last changes fastest.
Arguments:
- frames_in: bfloat16 [16, 256, 1536], P('dp', 'tensor'), may hold values from -6 to 6
- lengths: int32 [16], P('dp'), may hold values from 85 to 256, as said below
- ln_gain: float32 [1536], replicated, may hold values from 0.5 to 2
- ln_bias: float32 [1536], replicated, may hold values from -3 to 3
- glu_weight: bfloat16 [2, 1536, 1536], P(None, 'tensor'), may hold values from -0.15625 to 0.15625
- conv_kernel: bfloat16 [32, 1536], P(None, 'tensor'), may hold values from -1 to 1
- bn_gain: float32 [1536], P('tensor'), may hold values from 0.5 to 2
- bn_bias: float32 [1536], P('tensor'), may hold values from -3 to 3
- out_weight: bfloat16 [1536, 1536], P('tensor'), may hold values from -0.15625 to 0.15625
Outputs:
- frames_out: bfloat16 [16, 256, 1536], P('dp', 'tensor')
The draws below stay inside these ranges and needn't reach their ends.
Inputs may be any that keep to these rules, and one draw needn't show every extreme that they name: `lengths`: each span's length lies between 85 and 256; some span is full in every draw.
All inputs are finite; a program needn't handle non-finite values.
Results may differ from the reference program's by a relative error of at most 0.0095.
Values may be sent and summed in bfloat16 or wider, within the bound.
No kernel may reach another device: no remote copies, remote signals or barrier semaphores. Data moves between devices by JAX's collectives and lax.ppermute only.
A program may use at most 64 MiB of HBM per device.

```python
import math
import jax
import jax.numpy as jnp
from jax import lax

D = 1536
KERNEL = 32
FRAMES = 256
SPANS = 16


def draw_lengths(key, part):
    index = jnp.arange(SPANS, dtype=jnp.int32)
    low = FRAMES // 3
    base = low + index * (FRAMES - low) // max(SPANS - 1, 1)
    jitter = jax.random.randint(key, (SPANS,), 0, FRAMES // 8 + 1)
    values = jnp.minimum(base + jitter, FRAMES)
    where_full = jax.random.randint(jax.random.fold_in(key, 7), (), 0, SPANS)
    return values.at[where_full].set(FRAMES).astype(jnp.int32)


def draw_frames_in(key, part):
    key_base = jax.random.fold_in(key, 11)
    key_gain = jax.random.fold_in(key, 12)
    key_offset = jax.random.fold_in(key, 13)
    base = jax.random.normal(key_base, (SPANS, FRAMES, D), jnp.float32)
    spread = 0.7
    shift = 0.5
    gains = jnp.exp(jax.random.uniform(key_gain, (SPANS, 1, D), jnp.float32, -spread, spread))
    offsets = shift * jax.random.normal(key_offset, (SPANS, 1, D), jnp.float32)
    values = jnp.clip(base * gains + offsets, -6.0, 6.0)
    return values.astype(jnp.bfloat16)


def level_of(key, dims, split, least, high):
    def one(dim, blocks):
        steps = jax.random.uniform(jax.random.fold_in(jax.random.fold_in(key, 6), dim), (blocks,), jnp.float32, least / len(split), high / len(split))
        return jnp.repeat(jnp.exp(steps), dims[dim] // blocks).reshape((-1,) + (1,) * (len(dims) - dim - 1))

    loudness = one(*split[0])
    for cut in split[1:]:
        loudness = loudness * one(*cut)
    return loudness


def bell_draw(key, extent, deviation, most, pieces=(), kind=jnp.bfloat16):
    drawn = jax.random.normal(key, extent, jnp.float32) * deviation
    if len(pieces) > 0:
        drawn = level_of(key, extent, pieces, -0.22, 0.18) * drawn
    return jnp.clip(drawn, min=-most, max=most).astype(kind)


def setup_inputs(seed: int = 0) -> dict:
    arg_keys = jax.random.split(jax.random.key(seed), 10)
    frames_in = draw_frames_in(jax.random.fold_in(arg_keys[9], 71), 0)
    lengths = draw_lengths(jax.random.fold_in(arg_keys[9], 71), 0)
    ln_gain = jnp.clip(jnp.exp(jax.random.uniform(arg_keys[2], (D,), jnp.float32, math.log(0.5), math.log(2.0))), 0.5, 2.0)
    ln_bias = bell_draw(arg_keys[3], (D,), 0.5, 3.0, (), jnp.float32)
    glu_weight = bell_draw(arg_keys[4], (2, D, D), D ** -0.5, 0.15625, ((1, 2),))
    conv_kernel = bell_draw(arg_keys[5], (KERNEL, D), KERNEL ** -0.5, 1.0, ((1, 2),))
    bn_gain = jnp.clip(jnp.exp(math.log(2.0) - 1.3862944 * jax.random.uniform(arg_keys[6], (D,), jnp.float32) ** level_of(arg_keys[6], (D,), ((0, 2),), -0.2, 0.2)), 0.5, 2.0)
    bn_bias = bell_draw(arg_keys[7], (D,), 0.5, 3.0, ((0, 2),), jnp.float32)
    out_weight = bell_draw(arg_keys[8], (D, D), D ** -0.5, 0.15625, ((0, 2),))
    return {"frames_in": frames_in, "lengths": lengths, "ln_gain": ln_gain, "ln_bias": ln_bias, "glu_weight": glu_weight, "conv_kernel": conv_kernel, "bn_gain": bn_gain, "bn_bias": bn_bias, "out_weight": out_weight}


def layer_norm(rows, gain, bias):
    values = rows.astype(jnp.float32)
    center = lax.optimization_barrier(jnp.mean(values, axis=-1, keepdims=True))
    spread = lax.optimization_barrier(jnp.mean((values - center) ** 2, axis=-1, keepdims=True))
    return ((values - center) * lax.rsqrt(spread + 1e-05) * gain + bias).astype(jnp.bfloat16)

def span_conv(item, ln_gain, ln_bias, glu_weight, conv_kernel):
    rows, length = item
    normed = layer_norm(rows, ln_gain, ln_bias)
    value = jnp.dot(normed, glu_weight[0].T, preferred_element_type=jnp.float32)
    gate = jnp.dot(normed, glu_weight[1].T, preferred_element_type=jnp.float32)
    glu = (value * jax.nn.sigmoid(gate)).astype(jnp.bfloat16)
    valid = jnp.arange(rows.shape[0], dtype=jnp.int32) < length
    glu = jnp.where(valid[:, None], glu, jnp.zeros_like(glu)).astype(jnp.float32)
    padded = jnp.pad(glu, ((15, KERNEL - 16), (0, 0)))
    taps = conv_kernel.astype(jnp.float32)
    total = jnp.zeros_like(glu)
    for k in range(KERNEL):
        total = total + padded[k:k + rows.shape[0]] * taps[k]
    return total

def reference(frames_in, lengths, ln_gain, ln_bias, glu_weight, conv_kernel, bn_gain, bn_bias, out_weight):
    conv = lax.map(lambda item: span_conv(item, ln_gain, ln_bias, glu_weight, conv_kernel), (frames_in, lengths))
    valid = (jnp.arange(FRAMES, dtype=jnp.int32)[None, :] < lengths[:, None]).astype(jnp.float32)[:, :, None]
    count = jnp.sum(lengths.astype(jnp.float32))
    mean = lax.optimization_barrier(jnp.sum(conv * valid, axis=(0, 1))) / count
    var = lax.optimization_barrier(jnp.sum(((conv - mean) * valid) ** 2, axis=(0, 1))) / count
    scale = lax.rsqrt(var + 1e-05) * bn_gain

    def finish(item):
        rows, conv_rows = item
        z = (conv_rows - mean) * scale + bn_bias
        act = (z * jax.nn.sigmoid(z)).astype(jnp.bfloat16)
        branch = jnp.dot(act, out_weight.T, preferred_element_type=jnp.float32)
        return (rows.astype(jnp.float32) + branch).astype(jnp.bfloat16)
    return lax.map(finish, (frames_in, conv))
```

```python
import functools

import jax
import jax.numpy as jnp
from jax import lax
from jax.experimental import pallas as pl
from jax.experimental.pallas import tpu as pltpu
from jax.sharding import PartitionSpec as P

KERNEL = 32
HEAD = 16
LANES = 128
F32 = jnp.float32
BF16 = jnp.bfloat16

VMEM = pl.BlockSpec(memory_space=pltpu.VMEM)
SMEM = pl.BlockSpec(memory_space=pltpu.SMEM)


def contract_last(left, right):
    return lax.dot_general(
        left, right, (((1,), (1,)), ((), ())), preferred_element_type=F32
    )


def layer_norm(rows, gain, bias):
    values = rows.astype(F32)
    center = jnp.mean(values, axis=-1, keepdims=True)
    values = values - center
    spread = jnp.mean(values * values, axis=-1, keepdims=True)
    return (values * lax.rsqrt(spread + 1e-05) * gain + bias).astype(BF16)


def swish(z):
    return z * jax.nn.sigmoid(z)


def cuts(width, most):
    step = most if width % most == 0 else width
    return [slice(at, at + step) for at in range(0, width, step)]


def glu_of(normed, weight_ref, cut, keep):
    value = contract_last(normed, weight_ref[0, cut, :])
    gate = contract_last(normed, weight_ref[1, cut, :])
    glu = (value * jax.nn.sigmoid(gate)).astype(BF16)
    return jnp.where(keep, glu.astype(F32), 0.0)


def own_rows_valid(first, rows, length):
    index = first + lax.broadcasted_iota(jnp.int32, (rows, 1), 0)
    return index < length


def glu_kernel(shift, parts, where_ref, rows_ref, gain_ref, bias_ref, weight_ref, glu_ref):
    rows, chans = glu_ref.shape
    first = lax.rem(where_ref[0] + shift, parts) * rows
    keep = own_rows_valid(first, rows, where_ref[1])
    normed = layer_norm(rows_ref[...], gain_ref[...], bias_ref[...])
    for cut in cuts(chans, 256):
        glu_ref[:, cut] = glu_of(normed, weight_ref, cut, keep).astype(BF16)


def conv_rows(padded_ref, taps_ref, at, rows, cut):
    total = jnp.zeros((rows, cut.stop - cut.start), F32)
    for offset in range(8):
        last = 4 if offset == 0 else 3
        seen = padded_ref[at + offset : at + offset + rows + 8 * last, cut]
        for step in range(last + 1):
            tap = 8 * step + offset - 1
            if tap >= 0:
                total += seen[8 * step : 8 * step + rows] * taps_ref[tap : tap + 1, cut]
    return total


def fill_ends(padded_ref, cut):
    total = padded_ref.shape[0]
    width = cut.stop - cut.start
    padded_ref[0:HEAD, cut] = jnp.zeros((HEAD, width), F32)
    padded_ref[total - HEAD : total, cut] = jnp.zeros((HEAD, width), F32)


def place_block(padded_ref, block, slot, rows, cut):
    at = pl.multiple_of(HEAD + slot * rows, 16)
    padded_ref[pl.ds(at, rows), cut] = block


def last_block_kernel(
    parts, where_ref, rows_ref, gain_ref, bias_ref, weight_ref, early_ref, taps_ref,
    glu_ref, conv_ref, sums_ref, padded_ref,
):
    rows, chans = glu_ref.shape
    total_rows = conv_ref.shape[0]
    own, length = where_ref[0], where_ref[1]
    slot = lax.rem(own + parts - 1, parts)
    keep = own_rows_valid(slot * rows, rows, length)
    count = length.astype(F32)
    normed = layer_norm(rows_ref[...], gain_ref[...], bias_ref[...])
    valid = own_rows_valid(0, total_rows, length).astype(F32)
    for wide in cuts(chans, 256):
        glu = glu_of(normed, weight_ref, wide, keep)
        glu_ref[:, wide] = glu.astype(BF16)
        fill_ends(padded_ref, wide)
        place_block(padded_ref, glu, slot, rows, wide)
        for shift in range(parts - 1):
            place = lax.rem(own + shift, parts)
            place_block(padded_ref, early_ref[shift, :, wide].astype(F32), place, rows, wide)
        span = wide.stop - wide.start
        for narrow in cuts(span, LANES):
            cut = slice(wide.start + narrow.start, wide.start + narrow.stop)
            sums = jnp.zeros((1, cut.stop - cut.start), F32)
            for at in range(0, total_rows, rows):
                conv = conv_rows(padded_ref, taps_ref, at, rows, cut)
                conv_ref[at : at + rows, cut] = conv
                sums += jnp.sum(conv * valid[at : at + rows], axis=0, keepdims=True)
            mean = sums / count
            squares = jnp.zeros_like(sums)
            for at in range(0, total_rows, rows):
                off = (conv_ref[at : at + rows, cut] - mean) * valid[at : at + rows]
                squares += jnp.sum(off * off, axis=0, keepdims=True)
            sums_ref[:, cut] = sums
            sums_ref[:, chans + cut.start : chans + cut.stop] = squares
    sums_ref[:, 2 * chans :] = jnp.full((1, LANES), count, F32)


def conv_kernel_of_peer(shift, parts, where_ref, early_ref, late_ref, taps_ref, conv_ref, padded_ref):
    rows, chans = late_ref.shape
    total_rows = conv_ref.shape[0]
    peer = lax.rem(where_ref[0] + shift, parts)
    for cut in cuts(chans, LANES):
        fill_ends(padded_ref, cut)
        for step in range(parts - 1):
            block = early_ref[step, :, cut].astype(F32)
            place_block(padded_ref, block, lax.rem(peer + step, parts), rows, cut)
        block = late_ref[:, cut].astype(F32)
        place_block(padded_ref, block, lax.rem(peer + parts - 1, parts), rows, cut)
        for at in range(0, total_rows, rows):
            conv_ref[at : at + rows, cut] = conv_rows(padded_ref, taps_ref, at, rows, cut)


def scale_and_shift(stats_ref, place, chans):
    seen = stats_ref[:, pl.ds(place, 1), :, :]
    sums = seen[..., :chans]
    squares = seen[..., chans : 2 * chans]
    counts = seen[..., 2 * chans : 2 * chans + 1]
    count = jnp.sum(counts, axis=0)[0]
    mean = jnp.sum(sums, axis=0)[0] / count
    off = sums / counts - mean
    var = jnp.sum(squares + counts * off * off, axis=0)[0] / count
    return mean, lax.rsqrt(var + 1e-05)


def branch_rows(parts, own, slot, rows, stats_ref, conv_refs, norm_refs, weight_ref):
    chans = conv_refs[0].shape[1]
    total = None
    for shift in range(parts):
        place = lax.rem(own + shift, parts)
        mean, scale = scale_and_shift(stats_ref, place, chans)
        scale = scale * norm_refs[shift][0:1, :]
        conv = conv_refs[shift][pl.ds(pl.multiple_of(slot * rows, 16), rows), :]
        z = (conv - mean) * scale + norm_refs[shift][1:2, :]
        term = contract_last(swish(z).astype(BF16), weight_ref[place])
        total = term if total is None else total + term
    return total


def sent_kernel(parts, where_ref, stats_ref, weight_ref, *refs):
    conv_refs, norm_refs, out_ref = refs[:parts], refs[parts:-1], refs[-1]
    own = where_ref[0]
    rows = out_ref.shape[1]
    for shift in range(1, parts):
        slot = lax.rem(own + shift, parts)
        branch = branch_rows(parts, own, slot, rows, stats_ref, conv_refs, norm_refs, weight_ref)
        out_ref[shift - 1] = branch.astype(BF16)


def kept_kernel(parts, where_ref, stats_ref, weight_ref, *refs):
    conv_refs, norm_refs, out_ref = refs[:parts], refs[parts:-1], refs[-1]
    own = where_ref[0]
    rows = out_ref.shape[0]
    out_ref[...] = branch_rows(parts, own, own, rows, stats_ref, conv_refs, norm_refs, weight_ref)


def finish_kernel(parts, where_ref, rows_ref, kept_ref, *refs):
    got_refs, out_ref = refs[:-1], refs[-1]
    own = where_ref[0]
    cols = kept_ref.shape[1]
    for shift in range(parts):
        branch = kept_ref[...] if shift == 0 else got_refs[shift - 1][...].astype(F32)
        place = lax.rem(own + shift, parts)
        if cols % LANES == 0:
            at = pl.ds(pl.multiple_of(place * cols, LANES), cols)
            out_ref[:, at] = (rows_ref[:, at].astype(F32) + branch).astype(BF16)
        else:
            for block in range(parts):

                @pl.when(place == block)
                def _():
                    cut = slice(block * cols, (block + 1) * cols)
                    out_ref[:, cut] = (rows_ref[:, cut].astype(F32) + branch).astype(BF16)


def shape(dims, kind):
    return jax.ShapeDtypeStruct(dims, kind)


def call(kernel, out, operands, scratch=(), flops=0, name=None):
    single = not isinstance(out, (tuple, list))
    outs = [out] if single else list(out)
    moved = sum(x.size * x.dtype.itemsize for x in list(operands) + outs)
    result = pl.pallas_call(
        kernel,
        out_shape=tuple(outs),
        in_specs=[SMEM] + [VMEM] * (len(operands) - 1),
        out_specs=tuple([VMEM] * len(outs)),
        scratch_shapes=list(scratch),
        compiler_params=pltpu.CompilerParams(vmem_limit_bytes=32 * 1024 * 1024),
        cost_estimate=pl.CostEstimate(flops=flops, bytes_accessed=moved, transcendentals=0),
        name=name,
    )(*operands)
    return result[0] if single else result


def per_device(
    parts, devices, frames_in, lengths, ln_gain, ln_bias, glu_weight, conv_kernel, bn_gain, bn_bias,
    out_weight,
):
    rows = frames_in[0]
    span, width = rows.shape
    chans = glu_weight.shape[1]
    cols = out_weight.shape[0]
    total_rows = span * parts
    own = lax.axis_index("tensor").astype(jnp.int32)
    where = jnp.stack([own, lengths[0]])

    def from_peer(value, shift):
        pairs = [((at + shift) % parts, at) for at in range(parts)]
        return lax.ppermute(value, "tensor", pairs)

    gain, bias = ln_gain[None], ln_bias[None]
    small = jnp.concatenate([conv_kernel.astype(F32), bn_gain[None], bn_bias[None]])
    frames = [rows] + [from_peer(rows, shift) for shift in range(1, parts)]
    smalls = [small] + [from_peer(small, shift) for shift in range(1, parts)]
    taps = [each[:KERNEL] for each in smalls]
    norms = [each[KERNEL:] for each in smalls]
    weight = out_weight.reshape(cols, parts, chans).transpose(1, 0, 2)

    glu_flops = 4 * span * width * chans
    early = jnp.stack([
        call(
            functools.partial(glu_kernel, shift, parts),
            shape((span, chans), BF16),
            (where, frames[shift], gain, bias, glu_weight),
            flops=glu_flops,
            name="glu",
        )
        for shift in range(parts - 1)
    ])
    padded = pltpu.VMEM((total_rows + 2 * HEAD, chans), F32)
    late, conv, sums = call(
        functools.partial(last_block_kernel, parts),
        (
            shape((span, chans), BF16),
            shape((total_rows, chans), F32),
            shape((1, 2 * chans + LANES), F32),
        ),
        (where, frames[-1], gain, bias, glu_weight, early, taps[0]),
        scratch=(padded,),
        flops=glu_flops + 2 * KERNEL * total_rows * chans,
        name="glu_conv_sums",
    )
    spread = jnp.broadcast_to(sums[None], (devices,) + sums.shape)
    stats = lax.all_to_all(spread, ("dp", "tensor"), split_axis=0, concat_axis=0, tiled=True)
    stats = stats.reshape((devices // parts, parts) + sums.shape)

    convs = [conv]
    for shift in range(1, parts):
        convs.append(
            call(
                functools.partial(conv_kernel_of_peer, shift, parts),
                shape((total_rows, chans), F32),
                (where, from_peer(early, shift), from_peer(late, shift), taps[shift]),
                scratch=(padded,),
                flops=2 * KERNEL * total_rows * chans,
                name="conv_of_peer",
            )
        )
    operands = (where, stats, weight, *convs, *norms)
    branch_flops = 2 * span * width * cols
    sent = call(
        functools.partial(sent_kernel, parts),
        shape((parts - 1, span, cols), BF16),
        operands,
        flops=branch_flops * (parts - 1),
        name="branch_sent",
    )
    got = [from_peer(sent[parts - shift - 1], shift) for shift in range(1, parts)]
    kept = call(
        functools.partial(kept_kernel, parts),
        shape((span, cols), F32),
        operands,
        flops=branch_flops,
        name="branch_kept",
    )
    out = call(
        functools.partial(finish_kernel, parts),
        shape((span, width), BF16),
        (where, rows, kept, *got),
        name="residual",
    )
    return out[None]


def solution(mesh):
    sizes = dict(mesh.shape)
    body = functools.partial(per_device, sizes["tensor"], sizes["tensor"] * sizes["dp"])
    return jax.shard_map(
        body,
        mesh=mesh,
        in_specs=(
            P("dp", "tensor", None),
            P("dp"),
            P(),
            P(),
            P(None, "tensor", None),
            P(None, "tensor"),
            P("tensor"),
            P("tensor"),
            P("tensor", None),
        ),
        out_specs=P("dp", "tensor", None),
        check_vma=False,
    )
```

```python
import functools

import jax
import jax.numpy as jnp
from jax import lax
from jax.experimental import pallas as pl
from jax.experimental.pallas import tpu as pltpu
from jax.sharding import PartitionSpec as P

KERNEL = 32
LANES = 128
HALO = 16
REACH = 32
EXTRA = 48
F32 = jnp.float32
BF16 = jnp.bfloat16

VMEM = pl.BlockSpec(memory_space=pltpu.VMEM)
SMEM = pl.BlockSpec(memory_space=pltpu.SMEM)
HBM = pl.BlockSpec(memory_space=pl.ANY)


def contract_last(left, right):
    return lax.dot_general(
        left, right, (((1,), (1,)), ((), ())), preferred_element_type=F32
    )


def layer_norm(rows, gain, bias):
    values = rows.astype(F32)
    center = jnp.mean(values, axis=-1, keepdims=True)
    values = values - center
    spread = jnp.mean(values * values, axis=-1, keepdims=True)
    return (values * lax.rsqrt(spread + 1e-05) * gain + bias).astype(BF16)


def swish(z):
    return z * jax.nn.sigmoid(z)


def cuts(width, most):
    step = most if width % most == 0 else LANES
    return [slice(at, at + step) for at in range(0, width, step)]


def valid_rows(first, rows, length):
    index = first + lax.broadcasted_iota(jnp.int32, (rows, 1), 0)
    return index < length


def glu_of(normed, weight_ref, cut, keep):
    value = contract_last(normed, weight_ref[0, cut, :])
    gate = contract_last(normed, weight_ref[1, cut, :])
    glu = (value * jax.nn.sigmoid(gate)).astype(BF16)
    return jnp.where(keep, glu.astype(F32), 0.0)


def three_parts(vector):
    parts = []
    for _ in range(3):
        part = vector.astype(BF16).astype(F32)
        parts.append(part)
        vector = vector - part
    return parts


def clear_ends(edge_ref):
    tiles, total, _ = edge_ref.shape
    zeros = jnp.zeros((REACH, LANES), F32)
    for tile in range(tiles):
        edge_ref[tile, 0:REACH, :] = zeros
        edge_ref[tile, total - REACH : total, :] = zeros


def add_block_conv(block, tile, edge_ref, taps_ref, sums_ref, first, fresh):
    rows = block.shape[0]
    edge_ref[tile, REACH : REACH + rows, :] = block
    count = (rows + 2 * HALO) // 8
    cut = slice(tile * LANES, (tile + 1) * LANES)
    total = [None] * count
    if not fresh:
        total = [sums_ref[tile, pl.ds(first + at, 8, stride=count), :] for at in range(count)]
    for seen in range(1, count + KERNEL):
        values = edge_ref[tile, pl.ds(seen, 8, stride=count), :]
        for at in range(count):
            tap = seen - at - 1
            if 0 <= tap < KERNEL:
                term = values * taps_ref[tap : tap + 1, cut]
                total[at] = term if total[at] is None else total[at] + term
    for at in range(count):
        sums_ref[tile, pl.ds(first + at, 8, stride=count), :] = total[at]


def first_block_kernel(
    parts, lengths_ref, frames_ref, vectors_ref, taps_ref, weight_ref,
    pack_ref, sums_ref, held_ref,
    rows_ref, wide_taps_ref, edge_ref, rows_sem, weight_sems,
):
    rows, width = rows_ref.shape
    chans = held_ref.shape[1]
    own = lax.axis_index("tensor")
    rows_copy = pltpu.make_async_copy(frames_ref.at[0], rows_ref, rows_sem)
    rows_copy.start()
    pieces = cuts(chans, 256)
    copies = []
    for at, cut in enumerate(pieces):
        for side in range(2):
            place = (side, pl.ds(cut.start, cut.stop - cut.start))
            copy = pltpu.make_async_copy(
                weight_ref.at[place], held_ref.at[place], weight_sems.at[at, side]
            )
            copy.start()
            copies.append(copy)
    clear_ends(edge_ref)
    taps = taps_ref[...]
    wide_taps_ref[...] = taps.astype(F32)
    gain, bias = vectors_ref[:, :width], vectors_ref[:, width : 2 * width]
    norms = [vectors_ref[:, 2 * width + at * chans : 2 * width + (at + 1) * chans] for at in range(2)]
    extra = three_parts(norms[0]) + three_parts(norms[1])
    extra.append(jnp.zeros((EXTRA - KERNEL - len(extra), chans), F32))
    pack_ref[rows : rows + KERNEL, :] = taps
    pack_ref[rows + KERNEL :, :] = jnp.concatenate(extra).astype(BF16)
    keep = valid_rows(own * rows, rows, lengths_ref[0])
    rows_copy.wait()
    normed = layer_norm(rows_ref[...], gain, bias)
    for at, cut in enumerate(pieces):
        copies[2 * at].wait()
        copies[2 * at + 1].wait()
        glu = glu_of(normed, held_ref, cut, keep)
        pack_ref[0:rows, cut] = glu.astype(BF16)
        for tile in range(cut.start // LANES, cut.stop // LANES):
            seen = slice(tile * LANES - cut.start, (tile + 1) * LANES - cut.start)
            add_block_conv(glu[:, seen], tile, edge_ref, wide_taps_ref, sums_ref, 0, True)


def middle_block_kernel(shift, parts, lengths_ref, rows_ref, vectors_ref, weight_ref, glu_ref):
    rows, chans = glu_ref.shape
    width = rows_ref.shape[1]
    first = lax.rem(lax.axis_index("tensor") + shift, parts) * rows
    keep = valid_rows(first, rows, lengths_ref[0])
    gain, bias = vectors_ref[:, :width], vectors_ref[:, width : 2 * width]
    normed = layer_norm(rows_ref[...], gain, bias)
    for cut in cuts(chans, 256):
        glu_ref[:, cut] = glu_of(normed, weight_ref, cut, keep).astype(BF16)


def last_block_kernel(
    parts, lengths_ref, rows_ref, vectors_ref, taps_ref, weight_ref, first_sums_ref, *refs
):
    middle_refs = refs[: parts - 2]
    glu_ref, conv_ref, spread_ref, wide_taps_ref, edge_ref, sums_ref, stats_ref, conv_sem = refs[parts - 2 :]
    rows, chans = glu_ref.shape
    width = rows_ref.shape[1]
    tiles = chans // LANES
    total_rows = parts * rows
    own = lax.axis_index("tensor")
    slot = lax.rem(own + parts - 1, parts)
    length = lengths_ref[0]
    count = length.astype(F32)
    keep = valid_rows(slot * rows, rows, length)
    valid = valid_rows(0, total_rows, length).astype(F32)
    clear_ends(edge_ref)
    wide_taps_ref[...] = taps_ref[...].astype(F32)
    reach = rows + 2 * HALO
    zeros = jnp.zeros((total_rows + 2 * HALO, LANES), F32)
    for tile in range(tiles):
        sums_ref[tile] = zeros
        sums_ref[tile, pl.ds(pl.multiple_of(own * rows, rows), reach), :] = first_sums_ref[tile]
    gain, bias = vectors_ref[:, :width], vectors_ref[:, width : 2 * width]
    normed = layer_norm(rows_ref[...], gain, bias)
    copies = []
    for cut in cuts(chans, 256):
        glu = glu_of(normed, weight_ref, cut, keep)
        glu_ref[:, cut] = glu.astype(BF16)
        for tile in range(cut.start // LANES, cut.stop // LANES):
            seen = slice(tile * LANES - cut.start, (tile + 1) * LANES - cut.start)
            lanes = slice(tile * LANES, (tile + 1) * LANES)
            for at, middle in enumerate(middle_refs):
                first = pl.multiple_of(lax.rem(own + at + 1, parts) * rows, rows)
                block = middle[:, lanes].astype(F32)
                add_block_conv(block, tile, edge_ref, wide_taps_ref, sums_ref, first, False)
            first = pl.multiple_of(slot * rows, rows)
            add_block_conv(glu[:, seen], tile, edge_ref, wide_taps_ref, sums_ref, first, False)
            copy = pltpu.make_async_copy(
                sums_ref.at[tile, pl.ds(HALO, total_rows)], conv_ref.at[tile], conv_sem.at[tile]
            )
            copy.start()
            copies.append(copy)
            conv = sums_ref[tile, HALO : HALO + total_rows, :]
            sums = jnp.sum(conv * valid, axis=0, keepdims=True)
            off = (conv - sums / count) * valid
            stats_ref[:, lanes] = sums
            stats_ref[:, chans + lanes.start : chans + lanes.stop] = jnp.sum(
                off * off, axis=0, keepdims=True
            )
    stats_ref[:, 2 * chans :] = jnp.full((1, LANES), count, F32)
    stats = stats_ref[...]
    for at in range(spread_ref.shape[0]):
        spread_ref[at] = stats
    for copy in copies:
        copy.wait()


def peer_conv_kernel(parts, vectors_ref, conv_ref, weight_ref, *refs):
    packs, middles, lates = refs[: parts - 1], refs[parts - 1 : (parts - 1) ** 2], refs[(parts - 1) ** 2 :]
    lates, (convs_ref, norms_ref, held_ref) = lates[: parts - 1], lates[parts - 1 : parts + 2]
    wide_taps_ref, edge_ref, sums_ref, conv_sem, weight_sem = refs[-5:]
    rows, chans = lates[0].shape
    tiles = chans // LANES
    total_rows = parts * rows
    conv_copy = pltpu.make_async_copy(conv_ref, convs_ref.at[0], conv_sem)
    conv_copy.start()
    weight_copy = pltpu.make_async_copy(weight_ref, held_ref, weight_sem)
    weight_copy.start()
    own = lax.axis_index("tensor")
    clear_ends(edge_ref)
    skip = vectors_ref.shape[1] - 2 * chans
    norms_ref[0, 0:1, :] = vectors_ref[:, skip : skip + chans]
    norms_ref[0, 1:2, :] = vectors_ref[:, skip + chans :]
    zeros = jnp.zeros((total_rows + 2 * HALO, LANES), F32)
    for shift in range(1, parts):
        peer = lax.rem(own + shift, parts)
        pack = packs[shift - 1]
        wide_taps_ref[...] = pack[rows : rows + KERNEL, :].astype(F32)
        extra = pack[rows + KERNEL :, :].astype(F32)
        norms_ref[shift, 0:1, :] = extra[0:1] + (extra[1:2] + extra[2:3])
        norms_ref[shift, 1:2, :] = extra[3:4] + (extra[4:5] + extra[5:6])
        mine = middles[(shift - 1) * (parts - 2) : shift * (parts - 2)]
        blocks = [pack] + list(mine) + [lates[shift - 1]]
        for tile in range(tiles):
            lanes = slice(tile * LANES, (tile + 1) * LANES)
            sums_ref[tile] = zeros
            for step, block in enumerate(blocks):
                first = pl.multiple_of(lax.rem(peer + step, parts) * rows, rows)
                values = block[0:rows, lanes].astype(F32)
                add_block_conv(values, tile, edge_ref, wide_taps_ref, sums_ref, first, False)
            convs_ref[shift, tile] = sums_ref[tile, HALO : HALO + total_rows, :]
    conv_copy.wait()
    weight_copy.wait()


def branch_rows(parts, slot, rows, stats_ref, convs_ref, norms_ref, weight_ref):
    chans = norms_ref.shape[2]
    own = lax.axis_index("tensor")
    first = pl.multiple_of(slot * rows, rows)
    total = None
    for shift in range(parts):
        place = lax.rem(own + shift, parts)
        seen = stats_ref[:, pl.ds(place, 1), :, :]
        counts = seen[..., 2 * chans : 2 * chans + 1]
        sums = seen[..., :chans]
        count = jnp.sum(counts, axis=0)[0]
        mean = jnp.sum(sums, axis=0)[0] / count
        off = sums / counts - mean
        var = jnp.sum(seen[..., chans : 2 * chans] + counts * off * off, axis=0)[0] / count
        scale = lax.rsqrt(var + 1e-05) * norms_ref[shift, 0:1, :]
        bias = norms_ref[shift, 1:2, :]
        acts = []
        for tile in range(chans // LANES):
            lanes = slice(tile * LANES, (tile + 1) * LANES)
            conv = convs_ref[shift, tile, pl.ds(first, rows), :]
            z = (conv - mean[:, lanes]) * scale[:, lanes] + bias[:, lanes]
            acts.append(swish(z).astype(BF16))
        if weight_ref.ndim == 3:
            weight = weight_ref[place]
        else:
            weight = weight_ref[:, pl.ds(pl.multiple_of(place * chans, LANES), chans)]
        term = contract_last(jnp.concatenate(acts, axis=1), weight)
        total = term if total is None else total + term
    return total


def sent_kernel(parts, stats_ref, convs_ref, norms_ref, weight_ref, out_ref):
    own = lax.axis_index("tensor")
    rows = out_ref.shape[1]
    for shift in range(1, parts):
        slot = lax.rem(own + shift, parts)
        branch = branch_rows(parts, slot, rows, stats_ref, convs_ref, norms_ref, weight_ref)
        out_ref[shift - 1] = branch.astype(BF16)


def columns(ref, place, cols):
    if len(ref.shape) == 3:
        return ref.at[place]
    return ref.at[:, pl.ds(pl.multiple_of(place * cols, LANES), cols)]


def kept_kernel(
    parts, stats_ref, convs_ref, norms_ref, weight_ref, frames_ref,
    out_ref, base_ref, mine_ref, frames_sems, out_sem,
):
    own = lax.axis_index("tensor")
    rows, cols = mine_ref.shape
    copies = []
    for shift in range(parts):
        target = mine_ref if shift == 0 else base_ref.at[shift - 1]
        source = columns(frames_ref, lax.rem(own + shift, parts), cols)
        copy = pltpu.make_async_copy(source, target, frames_sems.at[shift])
        copy.start()
        copies.append(copy)
    branch = branch_rows(parts, own, rows, stats_ref, convs_ref, norms_ref, weight_ref)
    for copy in copies:
        copy.wait()
    mine_ref[...] = (mine_ref[...].astype(F32) + branch).astype(BF16)
    out_copy = pltpu.make_async_copy(mine_ref, columns(out_ref, own, cols), out_sem)
    out_copy.start()
    out_copy.wait()


def finish_kernel(parts, filled_ref, base_ref, *refs):
    got_refs, (out_ref, done_ref, out_sems) = refs[: parts - 1], refs[parts - 1 :]
    own = lax.axis_index("tensor")
    cols = base_ref.shape[2]
    copies = []
    for shift in range(1, parts):
        branch = got_refs[shift - 1][...].astype(F32)
        done_ref[shift - 1] = (base_ref[shift - 1].astype(F32) + branch).astype(BF16)
        target = columns(out_ref, lax.rem(own + shift, parts), cols)
        copy = pltpu.make_async_copy(done_ref.at[shift - 1], target, out_sems.at[shift - 1])
        copy.start()
        copies.append(copy)
    for copy in copies:
        copy.wait()


def shape(dims, kind):
    return jax.ShapeDtypeStruct(dims, kind)


def call(kernel, outs, in_specs, operands, out_specs=None, scratch=(), flops=0, name=None, aliases=None):
    moved = sum(x.size * x.dtype.itemsize for x in list(operands) + list(outs))
    return pl.pallas_call(
        kernel,
        out_shape=tuple(outs),
        in_specs=list(in_specs),
        out_specs=tuple(out_specs or [VMEM] * len(outs)),
        scratch_shapes=list(scratch),
        input_output_aliases=aliases or {},
        compiler_params=pltpu.CompilerParams(vmem_limit_bytes=24 * 1024 * 1024),
        cost_estimate=pl.CostEstimate(flops=flops, bytes_accessed=moved, transcendentals=0),
        name=name,
    )(*operands)


def per_device(
    parts, devices, frames_in, lengths, ln_gain, ln_bias, glu_weight, conv_kernel, bn_gain, bn_bias,
    out_weight,
):
    _, span, width = frames_in.shape
    given = glu_weight.shape[1]
    cols = out_weight.shape[0]
    spare = -given % LANES
    if spare:
        glu_weight = jnp.pad(glu_weight, ((0, 0), (0, spare), (0, 0)))
        conv_kernel = jnp.pad(conv_kernel, ((0, 0), (0, spare)))
        bn_gain, bn_bias = jnp.pad(bn_gain, (0, spare)), jnp.pad(bn_bias, (0, spare))
        out_weight = out_weight.reshape(cols, parts, given).transpose(1, 0, 2)
        out_weight = jnp.pad(out_weight, ((0, 0), (0, 0), (0, spare)))
    chans = given + spare
    tiles = chans // LANES
    total_rows = span * parts

    def from_peer(value, shift):
        pairs = [((at + shift) % parts, at) for at in range(parts)]
        return lax.ppermute(value, "tensor", pairs)

    vectors = jnp.concatenate([ln_gain, ln_bias, bn_gain, bn_bias])[None]
    frames = [from_peer(frames_in[0], shift) for shift in range(1, parts)]

    glu_flops = 4 * span * width * chans
    wide_taps = pltpu.VMEM((KERNEL, chans), F32)
    edge = pltpu.VMEM((tiles, span + 2 * REACH, LANES), F32)
    sums = pltpu.VMEM((tiles, total_rows + 2 * HALO, LANES), F32)
    pack, first_sums, held = call(
        functools.partial(first_block_kernel, parts),
        (
            shape((span + EXTRA, chans), BF16),
            shape((tiles, span + 2 * HALO, LANES), F32),
            shape((2, chans, width), BF16),
        ),
        [SMEM, HBM, VMEM, VMEM, HBM],
        (lengths, frames_in, vectors, conv_kernel, glu_weight),
        scratch=(
            pltpu.VMEM((span, width), BF16),
            wide_taps,
            edge,
            pltpu.SemaphoreType.DMA,
            pltpu.SemaphoreType.DMA((len(cuts(chans, 256)), 2)),
        ),
        flops=glu_flops,
        name="first_block",
    )
    middle = [
        call(
            functools.partial(middle_block_kernel, shift, parts),
            (shape((span, chans), BF16),),
            [SMEM, VMEM, VMEM, VMEM],
            (lengths, frames[shift - 1], vectors, held),
            flops=glu_flops,
            name="middle_block",
        )[0]
        for shift in range(1, parts - 1)
    ]
    late, conv, spread = call(
        functools.partial(last_block_kernel, parts),
        (
            shape((span, chans), BF16),
            shape((tiles, total_rows, LANES), F32),
            shape((devices, 1, 2 * chans + LANES), F32),
        ),
        [SMEM] + [VMEM] * (5 + len(middle)),
        (lengths, frames[-1], vectors, conv_kernel, held, first_sums, *middle),
        out_specs=(VMEM, HBM, VMEM),
        scratch=(
            wide_taps,
            edge,
            sums,
            pltpu.VMEM((1, 2 * chans + LANES), F32),
            pltpu.SemaphoreType.DMA((tiles,)),
        ),
        flops=glu_flops,
        name="last_block",
    )
    stats = lax.all_to_all(spread, ("dp", "tensor"), split_axis=0, concat_axis=0, tiled=True)
    stats = stats.reshape((devices // parts, parts) + spread.shape[1:])

    shifts = range(1, parts)
    packs = [from_peer(pack, shift) for shift in shifts]
    middles = [from_peer(each, shift) for shift in shifts for each in middle]
    lates = [from_peer(late, shift) for shift in shifts]
    convs, norms, weight = call(
        functools.partial(peer_conv_kernel, parts),
        (
            shape((parts, tiles, total_rows, LANES), F32),
            shape((parts, 2, chans), F32),
            shape(out_weight.shape, BF16),
        ),
        [VMEM, HBM, HBM] + [VMEM] * (len(packs) + len(middles) + len(lates)),
        (vectors, conv, out_weight, *packs, *middles, *lates),
        scratch=(wide_taps, edge, sums, pltpu.SemaphoreType.DMA, pltpu.SemaphoreType.DMA),
        flops=2 * KERNEL * total_rows * chans,
        name="peer_conv",
    )
    operands = (stats, convs, norms, weight)
    branch_flops = 2 * span * width * cols
    (sent,) = call(
        functools.partial(sent_kernel, parts),
        (shape((parts - 1, span, cols), BF16),),
        [VMEM] * 4,
        operands,
        flops=branch_flops * (parts - 1),
        name="branch_sent",
    )
    got = [from_peer(sent[parts - shift - 1], shift) for shift in shifts]
    whole = cols % LANES == 0
    rows = frames_in[0]
    if not whole:
        rows = rows.reshape(span, parts, cols).transpose(1, 0, 2)
    filled, base = call(
        functools.partial(kept_kernel, parts),
        (shape(rows.shape, BF16), shape((parts - 1, span, cols), BF16)),
        [VMEM] * 4 + [HBM],
        (*operands, rows),
        out_specs=(HBM, VMEM),
        scratch=(
            pltpu.VMEM((span, cols), BF16),
            pltpu.SemaphoreType.DMA((parts,)),
            pltpu.SemaphoreType.DMA,
        ),
        flops=branch_flops,
        name="branch_kept",
    )
    (out,) = call(
        functools.partial(finish_kernel, parts),
        (shape(rows.shape, BF16),),
        [HBM] + [VMEM] * parts,
        (filled, base, *got),
        out_specs=(HBM,),
        scratch=(
            pltpu.VMEM((parts - 1, span, cols), BF16),
            pltpu.SemaphoreType.DMA((parts - 1,)),
        ),
        aliases={0: 0},
        name="residual",
    )
    if not whole:
        out = out.transpose(1, 0, 2).reshape(span, width)
    return out[None]


def solution(mesh):
    sizes = dict(mesh.shape)
    body = functools.partial(per_device, sizes["tensor"], sizes["tensor"] * sizes["dp"])
    return jax.shard_map(
        body,
        mesh=mesh,
        in_specs=(
            P("dp", "tensor", None),
            P("dp"),
            P(),
            P(),
            P(None, "tensor", None),
            P(None, "tensor"),
            P("tensor"),
            P("tensor"),
            P("tensor", None),
        ),
        out_specs=P("dp", "tensor", None),
        check_vma=False,
    )
```

```python
import functools

import jax
import jax.numpy as jnp
from jax import lax
from jax.experimental import pallas as pl
from jax.experimental.pallas import tpu as pltpu
from jax.sharding import PartitionSpec as P

KERNEL = 32
LANES = 128
WIDE = 256
HALO = 16
EDGE = 8
EXTRA = 48
F32 = jnp.float32
BF16 = jnp.bfloat16

VMEM = pl.BlockSpec(memory_space=pltpu.VMEM)
SMEM = pl.BlockSpec(memory_space=pltpu.SMEM)
HBM = pl.BlockSpec(memory_space=pltpu.HBM)


def layer_norm(rows, gain, bias):
    values = rows.astype(F32)
    center = jnp.mean(values, axis=-1, keepdims=True)
    values = values - center
    spread = jnp.mean(values * values, axis=-1, keepdims=True)
    return (values * lax.rsqrt(spread + 1e-05) * gain + bias).astype(BF16)


def swish(z):
    return z * jax.nn.sigmoid(z)


def cuts(width, most):
    return [slice(at, at + most) for at in range(0, width, most)]


def valid_rows(first, rows, length):
    index = first + lax.broadcasted_iota(jnp.int32, (rows, 1), 0)
    return index < length


def glu_of(normed, weight_ref, cut, keep):
    value = jnp.dot(normed, weight_ref[0, :, cut], preferred_element_type=F32)
    gate = jnp.dot(normed, weight_ref[1, :, cut], preferred_element_type=F32)
    glu = (value * jax.nn.sigmoid(gate)).astype(BF16)
    return jnp.where(keep, glu.astype(F32), 0.0)


def three_parts(vector):
    parts = []
    for _ in range(3):
        part = vector.astype(BF16).astype(F32)
        parts.append(part)
        vector = vector - part
    return parts


def affine(vectors_ref):
    rows = [vectors_ref[at : at + 1, :] for at in range(vectors_ref.shape[0] - 2)]
    half = len(rows) // 2
    return jnp.concatenate(rows[:half], axis=1), jnp.concatenate(rows[half:], axis=1)


def clear_ends(edge_ref):
    tiles, total, _ = edge_ref.shape
    zeros = jnp.zeros((EDGE, LANES), F32)
    for tile in range(tiles):
        edge_ref[tile, 0:EDGE, :] = zeros
        edge_ref[tile, total - EDGE : total, :] = zeros


def taps_at(taps_ref, offset, tile):
    cut = slice(tile * LANES, (tile + 1) * LANES)
    taps = {}
    for step in range(5):
        tap = 8 * step + offset - 1
        if 0 <= tap < KERNEL:
            taps[step] = jnp.broadcast_to(taps_ref[tap : tap + 1, cut], (8, LANES))
    return taps


def block_conv(block, tile, edge_ref, taps_ref):
    rows = block.shape[0]
    edge_ref[tile, EDGE : EDGE + rows, :] = block
    count = (rows + 2 * HALO) // 8
    total = [None] * count
    for offset in range(8):
        taps = taps_at(taps_ref, offset, tile)
        for at in range(count + 4):
            start = 8 * at + offset - 2 * HALO
            if start <= -8 or start >= rows:
                continue
            values = edge_ref[tile, EDGE + start : EDGE + start + 8, :]
            for step, tap in taps.items():
                if 0 <= at - step < count:
                    term = values * tap
                    seen = total[at - step]
                    total[at - step] = term if seen is None else seen + term
    return total


def first_block_kernel(
    lengths_ref, frames_ref, vectors_ref, taps_ref, weight_ref,
    pack_ref, sums_ref, held_ref,
    rows_ref, raw_ref, wide_taps_ref, edge_ref, rows_sem, weight_sems,
):
    rows = rows_ref.shape[0]
    chans = held_ref.shape[2]
    own = lax.axis_index("tensor")
    rows_copy = pltpu.make_async_copy(frames_ref.at[0], rows_ref, rows_sem)
    rows_copy.start()
    pieces = cuts(chans, WIDE)
    copies = []
    for at, cut in enumerate(pieces):
        for side in range(2):
            place = (side, pl.ds(cut.start, WIDE))
            copy = pltpu.make_async_copy(
                weight_ref.at[place], raw_ref.at[place], weight_sems.at[at, side]
            )
            copy.start()
            copies.append(copy)
    clear_ends(edge_ref)
    keep = valid_rows(own * rows, rows, lengths_ref[0])
    taps = taps_ref[...]
    wide_taps_ref[...] = taps.astype(F32)
    pack_ref[rows : rows + KERNEL, :] = taps
    last = vectors_ref.shape[0] - 2
    extra = three_parts(vectors_ref[last : last + 1, :])
    extra += three_parts(vectors_ref[last + 1 : last + 2, :])
    extra.append(jnp.zeros((EXTRA - KERNEL - len(extra), chans), F32))
    pack_ref[rows + KERNEL :, :] = jnp.concatenate(extra).astype(BF16)
    gain, bias = affine(vectors_ref)
    rows_copy.wait()
    normed = layer_norm(rows_ref[...], gain, bias)
    for at, cut in enumerate(pieces):
        for side in range(2):
            copies[2 * at + side].wait()
            held_ref[side, :, cut] = raw_ref[side, cut, :].T
        glu = glu_of(normed, held_ref, cut, keep)
        pack_ref[0:rows, cut] = glu.astype(BF16)
        for tile in range(cut.start // LANES, cut.stop // LANES):
            seen = slice(tile * LANES - cut.start, (tile + 1) * LANES - cut.start)
            total = block_conv(glu[:, seen], tile, edge_ref, wide_taps_ref)
            for step, each in enumerate(total):
                sums_ref[tile, 8 * step : 8 * step + 8, :] = each


def last_block_kernel(
    lengths_ref, rows_ref, vectors_ref, taps_ref, weight_ref, first_sums_ref,
    late_ref, near_ref, sent_ref, kept_ref, spread_ref,
    wide_taps_ref, edge_ref, sums_ref,
):
    rows, chans = late_ref.shape
    tiles = chans // LANES
    own = lax.axis_index("tensor")
    peer = 1 - own
    length = lengths_ref[0]
    count = length.astype(F32)
    keep = valid_rows(peer * rows, rows, length)
    own_valid, peer_valid = (valid_rows(at * rows, rows, length).astype(F32) for at in (own, peer))
    clear_ends(edge_ref)
    wide_taps_ref[...] = taps_ref[...].astype(F32)
    reach = rows + 2 * HALO
    own_at = pl.multiple_of(own * rows, rows)
    peer_at = pl.multiple_of(peer * rows, rows)
    for tile in range(tiles):
        sums_ref[tile, pl.ds(peer_at, reach), :] = jnp.zeros((reach, LANES), F32)
        sums_ref[tile, pl.ds(own_at, reach), :] = first_sums_ref[tile]
    normed = layer_norm(rows_ref[...], *affine(vectors_ref))
    for cut in cuts(chans, WIDE):
        glu = glu_of(normed, weight_ref, cut, keep)
        late_ref[:, cut] = glu.astype(BF16)
        for tile in range(cut.start // LANES, cut.stop // LANES):
            seen = slice(tile * LANES - cut.start, (tile + 1) * LANES - cut.start)
            lanes = slice(tile * LANES, (tile + 1) * LANES)
            for step, each in enumerate(block_conv(glu[:, seen], tile, edge_ref, wide_taps_ref)):
                at = pl.ds(peer_at + 8 * step, 8)
                sums_ref[tile, at, :] = sums_ref[tile, at, :] + each
            kept = sums_ref[tile, pl.ds(own_at + HALO, rows), :]
            sent = sums_ref[tile, pl.ds(peer_at + HALO, rows), :]
            kept_ref[tile] = kept
            sent_ref[tile] = sent
            sums = jnp.sum(kept * own_valid, axis=0, keepdims=True)
            sums += jnp.sum(sent * peer_valid, axis=0, keepdims=True)
            mean = sums / count
            off = (kept - mean) * own_valid
            squares = jnp.sum(off * off, axis=0, keepdims=True)
            off = (sent - mean) * peer_valid
            squares += jnp.sum(off * off, axis=0, keepdims=True)
            spread_ref[0, :, lanes] = sums
            spread_ref[0, :, chans + lanes.start : chans + lanes.stop] = squares
    near = pl.multiple_of(own * (rows - HALO), HALO)
    near_ref[...] = late_ref[pl.ds(near, HALO), :]
    spread_ref[0, :, 2 * chans :] = jnp.full((1, LANES), count, F32)
    stats = spread_ref[0]
    for at in range(1, spread_ref.shape[0]):
        spread_ref[at] = stats


def peer_conv_kernel(
    vectors_ref, weight_ref, pack_ref, sums_ref, taps_ref, norms_ref, held_ref,
    raw_ref, edge_ref, weight_sem,
):
    parts, chans, cols = held_ref.shape
    rows = pack_ref.shape[0] - EXTRA
    copy = pltpu.make_async_copy(weight_ref, raw_ref, weight_sem)
    copy.start()
    clear_ends(edge_ref)
    taps_ref[...] = pack_ref[rows : rows + KERNEL, :].astype(F32)
    extra = pack_ref[rows + KERNEL :, :].astype(F32)
    last = vectors_ref.shape[0] - 2
    norms_ref[0] = vectors_ref[last : last + 2, :]
    norms_ref[1, 0:1, :] = extra[0:1] + (extra[1:2] + extra[2:3])
    norms_ref[1, 1:2, :] = extra[3:4] + (extra[4:5] + extra[5:6])
    for tile in range(chans // LANES):
        lanes = slice(tile * LANES, (tile + 1) * LANES)
        block = pack_ref[0:rows, lanes].astype(F32)
        for step, each in enumerate(block_conv(block, tile, edge_ref, taps_ref)):
            sums_ref[tile, 8 * step : 8 * step + 8, :] = each
    copy.wait()
    for place in range(parts):
        for cut in cuts(chans, WIDE):
            at = place * chans
            held_ref[place, cut, :] = raw_ref[:, at + cut.start : at + cut.stop].T


def scales(stats_ref, norms_ref):
    chans = norms_ref.shape[2]
    own = lax.axis_index("tensor")
    found = []
    for shift, place in enumerate((own, 1 - own)):
        seen = stats_ref[:, pl.ds(place, 1), :, :]
        counts = seen[..., 2 * chans : 2 * chans + 1]
        sums = seen[..., :chans]
        count = jnp.sum(counts, axis=0)[0]
        mean = jnp.sum(sums, axis=0)[0] / count
        off = sums / counts - mean
        var = jnp.sum(seen[..., chans : 2 * chans] + counts * off * off, axis=0)[0] / count
        scale = lax.rsqrt(var + 1e-05) * norms_ref[shift, 0:1, :]
        found.append((mean, scale, norms_ref[shift, 1:2, :]))
    return found


def branch_rows(found, conv_of, weight_ref):
    own = lax.axis_index("tensor")
    total = None
    for shift, (mean, scale, bias) in enumerate(found):
        acts = []
        for tile in range(mean.shape[1] // LANES):
            lanes = slice(tile * LANES, (tile + 1) * LANES)
            z = (conv_of(shift, tile) - mean[:, lanes]) * scale[:, lanes] + bias[:, lanes]
            acts.append(swish(z).astype(BF16))
        place = own if shift == 0 else 1 - own
        term = jnp.dot(jnp.concatenate(acts, axis=1), weight_ref[place], preferred_element_type=F32)
        total = term if total is None else total + term
    return total


def sent_kernel(
    stats_ref, conv_ref, early_ref, near_ref, taps_ref, norms_ref, weight_ref,
    out_ref, peer_ref, edge_ref,
):
    own = lax.axis_index("tensor")
    tiles, rows, _ = conv_ref.shape
    target = pl.multiple_of(jnp.where(own == 0, 0, rows - HALO), HALO)
    source = pl.multiple_of(jnp.where(own == 0, 0, 2 * HALO), HALO)
    for tile in range(tiles):
        lanes = slice(tile * LANES, (tile + 1) * LANES)
        edge_ref[tile] = jnp.zeros((3 * HALO, LANES), F32)
        edge_ref[tile, pl.ds(source, HALO), :] = near_ref[:, lanes].astype(F32)
        peer_ref[tile] = early_ref[tile, HALO : HALO + rows, :]
        total = [peer_ref[tile, pl.ds(target + 8 * at, 8), :] for at in range(HALO // 8)]
        for tap in range(KERNEL):
            weight = jnp.broadcast_to(taps_ref[tap : tap + 1, lanes], (8, LANES))
            for at in range(HALO // 8):
                start = 8 * at + tap + 1
                total[at] += edge_ref[tile, start : start + 8, :] * weight
        for at in range(HALO // 8):
            peer_ref[tile, pl.ds(target + 8 * at, 8), :] = total[at]
    found = scales(stats_ref, norms_ref)
    branch = branch_rows(found, lambda shift, tile: (peer_ref if shift else conv_ref)[tile], weight_ref)
    out_ref[...] = branch.astype(BF16)


def columns(ref, place, cols):
    return ref.at[:, pl.ds(pl.multiple_of(place * cols, LANES), cols)]


def kept_kernel(
    stats_ref, conv_ref, early_ref, late_ref, taps_ref, norms_ref, weight_ref, frames_ref,
    out_ref, base_ref, mine_ref, edge_ref, peer_ref, sems, out_sem,
):
    own = lax.axis_index("tensor")
    rows, cols = mine_ref.shape
    tiles = conv_ref.shape[0]
    copies = [(columns(frames_ref, own, cols), mine_ref), (columns(frames_ref, 1 - own, cols), base_ref)]
    copies = [pltpu.make_async_copy(*pair, sems.at[at]) for at, pair in enumerate(copies)]
    for copy in copies:
        copy.start()
    clear_ends(edge_ref)
    source = pl.multiple_of(jnp.where(own == 0, 0, rows + HALO), HALO)
    target = pl.multiple_of(jnp.where(own == 0, rows - HALO, 0), HALO)
    for tile in range(tiles):
        lanes = slice(tile * LANES, (tile + 1) * LANES)
        total = block_conv(late_ref[:, lanes].astype(F32), tile, edge_ref, taps_ref)
        for step in range(rows // 8):
            peer_ref[tile, 8 * step : 8 * step + 8, :] = total[step + HALO // 8]
        for at in range(HALO // 8):
            place = pl.ds(target + 8 * at, 8)
            peer_ref[tile, place, :] = peer_ref[tile, place, :] + early_ref[tile, pl.ds(source + 8 * at, 8), :]
    found = scales(stats_ref, norms_ref)
    branch = branch_rows(found, lambda shift, tile: (peer_ref if shift else conv_ref)[tile], weight_ref)
    for copy in copies:
        copy.wait()
    mine_ref[...] = (mine_ref[...].astype(F32) + branch).astype(BF16)
    out_copy = pltpu.make_async_copy(mine_ref, columns(out_ref, own, cols), out_sem)
    out_copy.start()
    out_copy.wait()


def finish_kernel(filled_ref, base_ref, got_ref, out_ref, done_ref, out_sem):
    own = lax.axis_index("tensor")
    cols = base_ref.shape[1]
    done_ref[...] = (base_ref[...].astype(F32) + got_ref[...].astype(F32)).astype(BF16)
    copy = pltpu.make_async_copy(done_ref, columns(out_ref, 1 - own, cols), out_sem)
    copy.start()
    copy.wait()


def shape(dims, kind):
    return jax.ShapeDtypeStruct(dims, kind)


def call(kernel, outs, in_specs, operands, out_specs=None, scratch=(), name=None, aliases=None, room=32):
    return pl.pallas_call(
        kernel,
        out_shape=tuple(outs),
        in_specs=list(in_specs),
        out_specs=tuple(out_specs or [VMEM] * len(outs)),
        scratch_shapes=list(scratch),
        input_output_aliases=aliases or {},
        compiler_params=pltpu.CompilerParams(vmem_limit_bytes=room * 1024 * 1024),
        name=name,
    )(*operands)


def two_parts(
    devices, frames_in, lengths, ln_gain, ln_bias, glu_weight, conv_kernel, bn_gain, bn_bias, out_weight
):
    _, span, width = frames_in.shape
    chans = glu_weight.shape[1]
    cols = out_weight.shape[0]
    tiles = chans // LANES
    pieces = chans // WIDE

    def swap(value):
        return lax.ppermute(value, "tensor", [(0, 1), (1, 0)])

    frames = swap(frames_in[0])
    vectors = jnp.concatenate([ln_gain, ln_bias, bn_gain, bn_bias]).reshape(-1, chans)
    edge = pltpu.VMEM((tiles, span + 2 * EDGE, LANES), F32)
    wide_taps = pltpu.VMEM((KERNEL, chans), F32)
    dma = pltpu.SemaphoreType.DMA
    reach = shape((tiles, span + 2 * HALO, LANES), F32)
    block = shape((tiles, span, LANES), F32)
    pack, first_sums, held = call(
        first_block_kernel,
        (shape((span + EXTRA, chans), BF16), reach, shape((2, width, chans), BF16)),
        [SMEM, HBM, VMEM, VMEM, HBM],
        (lengths, frames_in, vectors, conv_kernel, glu_weight),
        scratch=(
            pltpu.VMEM((span, width), BF16),
            pltpu.VMEM((2, chans, width), BF16),
            wide_taps,
            edge,
            dma,
            dma((pieces, 2)),
        ),
        name="first_block",
        room=48,
    )
    early = swap(pack)
    late, near, sent_conv, kept_conv, spread = call(
        last_block_kernel,
        (
            shape((span, chans), BF16),
            shape((HALO, chans), BF16),
            block,
            block,
            shape((devices, 1, 2 * chans + LANES), F32),
        ),
        [SMEM] + [VMEM] * 5,
        (lengths, frames, vectors, conv_kernel, held, first_sums),
        scratch=(wide_taps, edge, pltpu.VMEM((tiles, 2 * span + 2 * HALO, LANES), F32)),
        name="last_block",
    )
    spread, early = lax.optimization_barrier((spread, early))
    stats = lax.all_to_all(spread, ("dp", "tensor"), split_axis=0, concat_axis=0, tiled=True)
    stats = stats.reshape((devices // 2, 2) + spread.shape[1:])
    near, late = swap(near), swap(late)
    early_sums, taps, norms, weight = call(
        peer_conv_kernel,
        (reach, shape((KERNEL, chans), F32), shape((2, 2, chans), F32), shape((2, chans, cols), BF16)),
        [VMEM, HBM, VMEM],
        (vectors, out_weight, early),
        scratch=(pltpu.VMEM(out_weight.shape, BF16), edge, dma),
        name="peer_conv",
    )
    (sent,) = call(
        sent_kernel,
        (shape((span, cols), BF16),),
        [VMEM] * 7,
        (stats, sent_conv, early_sums, near, taps, norms, weight),
        scratch=(pltpu.VMEM(block.shape, F32), pltpu.VMEM((tiles, 3 * HALO, LANES), F32)),
        name="branch_sent",
    )
    got = swap(sent)
    filled, base = call(
        kept_kernel,
        (shape((span, width), BF16), shape((span, cols), BF16)),
        [VMEM] * 7 + [HBM],
        (stats, kept_conv, early_sums, late, taps, norms, weight, frames_in[0]),
        out_specs=(HBM, VMEM),
        scratch=(
            pltpu.VMEM((span, cols), BF16),
            edge,
            pltpu.VMEM(block.shape, F32),
            dma((2,)),
            dma,
        ),
        name="branch_kept",
    )
    (out,) = call(
        finish_kernel,
        (shape((span, width), BF16),),
        [HBM, VMEM, VMEM],
        (filled, base, got),
        out_specs=(HBM,),
        scratch=(pltpu.VMEM((span, cols), BF16), dma),
        aliases={0: 0},
        name="residual",
    )
    return out[None]


def contract_last(left, right):
    return lax.dot_general(
        left, right, (((1,), (1,)), ((), ())), preferred_element_type=F32
    )


def many_parts(
    devices, frames_in, lengths, ln_gain, ln_bias, glu_weight, conv_kernel, bn_gain, bn_bias, out_weight
):
    rows = frames_in[0]
    chans = glu_weight.shape[1]
    normed = layer_norm(rows, ln_gain, ln_bias)
    proj = contract_last(
        lax.all_gather(normed, "tensor", axis=0, tiled=True),
        glu_weight.reshape(2 * chans, rows.shape[1]),
    )
    valid = valid_rows(0, proj.shape[0], lengths[0])
    glu = (proj[:, :chans] * jax.nn.sigmoid(proj[:, chans:])).astype(BF16)
    glu = jnp.where(valid, glu, jnp.zeros_like(glu)).astype(F32)
    padded = jnp.pad(glu, ((15, KERNEL - 16), (0, 0)))
    taps = conv_kernel.astype(F32)
    conv = jnp.zeros_like(glu)
    for tap in range(KERNEL):
        conv = conv + padded[tap : tap + glu.shape[0]] * taps[tap]
    own = lengths[0].astype(F32)
    local = jnp.sum(jnp.where(valid, conv, 0.0), axis=0) / own
    squares = jnp.sum(jnp.where(valid, conv - local, 0.0) ** 2, axis=0)
    count = lax.psum(own, "dp")
    mean = lax.psum(local * own, "dp") / count
    var = lax.psum(squares + own * (local - mean) ** 2, "dp") / count
    z = (conv - mean) * (lax.rsqrt(var + 1e-05) * bn_gain) + bn_bias
    act = lax.all_gather(swish(z).astype(BF16), "tensor", axis=1, tiled=True)
    branch = contract_last(act, out_weight)
    branch = lax.all_to_all(branch, "tensor", split_axis=0, concat_axis=1, tiled=True)
    return (rows.astype(F32) + branch).astype(BF16)[None]


def solution(mesh):
    sizes = dict(mesh.shape)
    body = two_parts if sizes["tensor"] == 2 else many_parts
    body = functools.partial(body, sizes["tensor"] * sizes["dp"])
    return jax.shard_map(
        body,
        mesh=mesh,
        in_specs=(
            P("dp", "tensor", None),
            P("dp"),
            P(),
            P(),
            P(None, "tensor", None),
            P(None, "tensor"),
            P("tensor"),
            P("tensor"),
            P("tensor", None),
        ),
        out_specs=P("dp", "tensor", None),
        check_vma=False,
    )
```

```python
import functools

import jax
import jax.numpy as jnp
from jax import lax
from jax.experimental import pallas as pl
from jax.experimental.pallas import tpu as pltpu
from jax.sharding import PartitionSpec as P

KERNEL = 32
LANES = 128
WIDE = 256
HALO = 16
EDGE = 8
KEPT, SENT, HALF, OTHER, REST, BLOCKS = 0, 1, 2, 3, 4, 72
EXTRA = 48
F32 = jnp.float32
BF16 = jnp.bfloat16

VMEM = pl.BlockSpec(memory_space=pltpu.VMEM)
SMEM = pl.BlockSpec(memory_space=pltpu.SMEM)
HBM = pl.BlockSpec(memory_space=pltpu.HBM)


def layer_norm(rows, gain, bias):
    values = rows.astype(F32)
    center = jnp.mean(values, axis=-1, keepdims=True)
    values = values - center
    spread = jnp.mean(values * values, axis=-1, keepdims=True)
    return (values * lax.rsqrt(spread + 1e-05) * gain + bias).astype(BF16)


def swish(z):
    return z * jax.nn.sigmoid(z)


def cuts(width, most):
    return [slice(at, at + most) for at in range(0, width, most)]


def valid_rows(first, rows, length):
    index = first + lax.broadcasted_iota(jnp.int32, (rows, 1), 0)
    return index < length


def glu_of(normed, weight_ref, cut, keep):
    value = jnp.dot(normed, weight_ref[0, :, cut], preferred_element_type=F32)
    gate = jnp.dot(normed, weight_ref[1, :, cut], preferred_element_type=F32)
    glu = (value * jax.nn.sigmoid(gate)).astype(BF16)
    return jnp.where(keep, glu.astype(F32), 0.0)


def three_parts(vector):
    parts = []
    for _ in range(3):
        part = vector.astype(BF16).astype(F32)
        parts.append(part)
        vector = vector - part
    return parts


def affine(vectors_ref):
    rows = [vectors_ref[at : at + 1, :] for at in range(vectors_ref.shape[0] - 2)]
    half = len(rows) // 2
    return jnp.concatenate(rows[:half], axis=1), jnp.concatenate(rows[half:], axis=1)


def clear_ends(edge_ref):
    tiles, total, _ = edge_ref.shape
    zeros = jnp.zeros((EDGE, LANES), F32)
    for tile in range(tiles):
        edge_ref[tile, 0:EDGE, :] = zeros
        edge_ref[tile, total - EDGE : total, :] = zeros


def taps_at(taps_ref, offset, tile):
    cut = slice(tile * LANES, (tile + 1) * LANES)
    taps = {}
    for step in range(5):
        tap = 8 * step + offset - 1
        if 0 <= tap < KERNEL:
            taps[step] = jnp.broadcast_to(taps_ref[tap : tap + 1, cut], (8, LANES))
    return taps


def block_conv(block, tile, edge_ref, taps_ref):
    rows = block.shape[0]
    edge_ref[tile, EDGE : EDGE + rows, :] = block
    count = (rows + 2 * HALO) // 8
    total = [None] * count
    for offset in range(8):
        taps = taps_at(taps_ref, offset, tile)
        for at in range(count + 4):
            start = 8 * at + offset - 2 * HALO
            if start <= -8 or start >= rows:
                continue
            values = edge_ref[tile, EDGE + start : EDGE + start + 8, :]
            for step, tap in taps.items():
                if 0 <= at - step < count:
                    term = values * tap
                    seen = total[at - step]
                    total[at - step] = term if seen is None else seen + term
    return total


def first_block_kernel(
    lengths_ref, frames_ref, vectors_ref, taps_ref, weight_ref,
    glu_ref, sums_ref, held_ref, store_ref,
    rows_ref, raw_ref, wide_taps_ref, edge_ref, base_ref, rows_sem, weight_sems, base_sem,
):
    rows = rows_ref.shape[0]
    chans = held_ref.shape[2]
    own = lax.axis_index("tensor")
    rows_copy = pltpu.make_async_copy(frames_ref.at[0], rows_ref, rows_sem)
    rows_copy.start()
    pieces = cuts(chans, WIDE)
    copies = []
    for at, cut in enumerate(pieces):
        for side in range(2):
            place = (side, pl.ds(cut.start, WIDE))
            copy = pltpu.make_async_copy(
                weight_ref.at[place], raw_ref.at[place], weight_sems.at[at, side]
            )
            copy.start()
            copies.append(copy)
    clear_ends(edge_ref)
    keep = valid_rows(own * rows, rows, lengths_ref[0])
    wide_taps_ref[...] = taps_ref[...].astype(F32)
    gain, bias = affine(vectors_ref)
    rows_copy.wait()
    normed = layer_norm(rows_ref[...], gain, bias)
    tiles = chans // LANES
    for shift, half in enumerate((own, 1 - own)):
        for tile in range(tiles):
            lanes = pl.ds(pl.multiple_of((half * tiles + tile) * LANES, LANES), LANES)
            base_ref[shift, tile] = rows_ref[:, lanes].astype(F32)
    base_copy = pltpu.make_async_copy(base_ref, store_ref.at[pl.ds(HALF, 2)], base_sem)
    base_copy.start()
    for at, cut in enumerate(pieces):
        for side in range(2):
            copies[2 * at + side].wait()
            held_ref[side, :, cut] = raw_ref[side, cut, :].T
        glu = glu_of(normed, held_ref, cut, keep)
        glu_ref[:, cut] = glu.astype(BF16)
        for tile in range(cut.start // LANES, cut.stop // LANES):
            seen = slice(tile * LANES - cut.start, (tile + 1) * LANES - cut.start)
            total = block_conv(glu[:, seen], tile, edge_ref, wide_taps_ref)
            for step, each in enumerate(total):
                sums_ref[tile, 8 * step : 8 * step + 8, :] = each
    base_copy.wait()


def last_block_kernel(
    lengths_ref, rows_ref, vectors_ref, taps_ref, weight_ref, first_sums_ref, _,
    late_ref, near_ref, spread_ref, store_ref,
    wide_taps_ref, edge_ref, sums_ref, glu_ref, stats_ref, glu_sems, conv_sems, stats_sem,
):
    rows, chans = glu_ref.shape
    tiles = chans // LANES
    own = lax.axis_index("tensor")
    peer = 1 - own
    length = lengths_ref[0]
    count = length.astype(F32)
    keep = valid_rows(peer * rows, rows, length)
    own_valid, peer_valid = (valid_rows(at * rows, rows, length).astype(F32) for at in (own, peer))
    clear_ends(edge_ref)
    taps = taps_ref[...]
    wide_taps_ref[...] = taps.astype(F32)
    near_ref[HALO : HALO + KERNEL, :] = taps
    last = vectors_ref.shape[0] - 2
    extra = three_parts(vectors_ref[last : last + 1, :])
    extra += three_parts(vectors_ref[last + 1 : last + 2, :])
    extra.append(jnp.zeros((EXTRA - KERNEL - len(extra), chans), F32))
    near_ref[HALO + KERNEL :, :] = jnp.concatenate(extra).astype(BF16)
    reach = rows + 2 * HALO
    own_at = pl.multiple_of(own * rows, rows)
    peer_at = pl.multiple_of(peer * rows, rows)
    for tile in range(tiles):
        sums_ref[tile, pl.ds(peer_at, reach), :] = jnp.zeros((reach, LANES), F32)
        sums_ref[tile, pl.ds(own_at, reach), :] = first_sums_ref[tile]
    normed = layer_norm(rows_ref[...], *affine(vectors_ref))
    copies = []
    for piece, cut in enumerate(cuts(chans, WIDE)):
        glu = glu_of(normed, weight_ref, cut, keep)
        glu_ref[:, cut] = glu.astype(BF16)
        lanes = pl.ds(cut.start, WIDE)
        copies.append(
            pltpu.make_async_copy(glu_ref.at[:, lanes], late_ref.at[:, lanes], glu_sems.at[piece])
        )
        copies[-1].start()
        for tile in range(cut.start // LANES, cut.stop // LANES):
            seen = slice(tile * LANES - cut.start, (tile + 1) * LANES - cut.start)
            for step, each in enumerate(block_conv(glu[:, seen], tile, edge_ref, wide_taps_ref)):
                at = pl.ds(peer_at + 8 * step, 8)
                sums_ref[tile, at, :] = sums_ref[tile, at, :] + each
            own_rows, peer_rows = (pl.ds(at + HALO, rows) for at in (own_at, peer_at))
            for block, place in ((KEPT, own_rows), (SENT, peer_rows)):
                copies.append(
                    pltpu.make_async_copy(
                        sums_ref.at[tile, place], store_ref.at[block, tile], conv_sems.at[tile, block]
                    )
                )
                copies[-1].start()
            kept = sums_ref[tile, own_rows, :]
            sent = sums_ref[tile, peer_rows, :]
            mean = jnp.sum(kept * own_valid, axis=0, keepdims=True)
            mean += jnp.sum(sent * peer_valid, axis=0, keepdims=True)
            mean = mean / count
            high = mean.astype(BF16)
            low = (mean - high.astype(F32)).astype(BF16)
            mean = high.astype(F32) + low.astype(F32)
            off = (kept - mean) * own_valid
            squares = jnp.sum(off * off, axis=0, keepdims=True)
            off = (sent - mean) * peer_valid
            squares += jnp.sum(off * off, axis=0, keepdims=True)
            put_sums(stats_ref, tile, chans, high, low, squares.astype(BF16))
    near = pl.multiple_of(own * (rows - HALO), HALO)
    near_ref[0:HALO, :] = glu_ref[pl.ds(near, HALO), :]
    high = jnp.full((1, LANES), count, F32).astype(BF16)
    low = (jnp.full((1, LANES), count, F32) - high.astype(F32)).astype(BF16)
    stats_ref[0, :, chans + chans // 2 :] = jnp.concatenate([high, low])
    stats = stats_ref[0]
    for at in range(1, stats_ref.shape[0]):
        stats_ref[at] = stats
    copies.append(pltpu.make_async_copy(stats_ref, spread_ref, stats_sem))
    copies[-1].start()
    for copy in copies:
        copy.wait()


def put_sums(spread_ref, tile, chans, high, low, squares):
    lanes = slice(tile * LANES, (tile + 1) * LANES)
    spread_ref[0, :, lanes] = jnp.concatenate([high, low])
    half = chans // 2
    row, at = divmod(tile * LANES, half)
    spread_ref[0, row : row + 1, chans + at : chans + at + LANES] = squares


def turn_kernel(weight_ref, held_ref):
    parts, chans, _ = held_ref.shape
    for place in range(parts):
        for cut in cuts(chans, WIDE):
            at = place * chans
            held_ref[place, cut, :] = weight_ref[:, at + cut.start : at + cut.stop].T


def peer_conv_kernel(
    vectors_ref, near_ref, early_ref, given_ref,
    sent_ref, norms_ref, store_ref,
    edge_ref, wide_taps_ref, rest_ref, part_ref, rest_sem, conv_sem,
):
    rows, chans = early_ref.shape
    own = lax.axis_index("tensor")
    conv_copy = pltpu.make_async_copy(given_ref.at[SENT], sent_ref.at[0], conv_sem)
    conv_copy.start()
    clear_ends(edge_ref)
    taps = near_ref[HALO : HALO + KERNEL, :].astype(F32)
    wide_taps_ref[...] = taps
    extra = near_ref[HALO + KERNEL :, :].astype(F32)
    last = vectors_ref.shape[0] - 2
    norms_ref[0:2, :] = vectors_ref[last:, :]
    norms_ref[2:3, :] = extra[0:1] + (extra[1:2] + extra[2:3])
    norms_ref[3:4, :] = extra[3:4] + (extra[4:5] + extra[5:6])
    norms = norms_ref[...]
    target = pl.multiple_of(jnp.where(own == 0, 0, rows - HALO), HALO)
    source = pl.multiple_of(jnp.where(own == 0, 0, 2 * HALO), HALO)
    eighths = HALO // 8
    for tile in range(chans // LANES):
        lanes = slice(tile * LANES, (tile + 1) * LANES)
        rest_ref[tile, 0:KERNEL, :] = taps[:, lanes]
        rest_ref[tile, KERNEL : KERNEL + 4, :] = norms[:, lanes]
        part_ref[tile] = jnp.zeros((3 * HALO, LANES), F32)
        part_ref[tile, pl.ds(source, HALO), :] = near_ref[0:HALO, lanes].astype(F32)
        total = block_conv(early_ref[:, lanes].astype(F32), tile, edge_ref, wide_taps_ref)
        for at in range(eighths):
            start = KERNEL + 8 + 8 * at
            rest_ref[tile, start : start + 8, :] = jnp.where(own == 0, total[at], total[at - eighths])
        for step in range(rows // 8):
            sent_ref[1, tile, 8 * step : 8 * step + 8, :] = total[step + eighths]
        total = [sent_ref[1, tile, pl.ds(target + 8 * at, 8), :] for at in range(eighths)]
        for tap in range(KERNEL):
            weight = jnp.broadcast_to(wide_taps_ref[tap : tap + 1, lanes], (8, LANES))
            for at in range(eighths):
                start = 8 * at + tap + 1
                total[at] += part_ref[tile, start : start + 8, :] * weight
        for at in range(eighths):
            sent_ref[1, tile, pl.ds(target + 8 * at, 8), :] = total[at]
    rest_copy = pltpu.make_async_copy(rest_ref, store_ref.at[REST], rest_sem)
    rest_copy.start()
    conv_copy.wait()
    rest_copy.wait()


def scales(stats_ref, norms):
    chans = norms.shape[1]
    half = chans // 2
    own = lax.axis_index("tensor")
    found = []
    for shift, place in enumerate((own, 1 - own)):
        seen = stats_ref[:, pl.ds(place, 1), :, :].astype(F32)
        both = seen[:, :, 0:1, :] + seen[:, :, 1:2, :]
        means, counts = both[..., :chans], both[..., chans + half : chans + half + 1]
        squares = jnp.concatenate([seen[:, :, at : at + 1, chans : chans + half] for at in range(2)], axis=-1)
        count = jnp.sum(counts, axis=0)[0]
        mean = jnp.sum(means * counts, axis=0)[0] / count
        off = means - mean
        var = jnp.sum(squares + counts * off * off, axis=0)[0] / count
        scale = lax.rsqrt(var + 1e-05) * norms[2 * shift : 2 * shift + 1]
        found.append((mean, scale, norms[2 * shift + 1 : 2 * shift + 2]))
    return found


def branch_rows(found, conv_of, weight_ref):
    own = lax.axis_index("tensor")
    total = None
    for shift, (mean, scale, bias) in reversed(list(enumerate(found))):
        acts = []
        for tile in range(mean.shape[1] // LANES):
            lanes = slice(tile * LANES, (tile + 1) * LANES)
            z = (conv_of(shift, tile) - mean[:, lanes]) * scale[:, lanes] + bias[:, lanes]
            acts.append(swish(z).astype(BF16))
        place = own if shift == 0 else 1 - own
        term = jnp.dot(jnp.concatenate(acts, axis=1), weight_ref[place], preferred_element_type=F32)
        total = term if total is None else total + term
    return total


def sent_kernel(stats_ref, conv_ref, norms_ref, weight_ref, out_ref):
    found = scales(stats_ref, norms_ref[...])
    branch = branch_rows(found, lambda shift, tile: conv_ref[shift, tile], weight_ref)
    out_ref[...] = branch.astype(BF16)


def columns(ref, place, cols):
    return ref.at[:, pl.ds(pl.multiple_of(place * cols, LANES), cols)]


def kept_kernel(
    stats_ref, late_ref, weight_ref, store_ref,
    mine_ref, base_ref, rest_ref, edge_ref, wide_taps_ref, conv_ref, sums_ref, glu_ref, half_ref, sems,
):
    own = lax.axis_index("tensor")
    rows, _ = mine_ref.shape
    tiles = conv_ref.shape[0]
    copies = [
        (store_ref.at[REST], rest_ref),
        (late_ref, glu_ref),
        (store_ref.at[KEPT], conv_ref),
        (store_ref.at[HALF], half_ref),
        (store_ref.at[OTHER], base_ref),
    ]
    copies = [pltpu.make_async_copy(*pair, sems.at[at]) for at, pair in enumerate(copies)]
    for copy in copies:
        copy.start()
    clear_ends(edge_ref)
    target = pl.multiple_of(jnp.where(own == 0, rows - HALO, 0), HALO)
    copies[0].wait()
    copies[1].wait()
    for tile in range(tiles):
        lanes = slice(tile * LANES, (tile + 1) * LANES)
        wide_taps_ref[:, lanes] = rest_ref[tile, 0:KERNEL, :]
        total = block_conv(glu_ref[:, lanes].astype(F32), tile, edge_ref, wide_taps_ref)
        for step in range(rows // 8):
            sums_ref[tile, 8 * step : 8 * step + 8, :] = total[step + HALO // 8]
        for at in range(HALO // 8):
            place, start = pl.ds(target + 8 * at, 8), KERNEL + 8 + 8 * at
            sums_ref[tile, place, :] = sums_ref[tile, place, :] + rest_ref[tile, start : start + 8, :]
    norms = [rest_ref[tile, KERNEL : KERNEL + 4, :] for tile in range(tiles)]
    found = scales(stats_ref, jnp.concatenate(norms, axis=1))
    copies[2].wait()
    branch = branch_rows(found, lambda shift, tile: (sums_ref if shift else conv_ref)[tile], weight_ref)
    copies[3].wait()
    for tile in range(tiles):
        lanes = slice(tile * LANES, (tile + 1) * LANES)
        mine_ref[:, lanes] = (half_ref[tile] + branch[:, lanes]).astype(BF16)
    copies[4].wait()


def finish_kernel(mine_ref, base_ref, got_ref, out_ref, done_ref, sems):
    own = lax.axis_index("tensor")
    rows, cols = mine_ref.shape
    copies = [pltpu.make_async_copy(mine_ref, columns(out_ref, own, cols), sems.at[0])]
    copies[0].start()
    for tile in range(cols // LANES):
        lanes = slice(tile * LANES, (tile + 1) * LANES)
        done_ref[:, lanes] = (base_ref[tile] + got_ref[:, lanes].astype(F32)).astype(BF16)
    copies.append(pltpu.make_async_copy(done_ref, columns(out_ref, 1 - own, cols), sems.at[1]))
    copies[1].start()
    for copy in copies:
        copy.wait()


def shape(dims, kind):
    return jax.ShapeDtypeStruct(dims, kind)


def call(kernel, outs, in_specs, operands, out_specs=None, scratch=(), name=None, aliases=None, room=32):
    return pl.pallas_call(
        kernel,
        out_shape=tuple(outs),
        in_specs=list(in_specs),
        out_specs=tuple(out_specs or [VMEM] * len(outs)),
        scratch_shapes=list(scratch),
        input_output_aliases=aliases or {},
        compiler_params=pltpu.CompilerParams(vmem_limit_bytes=room * 1024 * 1024),
        name=name,
    )(*operands)


def two_parts(
    devices, frames_in, lengths, ln_gain, ln_bias, glu_weight, conv_kernel, bn_gain, bn_bias, out_weight
):
    _, span, width = frames_in.shape
    chans = glu_weight.shape[1]
    cols = out_weight.shape[0]
    tiles = chans // LANES
    pieces = chans // WIDE

    def swap(value):
        return lax.ppermute(value, "tensor", [(0, 1), (1, 0)])

    frames = swap(frames_in[0])
    vectors = jnp.concatenate([ln_gain, ln_bias, bn_gain, bn_bias]).reshape(-1, chans)
    edge = pltpu.VMEM((tiles, span + 2 * EDGE, LANES), F32)
    wide_taps = pltpu.VMEM((KERNEL, chans), F32)
    dma = pltpu.SemaphoreType.DMA
    reach = shape((tiles, span + 2 * HALO, LANES), F32)
    block = shape((tiles, span, LANES), F32)
    rest = pltpu.VMEM(block.shape, F32)
    store = shape((BLOCKS,) + block.shape, F32)
    early, first_sums, held, store_first = call(
        first_block_kernel,
        (shape((span, chans), BF16), reach, shape((2, width, chans), BF16), store),
        [SMEM, HBM, VMEM, VMEM, HBM],
        (lengths, frames_in, vectors, conv_kernel, glu_weight),
        out_specs=(VMEM, VMEM, VMEM, HBM),
        scratch=(
            pltpu.VMEM((span, width), BF16),
            pltpu.VMEM((2, chans, width), BF16),
            wide_taps,
            edge,
            pltpu.VMEM((2,) + block.shape, F32),
            dma,
            dma((pieces, 2)),
            dma,
        ),
        name="first_block",
        room=48,
    )
    early = swap(early)
    late, near, spread, store_second = call(
        last_block_kernel,
        (
            shape((span, chans), BF16),
            shape((HALO + EXTRA, chans), BF16),
            shape((devices, 2, chans + chans // 2 + LANES), BF16),
            store,
        ),
        [SMEM] + [VMEM] * 5 + [HBM],
        (lengths, frames, vectors, conv_kernel, held, first_sums, store_first),
        out_specs=(HBM, VMEM, HBM, HBM),
        scratch=(
            wide_taps,
            edge,
            pltpu.VMEM((tiles, 2 * span + 2 * HALO, LANES), F32),
            pltpu.VMEM((span, chans), BF16),
            pltpu.VMEM((devices, 2, chans + chans // 2 + LANES), BF16),
            dma((pieces,)),
            dma((tiles, 2)),
            dma,
        ),
        aliases={6: 3},
        name="last_block",
        room=40,
    )
    spread, early, out_weight = lax.optimization_barrier((spread, early, out_weight))
    stats = lax.all_to_all(spread, ("dp", "tensor"), split_axis=0, concat_axis=0, tiled=True)
    stats = stats.reshape((devices // 2, 2) + spread.shape[1:])
    near, late = swap(near), swap(late)
    (weight,) = call(turn_kernel, (shape((2, chans, cols), BF16),), [VMEM], (out_weight,), name="turn")
    sent_conv, norms, store_third = call(
        peer_conv_kernel,
        (shape((2,) + block.shape, F32), shape((4, chans), F32), store),
        [VMEM, VMEM, VMEM, HBM],
        (vectors, near, early, store_second),
        out_specs=(VMEM, VMEM, HBM),
        scratch=(edge, wide_taps, rest, pltpu.VMEM((tiles, 3 * HALO, LANES), F32), dma, dma),
        aliases={3: 2},
        name="peer_conv",
        room=40,
    )
    (sent,) = call(
        sent_kernel,
        (shape((span, cols), BF16),),
        [VMEM] * 4,
        (stats, sent_conv, norms, weight),
        name="branch_sent",
    )
    got = swap(sent)
    mine, base = call(
        kept_kernel,
        (shape((span, cols), BF16), block),
        [VMEM, HBM, VMEM, HBM],
        (stats, late, weight, store_third),
        scratch=(
            rest,
            edge,
            wide_taps,
            pltpu.VMEM(block.shape, F32),
            pltpu.VMEM(block.shape, F32),
            pltpu.VMEM((span, chans), BF16),
            pltpu.VMEM(block.shape, F32),
            dma((5,)),
        ),
        name="branch_kept",
    )
    (out,) = call(
        finish_kernel,
        (shape((span, width), BF16),),
        [VMEM] * 3,
        (mine, base, got),
        out_specs=(HBM,),
        scratch=(pltpu.VMEM((span, cols), BF16), dma((2,))),
        name="residual",
    )
    return out[None]


def contract_last(left, right):
    return lax.dot_general(
        left, right, (((1,), (1,)), ((), ())), preferred_element_type=F32
    )


def many_parts(
    devices, frames_in, lengths, ln_gain, ln_bias, glu_weight, conv_kernel, bn_gain, bn_bias, out_weight
):
    rows = frames_in[0]
    chans = glu_weight.shape[1]
    normed = layer_norm(rows, ln_gain, ln_bias)
    proj = contract_last(
        lax.all_gather(normed, "tensor", axis=0, tiled=True),
        glu_weight.reshape(2 * chans, rows.shape[1]),
    )
    valid = valid_rows(0, proj.shape[0], lengths[0])
    glu = (proj[:, :chans] * jax.nn.sigmoid(proj[:, chans:])).astype(BF16)
    glu = jnp.where(valid, glu, jnp.zeros_like(glu)).astype(F32)
    padded = jnp.pad(glu, ((15, KERNEL - 16), (0, 0)))
    taps = conv_kernel.astype(F32)
    conv = jnp.zeros_like(glu)
    for tap in range(KERNEL):
        conv = conv + padded[tap : tap + glu.shape[0]] * taps[tap]
    own = lengths[0].astype(F32)
    local = jnp.sum(jnp.where(valid, conv, 0.0), axis=0) / own
    squares = jnp.sum(jnp.where(valid, conv - local, 0.0) ** 2, axis=0)
    count = lax.psum(own, "dp")
    mean = lax.psum(local * own, "dp") / count
    var = lax.psum(squares + own * (local - mean) ** 2, "dp") / count
    z = (conv - mean) * (lax.rsqrt(var + 1e-05) * bn_gain) + bn_bias
    act = lax.all_gather(swish(z).astype(BF16), "tensor", axis=1, tiled=True)
    branch = contract_last(act, out_weight)
    branch = lax.all_to_all(branch, "tensor", split_axis=0, concat_axis=1, tiled=True)
    return (rows.astype(F32) + branch).astype(BF16)[None]


def solution(mesh):
    sizes = dict(mesh.shape)
    body = two_parts if sizes["tensor"] == 2 else many_parts
    body = functools.partial(body, sizes["tensor"] * sizes["dp"])
    return jax.shard_map(
        body,
        mesh=mesh,
        in_specs=(
            P("dp", "tensor", None),
            P("dp"),
            P(),
            P(),
            P(None, "tensor", None),
            P(None, "tensor"),
            P("tensor"),
            P("tensor"),
            P("tensor", None),
        ),
        out_specs=P("dp", "tensor", None),
        check_vma=False,
    )
```

```python
import functools

import jax
import jax.numpy as jnp
from jax import lax
from jax.experimental import pallas as pl
from jax.experimental.pallas import tpu as pltpu
from jax.sharding import PartitionSpec as P

KERNEL = 32
LANES = 128
WIDE = 256
HALO = 16
EDGE = 8
KEPT, SENT, HALF, OTHER, BLOCKS = 0, 1, 2, 3, 72
EXTRA = 8
F32 = jnp.float32
BF16 = jnp.bfloat16

VMEM = pl.BlockSpec(memory_space=pltpu.VMEM)
SMEM = pl.BlockSpec(memory_space=pltpu.SMEM)
HBM = pl.BlockSpec(memory_space=pltpu.HBM)


def layer_norm(rows, gain, bias):
    values = rows.astype(F32)
    center = jnp.mean(values, axis=-1, keepdims=True)
    values = values - center
    spread = jnp.mean(values * values, axis=-1, keepdims=True)
    return (values * lax.rsqrt(spread + 1e-05) * gain + bias).astype(BF16)


def swish(z):
    return z * jax.nn.sigmoid(z)


def cuts(width, most):
    return [slice(at, at + most) for at in range(0, width, most)]


def valid_rows(first, rows, length):
    index = first + lax.broadcasted_iota(jnp.int32, (rows, 1), 0)
    return index < length


def glu_of(normed, weight_ref, cut, keep):
    value = jnp.dot(normed, weight_ref[0, :, cut], preferred_element_type=F32)
    gate = jnp.dot(normed, weight_ref[1, :, cut], preferred_element_type=F32)
    glu = (value * jax.nn.sigmoid(gate)).astype(BF16)
    return jnp.where(keep, glu.astype(F32), 0.0)


def three_parts(vector):
    parts = []
    for _ in range(3):
        part = vector.astype(BF16).astype(F32)
        parts.append(part)
        vector = vector - part
    return parts


def affine(vectors_ref):
    rows = [vectors_ref[at : at + 1, :] for at in range(vectors_ref.shape[0] - 2)]
    half = len(rows) // 2
    return jnp.concatenate(rows[:half], axis=1), jnp.concatenate(rows[half:], axis=1)


def clear_ends(edge_ref):
    tiles, total, _ = edge_ref.shape
    zeros = jnp.zeros((EDGE, LANES), F32)
    for tile in range(tiles):
        edge_ref[tile, 0:EDGE, :] = zeros
        edge_ref[tile, total - EDGE : total, :] = zeros


def taps_at(taps_ref, offset, tile):
    cut = slice(tile * LANES, (tile + 1) * LANES)
    taps = {}
    for step in range(5):
        tap = 8 * step + offset - 1
        if 0 <= tap < KERNEL:
            taps[step] = jnp.broadcast_to(taps_ref[tap : tap + 1, cut], (8, LANES))
    return taps


def block_conv(block, tile, edge_ref, taps_ref):
    rows = block.shape[0]
    edge_ref[tile, EDGE : EDGE + rows, :] = block
    count = (rows + 2 * HALO) // 8
    total = [None] * count
    for offset in range(8):
        taps = taps_at(taps_ref, offset, tile)
        for at in range(count + 4):
            start = 8 * at + offset - 2 * HALO
            if start <= -8 or start >= rows:
                continue
            values = edge_ref[tile, EDGE + start : EDGE + start + 8, :]
            for step, tap in taps.items():
                if 0 <= at - step < count:
                    term = values * tap
                    seen = total[at - step]
                    total[at - step] = term if seen is None else seen + term
    return total


def half_lanes(tile, tiles):
    half, place = divmod(tile, tiles // 2)
    return half, slice(place * LANES, (place + 1) * LANES)


def first_block_kernel(
    lengths_ref, frames_ref, vectors_ref, taps_ref, weight_ref,
    soon_ref, later_ref, sums_ref, held_ref, pivot_ref, store_ref,
    rows_ref, raw_ref, wide_taps_ref, edge_ref, base_ref, rows_sem, weight_sems, base_sem,
):
    rows = rows_ref.shape[0]
    chans = held_ref.shape[2]
    own = lax.axis_index("tensor")
    rows_copy = pltpu.make_async_copy(frames_ref.at[0], rows_ref, rows_sem)
    rows_copy.start()
    pieces = cuts(chans, WIDE)
    copies = []
    for at, cut in enumerate(pieces):
        for side in range(2):
            place = (side, pl.ds(cut.start, WIDE))
            copy = pltpu.make_async_copy(
                weight_ref.at[place], raw_ref.at[place], weight_sems.at[at, side]
            )
            copy.start()
            copies.append(copy)
    clear_ends(edge_ref)
    keep = valid_rows(own * rows, rows, lengths_ref[0])
    wide_taps_ref[...] = taps_ref[...].astype(F32)
    gain, bias = affine(vectors_ref)
    rows_copy.wait()
    normed = layer_norm(rows_ref[...], gain, bias)
    tiles = chans // LANES
    for shift, half in enumerate((own, 1 - own)):
        for tile in range(tiles):
            lanes = pl.ds(pl.multiple_of((half * tiles + tile) * LANES, LANES), LANES)
            base_ref[shift, tile] = rows_ref[:, lanes].astype(F32)
    base_copy = pltpu.make_async_copy(base_ref, store_ref.at[pl.ds(HALF, 2)], base_sem)
    base_copy.start()
    for at, cut in enumerate(pieces):
        for side in range(2):
            copies[2 * at + side].wait()
            held_ref[side, :, cut] = raw_ref[side, cut, :].T
        glu = glu_of(normed, held_ref, cut, keep)
        for tile in range(cut.start // LANES, cut.stop // LANES):
            seen = slice(tile * LANES - cut.start, (tile + 1) * LANES - cut.start)
            total = block_conv(glu[:, seen], tile, edge_ref, wide_taps_ref)
            for step, each in enumerate(total):
                sums_ref[tile, 8 * step : 8 * step + 8, :] = each
            lanes = slice(tile * LANES, (tile + 1) * LANES)
            conv = sums_ref[tile, HALO : HALO + rows, :]
            pivot = jnp.sum(conv, axis=0, keepdims=True) * (1.0 / rows)
            pivot = pivot.astype(BF16).astype(F32)
            pivot_ref[:, lanes] = pivot
            half, there = half_lanes(tile, tiles)
            (soon_ref, later_ref)[half][:, there] = (conv - pivot).astype(BF16)
    base_copy.wait()


def last_block_kernel(
    lengths_ref, rows_ref, vectors_ref, taps_ref, weight_ref, first_sums_ref, pivot_ref, later_ref, _,
    late_ref, tail_ref, spread_ref, store_ref,
    wide_taps_ref, edge_ref, conv_ref, mask_ref, peer_rows_ref, stats_ref, late_sems, conv_sems, stats_sem,
):
    rows, chans = peer_rows_ref.shape
    tiles = chans // LANES
    own = lax.axis_index("tensor")
    peer = 1 - own
    length = lengths_ref[0]
    count = length.astype(F32)
    keep = valid_rows(peer * rows, rows, length)
    for at, place in enumerate((own, peer)):
        valid = valid_rows(place * rows, rows, length).astype(F32)
        mask_ref[at] = jnp.broadcast_to(valid, (rows, LANES))
    first_one = (own == 0).astype(F32)
    last_one = 1.0 - first_one
    clear_ends(edge_ref)
    wide_taps_ref[...] = taps_ref[...].astype(F32)
    last = vectors_ref.shape[0] - 2
    extra = three_parts(vectors_ref[last : last + 1, :])
    extra += three_parts(vectors_ref[last + 1 : last + 2, :])
    extra.append(pivot_ref[...])
    extra.append(jnp.zeros((EXTRA - len(extra), chans), F32))
    extra = jnp.concatenate(extra)
    wide = chans // 2
    tail_ref[0:rows, :] = later_ref[...]
    tail_ref[rows + 2 * HALO :, :] = jnp.concatenate([extra[:, :wide], extra[:, wide:]]).astype(BF16)
    normed = layer_norm(rows_ref[...], *affine(vectors_ref))
    copies = []
    for cut in cuts(chans, WIDE):
        glu = glu_of(normed, weight_ref, cut, keep)
        for tile in range(cut.start // LANES, cut.stop // LANES):
            seen = slice(tile * LANES - cut.start, (tile + 1) * LANES - cut.start)
            lanes = slice(tile * LANES, (tile + 1) * LANES)
            total = block_conv(glu[:, seen], tile, edge_ref, wide_taps_ref)
            first = [first_sums_ref[tile, 8 * at : 8 * at + 8, :] for at in range(len(total))]
            kept, sent = first[2:-2], total[2:-2]
            for at in range(2):
                kept[at] += total[at - 2] * last_one
                kept[at - 2] += total[at] * first_one
                sent[at] += first[at - 2] * first_one
                sent[at - 2] += first[at] * last_one
            near = jnp.concatenate(kept[:2]) * last_one + jnp.concatenate(kept[-2:]) * first_one
            kept, sent = jnp.concatenate(kept), jnp.concatenate(sent)
            for block, conv in ((KEPT, kept), (SENT, sent)):
                conv_ref[block, tile] = conv
                copies.append(
                    pltpu.make_async_copy(
                        conv_ref.at[block, tile], store_ref.at[block, tile], conv_sems.at[tile, block]
                    )
                )
                copies[-1].start()
            pivot = pivot_ref[:, lanes]
            near = (near - pivot).astype(BF16)
            half, there = half_lanes(tile, tiles)
            tail_ref[rows + half * HALO : rows + (half + 1) * HALO, there] = near
            peer_rows_ref[:, lanes] = (sent - pivot).astype(BF16)
            copies.append(
                pltpu.make_async_copy(
                    peer_rows_ref.at[:, pl.ds(lanes.start, LANES)],
                    late_ref.at[:, pl.ds(lanes.start, LANES)],
                    late_sems.at[tile],
                )
            )
            copies[-1].start()
            mean = jnp.sum(kept * mask_ref[0] + sent * mask_ref[1], axis=0, keepdims=True)
            mean = mean / count
            high = mean.astype(BF16)
            low = (mean - high.astype(F32)).astype(BF16)
            mean = high.astype(F32) + low.astype(F32)
            kept, sent = (kept - mean) * mask_ref[0], (sent - mean) * mask_ref[1]
            squares = jnp.sum(kept * kept + sent * sent, axis=0, keepdims=True)
            put_sums(stats_ref, tile, chans, high, low, squares.astype(BF16))
    high = jnp.full((1, LANES), count, F32).astype(BF16)
    low = (jnp.full((1, LANES), count, F32) - high.astype(F32)).astype(BF16)
    stats_ref[0, :, chans + chans // 2 :] = jnp.concatenate([high, low])
    stats = stats_ref[0]
    for at in range(1, stats_ref.shape[0]):
        stats_ref[at] = stats
    copies.append(pltpu.make_async_copy(stats_ref, spread_ref, stats_sem))
    copies[-1].start()
    for copy in copies:
        copy.wait()


def put_sums(spread_ref, tile, chans, high, low, squares):
    lanes = slice(tile * LANES, (tile + 1) * LANES)
    spread_ref[0, :, lanes] = jnp.concatenate([high, low])
    half = chans // 2
    row, at = divmod(tile * LANES, half)
    spread_ref[0, row : row + 1, chans + at : chans + at + LANES] = squares


def turn_kernel(weight_ref, vectors_ref, store_ref, held_ref, conv_ref, norms_ref, sem):
    parts, chans, _ = held_ref.shape
    copy = pltpu.make_async_copy(store_ref.at[SENT], conv_ref, sem)
    copy.start()
    norms_ref[...] = vectors_ref[vectors_ref.shape[0] - 2 :, :]
    for place in range(parts):
        for cut in cuts(chans, WIDE):
            at = place * chans
            held_ref[place, cut, :] = weight_ref[:, at + cut.start : at + cut.stop].T
    copy.wait()


def peer_vectors(tail_ref):
    first = tail_ref.shape[0] - 2 * EXTRA
    parts = tail_ref[first:, :].astype(F32)
    parts = jnp.concatenate([parts[:EXTRA], parts[EXTRA:]], axis=1)
    gain, bias = (parts[at : at + 1] + (parts[at + 1 : at + 2] + parts[at + 2 : at + 3]) for at in (0, 3))
    return gain, bias, parts[6:7]


def scales(stats_ref, norms_ref, tail_ref):
    chans = norms_ref.shape[1]
    gain, bias, pivot = peer_vectors(tail_ref)
    norms = [(norms_ref[0:1, :], norms_ref[1:2, :], 0.0), (gain, bias, pivot)]
    half = chans // 2
    own = lax.axis_index("tensor")
    found = []
    for shift, place in enumerate((own, 1 - own)):
        seen = stats_ref[:, pl.ds(place, 1), :, :].astype(F32)
        both = seen[:, :, 0:1, :] + seen[:, :, 1:2, :]
        means, counts = both[..., :chans], both[..., chans + half : chans + half + 1]
        squares = jnp.concatenate([seen[:, :, at : at + 1, chans : chans + half] for at in range(2)], axis=-1)
        count = jnp.sum(counts, axis=0)[0]
        mean = jnp.sum(means * counts, axis=0)[0] / count
        off = means - mean
        var = jnp.sum(squares + counts * off * off, axis=0)[0] / count
        gain, bias, pivot = norms[shift]
        found.append((mean - pivot, lax.rsqrt(var + 1e-05) * gain, bias))
    return found


def branch_rows(found, conv_ref, peer_ref, weight_ref):
    own = lax.axis_index("tensor")
    total = None
    for shift in (1, 0):
        mean, scale, bias = found[shift]
        acts = []
        for tile in range(conv_ref.shape[0]):
            lanes = slice(tile * LANES, (tile + 1) * LANES)
            conv = peer_ref[:, lanes].astype(F32) if shift else conv_ref[tile]
            z = (conv - mean[:, lanes]) * scale[:, lanes] + bias[:, lanes]
            acts.append(swish(z).astype(BF16))
        place = 1 - own if shift else own
        term = jnp.dot(jnp.concatenate(acts, axis=1), weight_ref[place], preferred_element_type=F32)
        total = term if total is None else total + term
    return total


def sent_kernel(stats_ref, conv_ref, soon_ref, tail_ref, norms_ref, weight_ref, out_ref, peer_ref):
    rows, wide = soon_ref.shape
    target = pl.multiple_of(jnp.where(lax.axis_index("tensor") == 0, 0, rows - HALO), HALO)
    peer_ref[:, :wide] = soon_ref[...]
    peer_ref[:, wide:] = tail_ref[0:rows, :]
    peer_ref[pl.ds(target, HALO), :wide] = tail_ref[rows : rows + HALO, :]
    peer_ref[pl.ds(target, HALO), wide:] = tail_ref[rows + HALO : rows + 2 * HALO, :]
    found = scales(stats_ref, norms_ref, tail_ref)
    branch = branch_rows(found, conv_ref, peer_ref, weight_ref)
    out_ref[...] = branch.astype(BF16)


def columns(ref, place, cols):
    return ref.at[:, pl.ds(pl.multiple_of(place * cols, LANES), cols)]


def kept_kernel(
    stats_ref, late_ref, tail_ref, norms_ref, weight_ref, store_ref,
    mine_ref, base_ref, conv_ref, half_ref, sems,
):
    copies = [
        (store_ref.at[KEPT], conv_ref),
        (store_ref.at[HALF], half_ref),
        (store_ref.at[OTHER], base_ref),
    ]
    copies = [pltpu.make_async_copy(*pair, sems.at[at]) for at, pair in enumerate(copies)]
    for copy in copies:
        copy.start()
    found = scales(stats_ref, norms_ref, tail_ref)
    copies[0].wait()
    branch = branch_rows(found, conv_ref, late_ref, weight_ref)
    copies[1].wait()
    for tile in range(conv_ref.shape[0]):
        lanes = slice(tile * LANES, (tile + 1) * LANES)
        mine_ref[:, lanes] = (half_ref[tile] + branch[:, lanes]).astype(BF16)
    copies[2].wait()


def finish_kernel(mine_ref, base_ref, got_ref, out_ref, done_ref, sems):
    own = lax.axis_index("tensor")
    rows, cols = mine_ref.shape
    copies = [pltpu.make_async_copy(mine_ref, columns(out_ref, own, cols), sems.at[0])]
    copies[0].start()
    for tile in range(cols // LANES):
        lanes = slice(tile * LANES, (tile + 1) * LANES)
        done_ref[:, lanes] = (base_ref[tile] + got_ref[:, lanes].astype(F32)).astype(BF16)
    copies.append(pltpu.make_async_copy(done_ref, columns(out_ref, 1 - own, cols), sems.at[1]))
    copies[1].start()
    for copy in copies:
        copy.wait()


def shape(dims, kind):
    return jax.ShapeDtypeStruct(dims, kind)


def call(kernel, outs, in_specs, operands, out_specs=None, scratch=(), name=None, aliases=None, room=32):
    return pl.pallas_call(
        kernel,
        out_shape=tuple(outs),
        in_specs=list(in_specs),
        out_specs=tuple(out_specs or [VMEM] * len(outs)),
        scratch_shapes=list(scratch),
        input_output_aliases=aliases or {},
        compiler_params=pltpu.CompilerParams(vmem_limit_bytes=room * 1024 * 1024),
        name=name,
    )(*operands)


def two_parts(
    devices, frames_in, lengths, ln_gain, ln_bias, glu_weight, conv_kernel, bn_gain, bn_bias, out_weight
):
    _, span, width = frames_in.shape
    chans = glu_weight.shape[1]
    cols = out_weight.shape[0]
    tiles = chans // LANES
    pieces = chans // WIDE

    def swap(value):
        return lax.ppermute(value, "tensor", [(0, 1), (1, 0)])

    frames = swap(frames_in[0])
    vectors = jnp.concatenate([ln_gain, ln_bias, bn_gain, bn_bias]).reshape(-1, chans)
    edge = pltpu.VMEM((tiles, span + 2 * EDGE, LANES), F32)
    wide_taps = pltpu.VMEM((KERNEL, chans), F32)
    dma = pltpu.SemaphoreType.DMA
    reach = shape((tiles, span + 2 * HALO, LANES), F32)
    block = shape((tiles, span, LANES), F32)
    store = shape((BLOCKS,) + block.shape, F32)
    soon, later, first_sums, held, pivot, store_first = call(
        first_block_kernel,
        (
            shape((span, chans // 2), BF16),
            shape((span, chans // 2), BF16),
            reach,
            shape((2, width, chans), BF16),
            shape((1, chans), F32),
            store,
        ),
        [SMEM, HBM, VMEM, VMEM, HBM],
        (lengths, frames_in, vectors, conv_kernel, glu_weight),
        out_specs=(VMEM,) * 5 + (HBM,),
        scratch=(
            pltpu.VMEM((span, width), BF16),
            pltpu.VMEM((2, chans, width), BF16),
            wide_taps,
            edge,
            pltpu.VMEM((2,) + block.shape, F32),
            dma,
            dma((pieces, 2)),
            dma,
        ),
        name="first_block",
        room=48,
    )
    soon = swap(soon)
    late, tail, spread, store_second = call(
        last_block_kernel,
        (
            shape((span, chans), BF16),
            shape((span + 2 * HALO + 2 * EXTRA, chans // 2), BF16),
            shape((devices, 2, chans + chans // 2 + LANES), BF16),
            store,
        ),
        [SMEM] + [VMEM] * 7 + [HBM],
        (lengths, frames, vectors, conv_kernel, held, first_sums, pivot, later, store_first),
        out_specs=(HBM, VMEM, HBM, HBM),
        scratch=(
            wide_taps,
            edge,
            pltpu.VMEM((2, tiles, span, LANES), F32),
            pltpu.VMEM((2, span, LANES), F32),
            pltpu.VMEM((span, chans), BF16),
            pltpu.VMEM((devices, 2, chans + chans // 2 + LANES), BF16),
            dma((tiles,)),
            dma((tiles, 2)),
            dma,
        ),
        aliases={8: 3},
        name="last_block",
        room=40,
    )
    spread, soon, out_weight = lax.optimization_barrier((spread, soon, out_weight))
    stats = lax.all_to_all(spread, ("dp", "tensor"), split_axis=0, concat_axis=0, tiled=True)
    stats = stats.reshape((devices // 2, 2) + spread.shape[1:])
    tail, late = swap(tail), swap(late)
    weight, sent_conv, norms = call(
        turn_kernel,
        (shape((2, chans, cols), BF16), block, shape((2, chans), F32)),
        [VMEM, VMEM, HBM],
        (out_weight, vectors, store_second),
        scratch=(dma,),
        name="turn",
    )
    (sent,) = call(
        sent_kernel,
        (shape((span, cols), BF16),),
        [VMEM] * 6,
        (stats, sent_conv, soon, tail, norms, weight),
        scratch=(pltpu.VMEM((span, chans), BF16),),
        name="branch_sent",
    )
    got = swap(sent)
    mine, base = call(
        kept_kernel,
        (shape((span, cols), BF16), block),
        [VMEM] * 5 + [HBM],
        (stats, late, tail, norms, weight, store_second),
        scratch=(pltpu.VMEM(block.shape, F32), pltpu.VMEM(block.shape, F32), dma((3,))),
        name="branch_kept",
    )
    (out,) = call(
        finish_kernel,
        (shape((span, width), BF16),),
        [VMEM] * 3,
        (mine, base, got),
        out_specs=(HBM,),
        scratch=(pltpu.VMEM((span, cols), BF16), dma((2,))),
        name="residual",
    )
    return out[None]


def contract_last(left, right):
    return lax.dot_general(
        left, right, (((1,), (1,)), ((), ())), preferred_element_type=F32
    )


def many_parts(
    devices, frames_in, lengths, ln_gain, ln_bias, glu_weight, conv_kernel, bn_gain, bn_bias, out_weight
):
    rows = frames_in[0]
    chans = glu_weight.shape[1]
    normed = layer_norm(rows, ln_gain, ln_bias)
    proj = contract_last(
        lax.all_gather(normed, "tensor", axis=0, tiled=True),
        glu_weight.reshape(2 * chans, rows.shape[1]),
    )
    valid = valid_rows(0, proj.shape[0], lengths[0])
    glu = (proj[:, :chans] * jax.nn.sigmoid(proj[:, chans:])).astype(BF16)
    glu = jnp.where(valid, glu, jnp.zeros_like(glu)).astype(F32)
    padded = jnp.pad(glu, ((15, KERNEL - 16), (0, 0)))
    taps = conv_kernel.astype(F32)
    conv = jnp.zeros_like(glu)
    for tap in range(KERNEL):
        conv = conv + padded[tap : tap + glu.shape[0]] * taps[tap]
    own = lengths[0].astype(F32)
    local = jnp.sum(jnp.where(valid, conv, 0.0), axis=0) / own
    squares = jnp.sum(jnp.where(valid, conv - local, 0.0) ** 2, axis=0)
    count = lax.psum(own, "dp")
    mean = lax.psum(local * own, "dp") / count
    var = lax.psum(squares + own * (local - mean) ** 2, "dp") / count
    z = (conv - mean) * (lax.rsqrt(var + 1e-05) * bn_gain) + bn_bias
    act = lax.all_gather(swish(z).astype(BF16), "tensor", axis=1, tiled=True)
    branch = contract_last(act, out_weight)
    branch = lax.all_to_all(branch, "tensor", split_axis=0, concat_axis=1, tiled=True)
    return (rows.astype(F32) + branch).astype(BF16)[None]


def solution(mesh):
    sizes = dict(mesh.shape)
    body = two_parts if sizes["tensor"] == 2 else many_parts
    body = functools.partial(body, sizes["tensor"] * sizes["dp"])
    return jax.shard_map(
        body,
        mesh=mesh,
        in_specs=(
            P("dp", "tensor", None),
            P("dp"),
            P(),
            P(),
            P(None, "tensor", None),
            P(None, "tensor"),
            P("tensor"),
            P("tensor"),
            P("tensor", None),
        ),
        out_specs=P("dp", "tensor", None),
        check_vma=False,
    )
```

```python
import functools

import jax
import jax.numpy as jnp
from jax import lax
from jax.experimental import pallas as pl
from jax.experimental.pallas import tpu as pltpu
from jax.sharding import PartitionSpec as P

KERNEL = 32
LANES = 128
WIDE = 256
HALO = 16
EDGE = 8
KEPT, SENT, HALF, OTHER, BLOCKS = 0, 1, 2, 3, 72
EXTRA = 8
F32 = jnp.float32
BF16 = jnp.bfloat16

VMEM = pl.BlockSpec(memory_space=pltpu.VMEM)
SMEM = pl.BlockSpec(memory_space=pltpu.SMEM)
HBM = pl.BlockSpec(memory_space=pltpu.HBM)


def layer_norm(rows, gain, bias):
    values = rows.astype(F32)
    center = jnp.mean(values, axis=-1, keepdims=True)
    values = values - center
    spread = jnp.mean(values * values, axis=-1, keepdims=True)
    return (values * lax.rsqrt(spread + 1e-05) * gain + bias).astype(BF16)


def swish(z):
    return z * jax.nn.sigmoid(z)


def cuts(width, most):
    return [slice(at, at + most) for at in range(0, width, most)]


def valid_rows(first, rows, length):
    index = first + lax.broadcasted_iota(jnp.int32, (rows, 1), 0)
    return index < length


def glu_of(normed, weight_ref, cut, keep):
    value = jnp.dot(normed, weight_ref[0, :, cut], preferred_element_type=F32)
    gate = jnp.dot(normed, weight_ref[1, :, cut], preferred_element_type=F32)
    glu = (value * jax.nn.sigmoid(gate)).astype(BF16)
    return jnp.where(keep, glu.astype(F32), 0.0)


def three_parts(vector):
    parts = []
    for _ in range(3):
        part = vector.astype(BF16).astype(F32)
        parts.append(part)
        vector = vector - part
    return parts


def affine(vectors_ref):
    rows = [vectors_ref[at : at + 1, :] for at in range(vectors_ref.shape[0] - 2)]
    half = len(rows) // 2
    return jnp.concatenate(rows[:half], axis=1), jnp.concatenate(rows[half:], axis=1)


def clear_ends(edge_ref):
    tiles, total, _ = edge_ref.shape
    zeros = jnp.zeros((EDGE, LANES), F32)
    for tile in range(tiles):
        edge_ref[tile, 0:EDGE, :] = zeros
        edge_ref[tile, total - EDGE : total, :] = zeros


def taps_at(taps_ref, offset, tile):
    cut = slice(tile * LANES, (tile + 1) * LANES)
    taps = {}
    for step in range(5):
        tap = 8 * step + offset - 1
        if 0 <= tap < KERNEL:
            taps[step] = jnp.broadcast_to(taps_ref[tap : tap + 1, cut], (8, LANES))
    return taps


def block_conv(block, tile, edge_ref, taps_ref):
    rows = block.shape[0]
    edge_ref[tile, EDGE : EDGE + rows, :] = block
    count = (rows + 2 * HALO) // 8
    total = [None] * count
    for offset in range(8):
        taps = taps_at(taps_ref, offset, tile)
        for at in range(count + 4):
            start = 8 * at + offset - 2 * HALO
            if start <= -8 or start >= rows:
                continue
            values = edge_ref[tile, EDGE + start : EDGE + start + 8, :]
            for step, tap in taps.items():
                if 0 <= at - step < count:
                    term = values * tap
                    seen = total[at - step]
                    total[at - step] = term if seen is None else seen + term
    return total


def half_lanes(tile, tiles):
    half, place = divmod(tile, tiles // 2)
    return half, slice(place * LANES, (place + 1) * LANES)


def first_block_kernel(
    lengths_ref, frames_ref, vectors_ref, taps_ref, weight_ref,
    soon_ref, later_ref, sums_ref, held_ref, pivot_ref, store_ref,
    rows_ref, raw_ref, wide_taps_ref, edge_ref, base_ref, rows_sem, weight_sems, base_sem,
):
    rows = rows_ref.shape[0]
    chans = held_ref.shape[2]
    own = lax.axis_index("tensor")
    rows_copy = pltpu.make_async_copy(frames_ref.at[0], rows_ref, rows_sem)
    rows_copy.start()
    pieces = cuts(chans, WIDE)
    copies = []
    for at, cut in enumerate(pieces):
        for side in range(2):
            place = (side, pl.ds(cut.start, WIDE))
            copy = pltpu.make_async_copy(
                weight_ref.at[place], raw_ref.at[place], weight_sems.at[at, side]
            )
            copy.start()
            copies.append(copy)
    clear_ends(edge_ref)
    keep = valid_rows(own * rows, rows, lengths_ref[0])
    wide_taps_ref[...] = taps_ref[...].astype(F32)
    gain, bias = affine(vectors_ref)
    rows_copy.wait()
    normed = layer_norm(rows_ref[...], gain, bias)
    tiles = chans // LANES
    for shift, half in enumerate((own, 1 - own)):
        for tile in range(tiles):
            lanes = pl.ds(pl.multiple_of((half * tiles + tile) * LANES, LANES), LANES)
            base_ref[shift, tile] = rows_ref[:, lanes].astype(F32)
    base_copy = pltpu.make_async_copy(base_ref, store_ref.at[pl.ds(HALF, 2)], base_sem)
    base_copy.start()
    for at, cut in enumerate(pieces):
        for side in range(2):
            copies[2 * at + side].wait()
            held_ref[side, :, cut] = raw_ref[side, cut, :].T
        glu = glu_of(normed, held_ref, cut, keep)
        for tile in range(cut.start // LANES, cut.stop // LANES):
            seen = slice(tile * LANES - cut.start, (tile + 1) * LANES - cut.start)
            total = block_conv(glu[:, seen], tile, edge_ref, wide_taps_ref)
            for step, each in enumerate(total):
                sums_ref[tile, 8 * step : 8 * step + 8, :] = each
            lanes = slice(tile * LANES, (tile + 1) * LANES)
            conv = sums_ref[tile, HALO : HALO + rows, :]
            pivot = jnp.sum(conv, axis=0, keepdims=True) * (1.0 / rows)
            pivot = pivot.astype(BF16).astype(F32)
            pivot_ref[:, lanes] = pivot
            half, there = half_lanes(tile, tiles)
            (soon_ref, later_ref)[half][:, there] = (conv - pivot).astype(BF16)
    base_copy.wait()


def last_block_kernel(
    lengths_ref, rows_ref, vectors_ref, taps_ref, weight_ref, first_sums_ref, pivot_ref, later_ref, _,
    late_ref, tail_ref, spread_ref, store_ref,
    wide_taps_ref, edge_ref, conv_ref, mask_ref, peer_rows_ref, stats_ref, late_sems, conv_sems, stats_sem,
):
    rows, chans = peer_rows_ref.shape
    tiles = chans // LANES
    own = lax.axis_index("tensor")
    peer = 1 - own
    length = lengths_ref[0]
    count = length.astype(F32)
    keep = valid_rows(peer * rows, rows, length)
    for at, place in enumerate((own, peer)):
        valid = valid_rows(place * rows, rows, length).astype(F32)
        mask_ref[at] = jnp.broadcast_to(valid, (rows, LANES))
    first_one = (own == 0).astype(F32)
    last_one = 1.0 - first_one
    clear_ends(edge_ref)
    wide_taps_ref[...] = taps_ref[...].astype(F32)
    last = vectors_ref.shape[0] - 2
    extra = three_parts(vectors_ref[last : last + 1, :])
    extra += three_parts(vectors_ref[last + 1 : last + 2, :])
    extra.append(pivot_ref[...])
    extra.append(jnp.zeros((EXTRA - len(extra), chans), F32))
    extra = jnp.concatenate(extra)
    wide = chans // 2
    tail_ref[0:rows, :] = later_ref[...]
    tail_ref[rows + 2 * HALO :, :] = jnp.concatenate([extra[:, :wide], extra[:, wide:]]).astype(BF16)
    normed = layer_norm(rows_ref[...], *affine(vectors_ref))
    copies = []
    for cut in cuts(chans, WIDE):
        glu = glu_of(normed, weight_ref, cut, keep)
        for tile in range(cut.start // LANES, cut.stop // LANES):
            seen = slice(tile * LANES - cut.start, (tile + 1) * LANES - cut.start)
            lanes = slice(tile * LANES, (tile + 1) * LANES)
            total = block_conv(glu[:, seen], tile, edge_ref, wide_taps_ref)
            first = [first_sums_ref[tile, 8 * at : 8 * at + 8, :] for at in range(len(total))]
            kept, sent = first[2:-2], total[2:-2]
            for at in range(2):
                kept[at] += total[at - 2] * last_one
                kept[at - 2] += total[at] * first_one
                sent[at] += first[at - 2] * first_one
                sent[at - 2] += first[at] * last_one
            near = jnp.concatenate(kept[:2]) * last_one + jnp.concatenate(kept[-2:]) * first_one
            kept, sent = jnp.concatenate(kept), jnp.concatenate(sent)
            for block, conv in ((KEPT, kept), (SENT, sent)):
                conv_ref[block, tile] = conv
                copies.append(
                    pltpu.make_async_copy(
                        conv_ref.at[block, tile], store_ref.at[block, tile], conv_sems.at[tile, block]
                    )
                )
                copies[-1].start()
            pivot = pivot_ref[:, lanes]
            near = (near - pivot).astype(BF16)
            half, there = half_lanes(tile, tiles)
            tail_ref[rows + half * HALO : rows + (half + 1) * HALO, there] = near
            peer_rows_ref[:, lanes] = (sent - pivot).astype(BF16)
            copies.append(
                pltpu.make_async_copy(
                    peer_rows_ref.at[:, pl.ds(lanes.start, LANES)],
                    late_ref.at[:, pl.ds(lanes.start, LANES)],
                    late_sems.at[tile],
                )
            )
            copies[-1].start()
            mean = jnp.sum(kept * mask_ref[0] + sent * mask_ref[1], axis=0, keepdims=True)
            mean = mean / count
            high = mean.astype(BF16)
            low = (mean - high.astype(F32)).astype(BF16)
            mean = high.astype(F32) + low.astype(F32)
            kept, sent = (kept - mean) * mask_ref[0], (sent - mean) * mask_ref[1]
            squares = jnp.sum(kept * kept + sent * sent, axis=0, keepdims=True)
            put_sums(stats_ref, tile, chans, high, low, squares.astype(BF16))
    high = jnp.full((1, LANES), count, F32).astype(BF16)
    low = (jnp.full((1, LANES), count, F32) - high.astype(F32)).astype(BF16)
    stats_ref[0, :, chans + chans // 2 :] = jnp.concatenate([high, low])
    stats = stats_ref[0]
    for at in range(1, stats_ref.shape[0]):
        stats_ref[at] = stats
    copies.append(pltpu.make_async_copy(stats_ref, spread_ref, stats_sem))
    copies[-1].start()
    for copy in copies:
        copy.wait()


def put_sums(spread_ref, tile, chans, high, low, squares):
    lanes = slice(tile * LANES, (tile + 1) * LANES)
    spread_ref[0, :, lanes] = jnp.concatenate([high, low])
    half = chans // 2
    row, at = divmod(tile * LANES, half)
    spread_ref[0, row : row + 1, chans + at : chans + at + LANES] = squares


def turn_kernel(weight_ref, vectors_ref, store_ref, held_ref, conv_ref, norms_ref, sem):
    parts, chans, _ = held_ref.shape
    copy = pltpu.make_async_copy(store_ref.at[SENT], conv_ref, sem)
    copy.start()
    norms_ref[...] = vectors_ref[vectors_ref.shape[0] - 2 :, :]
    for place in range(parts):
        for cut in cuts(chans, WIDE):
            at = place * chans
            held_ref[place, cut, :] = weight_ref[:, at + cut.start : at + cut.stop].T
    copy.wait()


def peer_vectors(tail_ref):
    first = tail_ref.shape[0] - 2 * EXTRA
    parts = tail_ref[first:, :].astype(F32)
    parts = jnp.concatenate([parts[:EXTRA], parts[EXTRA:]], axis=1)
    gain, bias = (parts[at : at + 1] + (parts[at + 1 : at + 2] + parts[at + 2 : at + 3]) for at in (0, 3))
    return gain, bias, parts[6:7]


def scales(stats_ref, norms_ref, tail_ref):
    chans = norms_ref.shape[1]
    gain, bias, pivot = peer_vectors(tail_ref)
    norms = [(norms_ref[0:1, :], norms_ref[1:2, :], 0.0), (gain, bias, pivot)]
    half = chans // 2
    own = lax.axis_index("tensor")
    found = []
    for shift, place in enumerate((1 - own, own)):
        seen = stats_ref[:, pl.ds(place, 1), :, :].astype(F32)
        both = seen[:, :, 0:1, :] + seen[:, :, 1:2, :]
        means, counts = both[..., :chans], both[..., chans + half : chans + half + 1]
        squares = jnp.concatenate([seen[:, :, at : at + 1, chans : chans + half] for at in range(2)], axis=-1)
        count = jnp.sum(counts, axis=0)[0]
        mean = jnp.sum(means * counts, axis=0)[0] / count
        off = means - mean
        var = jnp.sum(squares + counts * off * off, axis=0)[0] / count
        gain, bias, pivot = norms[shift]
        found.append((mean - pivot, lax.rsqrt(var + 1e-05) * gain, bias))
    return found


def branch_rows(found, conv_ref, peer_ref, weight_ref):
    own = lax.axis_index("tensor")
    total = None
    for shift in (1, 0):
        mean, scale, bias = found[shift]
        acts = []
        for tile in range(conv_ref.shape[0]):
            lanes = slice(tile * LANES, (tile + 1) * LANES)
            conv = peer_ref[:, lanes].astype(F32) if shift else conv_ref[tile]
            z = (conv - mean[:, lanes]) * scale[:, lanes] + bias[:, lanes]
            acts.append(swish(z).astype(BF16))
        place = 1 - own if shift else own
        term = jnp.dot(jnp.concatenate(acts, axis=1), weight_ref[place], preferred_element_type=F32)
        total = term if total is None else total + term
    return total


def sent_kernel(stats_ref, conv_ref, soon_ref, tail_ref, norms_ref, weight_ref, out_ref, peer_ref):
    rows, wide = soon_ref.shape
    target = pl.multiple_of(jnp.where(lax.axis_index("tensor") == 0, 0, rows - HALO), HALO)
    peer_ref[:, :wide] = soon_ref[...]
    peer_ref[:, wide:] = tail_ref[0:rows, :]
    peer_ref[pl.ds(target, HALO), :wide] = tail_ref[rows : rows + HALO, :]
    peer_ref[pl.ds(target, HALO), wide:] = tail_ref[rows + HALO : rows + 2 * HALO, :]
    found = scales(stats_ref, norms_ref, tail_ref)
    branch = branch_rows(found, conv_ref, peer_ref, weight_ref)
    out_ref[...] = branch.astype(BF16)


def columns(ref, place, cols):
    return ref.at[:, pl.ds(pl.multiple_of(place * cols, LANES), cols)]


def kept_kernel(
    stats_ref, late_ref, tail_ref, norms_ref, weight_ref, store_ref,
    mine_ref, base_ref, conv_ref, half_ref, sems,
):
    copies = [
        (store_ref.at[KEPT], conv_ref),
        (store_ref.at[HALF], half_ref),
        (store_ref.at[OTHER], base_ref),
    ]
    copies = [pltpu.make_async_copy(*pair, sems.at[at]) for at, pair in enumerate(copies)]
    for copy in copies:
        copy.start()
    found = scales(stats_ref, norms_ref, tail_ref)
    copies[0].wait()
    branch = branch_rows(found, conv_ref, late_ref, weight_ref)
    copies[1].wait()
    for tile in range(conv_ref.shape[0]):
        lanes = slice(tile * LANES, (tile + 1) * LANES)
        mine_ref[:, lanes] = (half_ref[tile] + branch[:, lanes]).astype(BF16)
    copies[2].wait()


def finish_kernel(mine_ref, base_ref, got_ref, out_ref, done_ref, sems):
    own = lax.axis_index("tensor")
    rows, cols = mine_ref.shape
    copies = [pltpu.make_async_copy(mine_ref, columns(out_ref, own, cols), sems.at[0])]
    copies[0].start()
    for tile in range(cols // LANES):
        lanes = slice(tile * LANES, (tile + 1) * LANES)
        done_ref[:, lanes] = (base_ref[tile] + got_ref[:, lanes].astype(F32)).astype(BF16)
    copies.append(pltpu.make_async_copy(done_ref, columns(out_ref, 1 - own, cols), sems.at[1]))
    copies[1].start()
    for copy in copies:
        copy.wait()


def shape(dims, kind):
    return jax.ShapeDtypeStruct(dims, kind)


def call(kernel, outs, in_specs, operands, out_specs=None, scratch=(), name=None, aliases=None, room=32):
    return pl.pallas_call(
        kernel,
        out_shape=tuple(outs),
        in_specs=list(in_specs),
        out_specs=tuple(out_specs or [VMEM] * len(outs)),
        scratch_shapes=list(scratch),
        input_output_aliases=aliases or {},
        compiler_params=pltpu.CompilerParams(vmem_limit_bytes=room * 1024 * 1024),
        name=name,
    )(*operands)


def two_parts(
    devices, frames_in, lengths, ln_gain, ln_bias, glu_weight, conv_kernel, bn_gain, bn_bias, out_weight
):
    _, span, width = frames_in.shape
    chans = glu_weight.shape[1]
    cols = out_weight.shape[0]
    tiles = chans // LANES
    pieces = chans // WIDE

    def swap(value):
        return lax.ppermute(value, "tensor", [(0, 1), (1, 0)])

    frames = swap(frames_in[0])
    vectors = jnp.concatenate([ln_gain, ln_bias, bn_gain, bn_bias]).reshape(-1, chans)
    edge = pltpu.VMEM((tiles, span + 2 * EDGE, LANES), F32)
    wide_taps = pltpu.VMEM((KERNEL, chans), F32)
    dma = pltpu.SemaphoreType.DMA
    reach = shape((tiles, span + 2 * HALO, LANES), F32)
    block = shape((tiles, span, LANES), F32)
    store = shape((BLOCKS,) + block.shape, F32)
    soon, later, first_sums, held, pivot, store_first = call(
        first_block_kernel,
        (
            shape((span, chans // 2), BF16),
            shape((span, chans // 2), BF16),
            reach,
            shape((2, width, chans), BF16),
            shape((1, chans), F32),
            store,
        ),
        [SMEM, HBM, VMEM, VMEM, HBM],
        (lengths, frames_in, vectors, conv_kernel, glu_weight),
        out_specs=(VMEM,) * 5 + (HBM,),
        scratch=(
            pltpu.VMEM((span, width), BF16),
            pltpu.VMEM((2, chans, width), BF16),
            wide_taps,
            edge,
            pltpu.VMEM((2,) + block.shape, F32),
            dma,
            dma((pieces, 2)),
            dma,
        ),
        name="first_block",
        room=48,
    )
    soon = swap(soon)
    late, tail, spread, store_second = call(
        last_block_kernel,
        (
            shape((span, chans), BF16),
            shape((span + 2 * HALO + 2 * EXTRA, chans // 2), BF16),
            shape((devices, 2, chans + chans // 2 + LANES), BF16),
            store,
        ),
        [SMEM] + [VMEM] * 7 + [HBM],
        (lengths, frames, vectors, conv_kernel, held, first_sums, pivot, later, store_first),
        out_specs=(HBM, VMEM, HBM, HBM),
        scratch=(
            wide_taps,
            edge,
            pltpu.VMEM((2, tiles, span, LANES), F32),
            pltpu.VMEM((2, span, LANES), F32),
            pltpu.VMEM((span, chans), BF16),
            pltpu.VMEM((devices, 2, chans + chans // 2 + LANES), BF16),
            dma((tiles,)),
            dma((tiles, 2)),
            dma,
        ),
        aliases={8: 3},
        name="last_block",
        room=40,
    )
    spread, soon, out_weight = lax.optimization_barrier((spread, soon, out_weight))
    stats = lax.all_to_all(
        spread, ("dp", "tensor"), split_axis=0, concat_axis=0, tiled=True,
        axis_index_groups=[list(reversed(range(devices)))],
    )
    stats = stats.reshape((devices // 2, 2) + spread.shape[1:])
    tail, late = swap(tail), swap(late)
    weight, sent_conv, norms = call(
        turn_kernel,
        (shape((2, chans, cols), BF16), block, shape((2, chans), F32)),
        [VMEM, VMEM, HBM],
        (out_weight, vectors, store_second),
        scratch=(dma,),
        name="turn",
    )
    (sent,) = call(
        sent_kernel,
        (shape((span, cols), BF16),),
        [VMEM] * 6,
        (stats, sent_conv, soon, tail, norms, weight),
        scratch=(pltpu.VMEM((span, chans), BF16),),
        name="branch_sent",
    )
    got = swap(sent)
    mine, base = call(
        kept_kernel,
        (shape((span, cols), BF16), block),
        [VMEM] * 5 + [HBM],
        (stats, late, tail, norms, weight, store_second),
        scratch=(pltpu.VMEM(block.shape, F32), pltpu.VMEM(block.shape, F32), dma((3,))),
        name="branch_kept",
    )
    (out,) = call(
        finish_kernel,
        (shape((span, width), BF16),),
        [VMEM] * 3,
        (mine, base, got),
        out_specs=(HBM,),
        scratch=(pltpu.VMEM((span, cols), BF16), dma((2,))),
        name="residual",
    )
    return out[None]


def contract_last(left, right):
    return lax.dot_general(
        left, right, (((1,), (1,)), ((), ())), preferred_element_type=F32
    )


def many_parts(
    devices, frames_in, lengths, ln_gain, ln_bias, glu_weight, conv_kernel, bn_gain, bn_bias, out_weight
):
    rows = frames_in[0]
    chans = glu_weight.shape[1]
    normed = layer_norm(rows, ln_gain, ln_bias)
    proj = contract_last(
        lax.all_gather(normed, "tensor", axis=0, tiled=True),
        glu_weight.reshape(2 * chans, rows.shape[1]),
    )
    valid = valid_rows(0, proj.shape[0], lengths[0])
    glu = (proj[:, :chans] * jax.nn.sigmoid(proj[:, chans:])).astype(BF16)
    glu = jnp.where(valid, glu, jnp.zeros_like(glu)).astype(F32)
    padded = jnp.pad(glu, ((15, KERNEL - 16), (0, 0)))
    taps = conv_kernel.astype(F32)
    conv = jnp.zeros_like(glu)
    for tap in range(KERNEL):
        conv = conv + padded[tap : tap + glu.shape[0]] * taps[tap]
    own = lengths[0].astype(F32)
    local = jnp.sum(jnp.where(valid, conv, 0.0), axis=0) / own
    squares = jnp.sum(jnp.where(valid, conv - local, 0.0) ** 2, axis=0)
    count = lax.psum(own, "dp")
    mean = lax.psum(local * own, "dp") / count
    var = lax.psum(squares + own * (local - mean) ** 2, "dp") / count
    z = (conv - mean) * (lax.rsqrt(var + 1e-05) * bn_gain) + bn_bias
    act = lax.all_gather(swish(z).astype(BF16), "tensor", axis=1, tiled=True)
    branch = contract_last(act, out_weight)
    branch = lax.all_to_all(branch, "tensor", split_axis=0, concat_axis=1, tiled=True)
    return (rows.astype(F32) + branch).astype(BF16)[None]


def solution(mesh):
    sizes = dict(mesh.shape)
    body = two_parts if sizes["tensor"] == 2 else many_parts
    body = functools.partial(body, sizes["tensor"] * sizes["dp"])
    return jax.shard_map(
        body,
        mesh=mesh,
        in_specs=(
            P("dp", "tensor", None),
            P("dp"),
            P(),
            P(),
            P(None, "tensor", None),
            P(None, "tensor"),
            P("tensor"),
            P("tensor"),
            P("tensor", None),
        ),
        out_specs=P("dp", "tensor", None),
        check_vma=False,
    )
```

```python
import functools

import jax
import jax.numpy as jnp
from jax import lax
from jax.experimental import pallas as pl
from jax.experimental.pallas import tpu as pltpu
from jax.sharding import PartitionSpec as P

KERNEL = 32
LANES = 128
WIDE = 256
HALO = 16
EDGE = 8
KEPT, SENT, HALF, OTHER, BLOCKS = 0, 1, 2, 3, 72
EXTRA = 8
F32 = jnp.float32
BF16 = jnp.bfloat16

VMEM = pl.BlockSpec(memory_space=pltpu.VMEM)
SMEM = pl.BlockSpec(memory_space=pltpu.SMEM)
HBM = pl.BlockSpec(memory_space=pltpu.HBM)


def layer_norm(rows, gain, bias):
    values = rows.astype(F32)
    center = jnp.mean(values, axis=-1, keepdims=True)
    values = values - center
    spread = jnp.mean(values * values, axis=-1, keepdims=True)
    return (values * lax.rsqrt(spread + 1e-05) * gain + bias).astype(BF16)


def swish(z):
    return z * jax.nn.sigmoid(z)


def cuts(width, most):
    return [slice(at, at + most) for at in range(0, width, most)]


def valid_rows(first, rows, length):
    index = first + lax.broadcasted_iota(jnp.int32, (rows, 1), 0)
    return index < length


def glu_of(normed, weight_ref, cut, keep):
    value = jnp.dot(normed, weight_ref[0, :, cut], preferred_element_type=F32)
    gate = jnp.dot(normed, weight_ref[1, :, cut], preferred_element_type=F32)
    glu = (value * jax.nn.sigmoid(gate)).astype(BF16)
    return jnp.where(keep, glu.astype(F32), 0.0)


def three_parts(vector):
    parts = []
    for _ in range(3):
        part = vector.astype(BF16).astype(F32)
        parts.append(part)
        vector = vector - part
    return parts


def affine(vectors_ref):
    rows = [vectors_ref[at : at + 1, :] for at in range(vectors_ref.shape[0] - 2)]
    half = len(rows) // 2
    return jnp.concatenate(rows[:half], axis=1), jnp.concatenate(rows[half:], axis=1)


def clear_ends(edge_ref):
    tiles, total, _ = edge_ref.shape
    zeros = jnp.zeros((EDGE, LANES), F32)
    for tile in range(tiles):
        edge_ref[tile, 0:EDGE, :] = zeros
        edge_ref[tile, total - EDGE : total, :] = zeros


def taps_at(taps_ref, offset, tile):
    cut = slice(tile * LANES, (tile + 1) * LANES)
    taps = {}
    for step in range(5):
        tap = 8 * step + offset - 1
        if 0 <= tap < KERNEL:
            taps[step] = jnp.broadcast_to(taps_ref[tap : tap + 1, cut], (8, LANES))
    return taps


def block_conv(block, tile, edge_ref, taps_ref):
    rows = block.shape[0]
    edge_ref[tile, EDGE : EDGE + rows, :] = block
    count = (rows + 2 * HALO) // 8
    total = [None] * count
    for offset in range(8):
        taps = taps_at(taps_ref, offset, tile)
        for at in range(count + 4):
            start = 8 * at + offset - 2 * HALO
            if start <= -8 or start >= rows:
                continue
            values = edge_ref[tile, EDGE + start : EDGE + start + 8, :]
            for step, tap in taps.items():
                if 0 <= at - step < count:
                    term = values * tap
                    seen = total[at - step]
                    total[at - step] = term if seen is None else seen + term
    return total


def half_lanes(tile, tiles):
    half, place = divmod(tile, tiles // 2)
    return half, slice(place * LANES, (place + 1) * LANES)


def first_block_kernel(
    lengths_ref, frames_ref, vectors_ref, taps_ref, weight_ref,
    soon_ref, later_ref, sums_ref, held_ref, pivot_ref, store_ref,
    rows_ref, raw_ref, wide_taps_ref, edge_ref, base_ref, rows_sem, weight_sems, base_sem,
):
    rows = rows_ref.shape[0]
    chans = held_ref.shape[2]
    own = lax.axis_index("tensor")
    rows_copy = pltpu.make_async_copy(frames_ref.at[0], rows_ref, rows_sem)
    rows_copy.start()
    pieces = cuts(chans, WIDE)
    copies = []
    for at, cut in enumerate(pieces):
        for side in range(2):
            place = (side, pl.ds(cut.start, WIDE))
            copy = pltpu.make_async_copy(
                weight_ref.at[place], raw_ref.at[place], weight_sems.at[at, side]
            )
            copy.start()
            copies.append(copy)
    clear_ends(edge_ref)
    keep = valid_rows(own * rows, rows, lengths_ref[0])
    wide_taps_ref[...] = taps_ref[...].astype(F32)
    valid = keep.astype(F32)
    valid_count = jnp.maximum(lengths_ref[0] - own * rows, 1)
    valid_count = jnp.minimum(valid_count, rows).astype(F32)
    gain, bias = affine(vectors_ref)
    rows_copy.wait()
    normed = layer_norm(rows_ref[...], gain, bias)
    tiles = chans // LANES
    for shift, half in enumerate((own, 1 - own)):
        for tile in range(tiles):
            lanes = pl.ds(pl.multiple_of((half * tiles + tile) * LANES, LANES), LANES)
            base_ref[shift, tile] = rows_ref[:, lanes].astype(F32)
    base_copy = pltpu.make_async_copy(base_ref, store_ref.at[pl.ds(HALF, 2)], base_sem)
    base_copy.start()
    for at, cut in enumerate(pieces):
        for side in range(2):
            copies[2 * at + side].wait()
            held_ref[side, :, cut] = raw_ref[side, cut, :].T
        glu = glu_of(normed, held_ref, cut, keep)
        for tile in range(cut.start // LANES, cut.stop // LANES):
            seen = slice(tile * LANES - cut.start, (tile + 1) * LANES - cut.start)
            total = block_conv(glu[:, seen], tile, edge_ref, wide_taps_ref)
            for step, each in enumerate(total):
                sums_ref[tile, 8 * step : 8 * step + 8, :] = each
            lanes = slice(tile * LANES, (tile + 1) * LANES)
            conv = sums_ref[tile, HALO : HALO + rows, :]
            pivot = jnp.sum(conv * valid, axis=0, keepdims=True) / valid_count
            pivot = pivot.astype(BF16).astype(F32)
            pivot_ref[:, lanes] = pivot
            half, there = half_lanes(tile, tiles)
            (soon_ref, later_ref)[half][:, there] = (conv - pivot).astype(BF16)
    base_copy.wait()


def last_block_kernel(
    lengths_ref, rows_ref, vectors_ref, taps_ref, weight_ref, first_sums_ref, pivot_ref, later_ref, _,
    late_ref, tail_ref, spread_ref, store_ref,
    wide_taps_ref, edge_ref, conv_ref, mask_ref, peer_rows_ref, stats_ref, late_sems, conv_sems, stats_sem,
):
    rows, chans = peer_rows_ref.shape
    tiles = chans // LANES
    own = lax.axis_index("tensor")
    peer = 1 - own
    length = lengths_ref[0]
    count = length.astype(F32)
    keep = valid_rows(peer * rows, rows, length)
    for at, place in enumerate((own, peer)):
        valid = valid_rows(place * rows, rows, length).astype(F32)
        mask_ref[at] = jnp.broadcast_to(valid, (rows, LANES))
    first_one = (own == 0).astype(F32)
    last_one = 1.0 - first_one
    clear_ends(edge_ref)
    wide_taps_ref[...] = taps_ref[...].astype(F32)
    last = vectors_ref.shape[0] - 2
    extra = three_parts(vectors_ref[last : last + 1, :])
    extra += three_parts(vectors_ref[last + 1 : last + 2, :])
    extra.append(pivot_ref[...])
    wide = chans // 2
    tail_ref[0:rows, :] = later_ref[...]
    means = []
    normed = layer_norm(rows_ref[...], *affine(vectors_ref))
    copies = []
    for cut in cuts(chans, WIDE):
        glu = glu_of(normed, weight_ref, cut, keep)
        for tile in range(cut.start // LANES, cut.stop // LANES):
            seen = slice(tile * LANES - cut.start, (tile + 1) * LANES - cut.start)
            lanes = slice(tile * LANES, (tile + 1) * LANES)
            total = block_conv(glu[:, seen], tile, edge_ref, wide_taps_ref)
            first = [first_sums_ref[tile, 8 * at : 8 * at + 8, :] for at in range(len(total))]
            kept, sent = first[2:-2], total[2:-2]
            for at in range(2):
                kept[at] += total[at - 2] * last_one
                kept[at - 2] += total[at] * first_one
                sent[at] += first[at - 2] * first_one
                sent[at - 2] += first[at] * last_one
            near = jnp.concatenate(kept[:2]) * last_one + jnp.concatenate(kept[-2:]) * first_one
            kept, sent = jnp.concatenate(kept), jnp.concatenate(sent)
            for block, conv in ((KEPT, kept), (SENT, sent)):
                conv_ref[block, tile] = conv
                copies.append(
                    pltpu.make_async_copy(
                        conv_ref.at[block, tile], store_ref.at[block, tile], conv_sems.at[tile, block]
                    )
                )
                copies[-1].start()
            pivot = pivot_ref[:, lanes]
            near = (near - pivot).astype(BF16)
            half, there = half_lanes(tile, tiles)
            tail_ref[rows + half * HALO : rows + (half + 1) * HALO, there] = near
            mean = jnp.sum(kept * mask_ref[0] + sent * mask_ref[1], axis=0, keepdims=True)
            mean = mean / count
            high = mean.astype(BF16)
            low = (mean - high.astype(F32)).astype(BF16)
            means.append(high.astype(F32))
            peer_rows_ref[:, lanes] = (sent - means[-1]).astype(BF16)
            copies.append(
                pltpu.make_async_copy(
                    peer_rows_ref.at[:, pl.ds(lanes.start, LANES)],
                    late_ref.at[:, pl.ds(lanes.start, LANES)],
                    late_sems.at[tile],
                )
            )
            copies[-1].start()
            mean = means[-1] + low.astype(F32)
            kept, sent = (kept - mean) * mask_ref[0], (sent - mean) * mask_ref[1]
            squares = jnp.sum(kept * kept + sent * sent, axis=0, keepdims=True)
            put_sums(stats_ref, tile, chans, high, low, squares.astype(BF16))
    high = jnp.full((1, LANES), count, F32).astype(BF16)
    low = (jnp.full((1, LANES), count, F32) - high.astype(F32)).astype(BF16)
    stats_ref[0, :, chans + chans // 2 :] = jnp.concatenate([high, low])
    stats = stats_ref[0]
    for at in range(1, stats_ref.shape[0]):
        stats_ref[at] = stats
    copies.append(pltpu.make_async_copy(stats_ref, spread_ref, stats_sem))
    copies[-1].start()
    extra = jnp.concatenate(extra + [jnp.concatenate(means, axis=1)])
    tail_ref[rows + 2 * HALO :, :] = jnp.concatenate([extra[:, :wide], extra[:, wide:]]).astype(BF16)
    for copy in copies:
        copy.wait()


def put_sums(spread_ref, tile, chans, high, low, squares):
    lanes = slice(tile * LANES, (tile + 1) * LANES)
    spread_ref[0, :, lanes] = jnp.concatenate([high, low])
    half = chans // 2
    row, at = divmod(tile * LANES, half)
    spread_ref[0, row : row + 1, chans + at : chans + at + LANES] = squares


def turn_kernel(weight_ref, vectors_ref, store_ref, held_ref, conv_ref, norms_ref, sem):
    parts, chans, _ = held_ref.shape
    copy = pltpu.make_async_copy(store_ref.at[SENT], conv_ref, sem)
    copy.start()
    norms_ref[...] = vectors_ref[vectors_ref.shape[0] - 2 :, :]
    for place in range(parts):
        for cut in cuts(chans, WIDE):
            at = place * chans
            held_ref[place, cut, :] = weight_ref[:, at + cut.start : at + cut.stop].T
    copy.wait()


def peer_vectors(tail_ref):
    first = tail_ref.shape[0] - 2 * EXTRA
    parts = tail_ref[first:, :].astype(F32)
    parts = jnp.concatenate([parts[:EXTRA], parts[EXTRA:]], axis=1)
    gain, bias = (parts[at : at + 1] + (parts[at + 1 : at + 2] + parts[at + 2 : at + 3]) for at in (0, 3))
    return gain, bias, parts[6:7], parts[7:8]


def scales(stats_ref, norms_ref, tail_ref, kept):
    chans = norms_ref.shape[1]
    gain, bias, *pivots = peer_vectors(tail_ref)
    norms = [(norms_ref[0:1, :], norms_ref[1:2, :], 0.0), (gain, bias, pivots[kept])]
    half = chans // 2
    own = lax.axis_index("tensor")
    found = []
    for shift, place in enumerate((1 - own, own)):
        seen = stats_ref[:, pl.ds(place, 1), :, :].astype(F32)
        both = seen[:, :, 0:1, :] + seen[:, :, 1:2, :]
        means, counts = both[..., :chans], both[..., chans + half : chans + half + 1]
        squares = jnp.concatenate([seen[:, :, at : at + 1, chans : chans + half] for at in range(2)], axis=-1)
        count = jnp.sum(counts, axis=0)[0]
        mean = jnp.sum(means * counts, axis=0)[0] / count
        off = means - mean
        var = jnp.sum(squares + counts * off * off, axis=0)[0] / count
        gain, bias, pivot = norms[shift]
        found.append((mean - pivot, lax.rsqrt(var + 1e-05) * gain, bias))
    return found


def branch_rows(found, conv_ref, peer_ref, weight_ref):
    own = lax.axis_index("tensor")
    total = None
    for shift in (1, 0):
        mean, scale, bias = found[shift]
        acts = []
        for tile in range(conv_ref.shape[0]):
            lanes = slice(tile * LANES, (tile + 1) * LANES)
            conv = peer_ref[:, lanes].astype(F32) if shift else conv_ref[tile]
            z = (conv - mean[:, lanes]) * scale[:, lanes] + bias[:, lanes]
            acts.append(swish(z).astype(BF16))
        place = 1 - own if shift else own
        term = jnp.dot(jnp.concatenate(acts, axis=1), weight_ref[place], preferred_element_type=F32)
        total = term if total is None else total + term
    return total


def sent_kernel(stats_ref, conv_ref, soon_ref, tail_ref, norms_ref, weight_ref, out_ref, peer_ref):
    rows, wide = soon_ref.shape
    target = pl.multiple_of(jnp.where(lax.axis_index("tensor") == 0, 0, rows - HALO), HALO)
    peer_ref[:, :wide] = soon_ref[...]
    peer_ref[:, wide:] = tail_ref[0:rows, :]
    peer_ref[pl.ds(target, HALO), :wide] = tail_ref[rows : rows + HALO, :]
    peer_ref[pl.ds(target, HALO), wide:] = tail_ref[rows + HALO : rows + 2 * HALO, :]
    found = scales(stats_ref, norms_ref, tail_ref, 0)
    branch = branch_rows(found, conv_ref, peer_ref, weight_ref)
    out_ref[...] = branch.astype(BF16)


def columns(ref, place, cols):
    return ref.at[:, pl.ds(pl.multiple_of(place * cols, LANES), cols)]


def kept_kernel(
    stats_ref, late_ref, tail_ref, norms_ref, weight_ref, store_ref,
    mine_ref, base_ref, conv_ref, half_ref, sems,
):
    copies = [
        (store_ref.at[KEPT], conv_ref),
        (store_ref.at[HALF], half_ref),
        (store_ref.at[OTHER], base_ref),
    ]
    copies = [pltpu.make_async_copy(*pair, sems.at[at]) for at, pair in enumerate(copies)]
    for copy in copies:
        copy.start()
    found = scales(stats_ref, norms_ref, tail_ref, 1)
    copies[0].wait()
    branch = branch_rows(found, conv_ref, late_ref, weight_ref)
    copies[1].wait()
    for tile in range(conv_ref.shape[0]):
        lanes = slice(tile * LANES, (tile + 1) * LANES)
        mine_ref[:, lanes] = (half_ref[tile] + branch[:, lanes]).astype(BF16)
    copies[2].wait()


def finish_kernel(mine_ref, base_ref, got_ref, out_ref, done_ref, sems):
    own = lax.axis_index("tensor")
    rows, cols = mine_ref.shape
    copies = [pltpu.make_async_copy(mine_ref, columns(out_ref, own, cols), sems.at[0])]
    copies[0].start()
    for tile in range(cols // LANES):
        lanes = slice(tile * LANES, (tile + 1) * LANES)
        done_ref[:, lanes] = (base_ref[tile] + got_ref[:, lanes].astype(F32)).astype(BF16)
    copies.append(pltpu.make_async_copy(done_ref, columns(out_ref, 1 - own, cols), sems.at[1]))
    copies[1].start()
    for copy in copies:
        copy.wait()


def shape(dims, kind):
    return jax.ShapeDtypeStruct(dims, kind)


def call(kernel, outs, in_specs, operands, out_specs=None, scratch=(), name=None, aliases=None, room=32):
    return pl.pallas_call(
        kernel,
        out_shape=tuple(outs),
        in_specs=list(in_specs),
        out_specs=tuple(out_specs or [VMEM] * len(outs)),
        scratch_shapes=list(scratch),
        input_output_aliases=aliases or {},
        compiler_params=pltpu.CompilerParams(vmem_limit_bytes=room * 1024 * 1024),
        name=name,
    )(*operands)


def two_parts(
    devices, frames_in, lengths, ln_gain, ln_bias, glu_weight, conv_kernel, bn_gain, bn_bias, out_weight
):
    _, span, width = frames_in.shape
    chans = glu_weight.shape[1]
    cols = out_weight.shape[0]
    tiles = chans // LANES
    pieces = chans // WIDE

    def swap(value):
        return lax.ppermute(value, "tensor", [(0, 1), (1, 0)])

    frames = swap(frames_in[0])
    vectors = jnp.concatenate([ln_gain, ln_bias, bn_gain, bn_bias]).reshape(-1, chans)
    edge = pltpu.VMEM((tiles, span + 2 * EDGE, LANES), F32)
    wide_taps = pltpu.VMEM((KERNEL, chans), F32)
    dma = pltpu.SemaphoreType.DMA
    reach = shape((tiles, span + 2 * HALO, LANES), F32)
    block = shape((tiles, span, LANES), F32)
    store = shape((BLOCKS,) + block.shape, F32)
    soon, later, first_sums, held, pivot, store_first = call(
        first_block_kernel,
        (
            shape((span, chans // 2), BF16),
            shape((span, chans // 2), BF16),
            reach,
            shape((2, width, chans), BF16),
            shape((1, chans), F32),
            store,
        ),
        [SMEM, HBM, VMEM, VMEM, HBM],
        (lengths, frames_in, vectors, conv_kernel, glu_weight),
        out_specs=(VMEM,) * 5 + (HBM,),
        scratch=(
            pltpu.VMEM((span, width), BF16),
            pltpu.VMEM((2, chans, width), BF16),
            wide_taps,
            edge,
            pltpu.VMEM((2,) + block.shape, F32),
            dma,
            dma((pieces, 2)),
            dma,
        ),
        name="first_block",
        room=48,
    )
    soon = swap(soon)
    late, tail, spread, store_second = call(
        last_block_kernel,
        (
            shape((span, chans), BF16),
            shape((span + 2 * HALO + 2 * EXTRA, chans // 2), BF16),
            shape((devices, 2, chans + chans // 2 + LANES), BF16),
            store,
        ),
        [SMEM] + [VMEM] * 7 + [HBM],
        (lengths, frames, vectors, conv_kernel, held, first_sums, pivot, later, store_first),
        out_specs=(HBM, VMEM, HBM, HBM),
        scratch=(
            wide_taps,
            edge,
            pltpu.VMEM((2, tiles, span, LANES), F32),
            pltpu.VMEM((2, span, LANES), F32),
            pltpu.VMEM((span, chans), BF16),
            pltpu.VMEM((devices, 2, chans + chans // 2 + LANES), BF16),
            dma((tiles,)),
            dma((tiles, 2)),
            dma,
        ),
        aliases={8: 3},
        name="last_block",
        room=40,
    )
    spread, soon, out_weight = lax.optimization_barrier((spread, soon, out_weight))
    stats = lax.all_to_all(
        spread, ("dp", "tensor"), split_axis=0, concat_axis=0, tiled=True,
        axis_index_groups=[list(reversed(range(devices)))],
    )
    stats = stats.reshape((devices // 2, 2) + spread.shape[1:])
    tail, late = swap(tail), swap(late)
    weight, sent_conv, norms = call(
        turn_kernel,
        (shape((2, chans, cols), BF16), block, shape((2, chans), F32)),
        [VMEM, VMEM, HBM],
        (out_weight, vectors, store_second),
        scratch=(dma,),
        name="turn",
    )
    (sent,) = call(
        sent_kernel,
        (shape((span, cols), BF16),),
        [VMEM] * 6,
        (stats, sent_conv, soon, tail, norms, weight),
        scratch=(pltpu.VMEM((span, chans), BF16),),
        name="branch_sent",
    )
    got = swap(sent)
    mine, base = call(
        kept_kernel,
        (shape((span, cols), BF16), block),
        [VMEM] * 5 + [HBM],
        (stats, late, tail, norms, weight, store_second),
        scratch=(pltpu.VMEM(block.shape, F32), pltpu.VMEM(block.shape, F32), dma((3,))),
        name="branch_kept",
    )
    (out,) = call(
        finish_kernel,
        (shape((span, width), BF16),),
        [VMEM] * 3,
        (mine, base, got),
        out_specs=(HBM,),
        scratch=(pltpu.VMEM((span, cols), BF16), dma((2,))),
        name="residual",
    )
    return out[None]


def contract_last(left, right):
    return lax.dot_general(
        left, right, (((1,), (1,)), ((), ())), preferred_element_type=F32
    )


def many_parts(
    devices, frames_in, lengths, ln_gain, ln_bias, glu_weight, conv_kernel, bn_gain, bn_bias, out_weight
):
    rows = frames_in[0]
    chans = glu_weight.shape[1]
    normed = layer_norm(rows, ln_gain, ln_bias)
    proj = contract_last(
        lax.all_gather(normed, "tensor", axis=0, tiled=True),
        glu_weight.reshape(2 * chans, rows.shape[1]),
    )
    valid = valid_rows(0, proj.shape[0], lengths[0])
    glu = (proj[:, :chans] * jax.nn.sigmoid(proj[:, chans:])).astype(BF16)
    glu = jnp.where(valid, glu, jnp.zeros_like(glu)).astype(F32)
    padded = jnp.pad(glu, ((15, KERNEL - 16), (0, 0)))
    taps = conv_kernel.astype(F32)
    conv = jnp.zeros_like(glu)
    for tap in range(KERNEL):
        conv = conv + padded[tap : tap + glu.shape[0]] * taps[tap]
    own = lengths[0].astype(F32)
    local = jnp.sum(jnp.where(valid, conv, 0.0), axis=0) / own
    squares = jnp.sum(jnp.where(valid, conv - local, 0.0) ** 2, axis=0)
    count = lax.psum(own, "dp")
    mean = lax.psum(local * own, "dp") / count
    var = lax.psum(squares + own * (local - mean) ** 2, "dp") / count
    z = (conv - mean) * (lax.rsqrt(var + 1e-05) * bn_gain) + bn_bias
    act = lax.all_gather(swish(z).astype(BF16), "tensor", axis=1, tiled=True)
    branch = contract_last(act, out_weight)
    branch = lax.all_to_all(branch, "tensor", split_axis=0, concat_axis=1, tiled=True)
    return (rows.astype(F32) + branch).astype(BF16)[None]


def solution(mesh):
    sizes = dict(mesh.shape)
    body = two_parts if sizes["tensor"] == 2 else many_parts
    body = functools.partial(body, sizes["tensor"] * sizes["dp"])
    return jax.shard_map(
        body,
        mesh=mesh,
        in_specs=(
            P("dp", "tensor", None),
            P("dp"),
            P(),
            P(),
            P(None, "tensor", None),
            P(None, "tensor"),
            P("tensor"),
            P("tensor"),
            P("tensor", None),
        ),
        out_specs=P("dp", "tensor", None),
        check_vma=False,
    )
```

```python
import functools

import jax
import jax.numpy as jnp
from jax import lax
from jax.experimental import pallas as pl
from jax.experimental.pallas import tpu as pltpu
from jax.sharding import PartitionSpec as P

KERNEL = 32
LANES = 128
WIDE = 256
HALO = 16
EDGE = 8
KEPT, SENT, HALF, OTHER, BLOCKS = 0, 1, 2, 3, 72
FOLDS = 3
EXTRA = 8
F32 = jnp.float32
BF16 = jnp.bfloat16

VMEM = pl.BlockSpec(memory_space=pltpu.VMEM)
SMEM = pl.BlockSpec(memory_space=pltpu.SMEM)
HBM = pl.BlockSpec(memory_space=pltpu.HBM)


def layer_norm(rows, gain, bias):
    values = rows.astype(F32)
    center = jnp.mean(values, axis=-1, keepdims=True)
    values = values - center
    spread = jnp.mean(values * values, axis=-1, keepdims=True)
    return (values * lax.rsqrt(spread + 1e-05) * gain + bias).astype(BF16)


def swish(z):
    return z * jax.nn.sigmoid(z)


def cuts(width, most):
    return [slice(at, at + most) for at in range(0, width, most)]


def valid_rows(first, rows, length):
    index = first + lax.broadcasted_iota(jnp.int32, (rows, 1), 0)
    return index < length


def glu_of(normed, weight_ref, cut, keep):
    value = jnp.dot(normed, weight_ref[0, :, cut], preferred_element_type=F32)
    gate = jnp.dot(normed, weight_ref[1, :, cut], preferred_element_type=F32)
    glu = (value * jax.nn.sigmoid(gate)).astype(BF16)
    return jnp.where(keep, glu.astype(F32), 0.0)


def three_parts(vector):
    parts = []
    for _ in range(3):
        part = vector.astype(BF16).astype(F32)
        parts.append(part)
        vector = vector - part
    return parts


def affine(vectors_ref):
    rows = [vectors_ref[at : at + 1, :] for at in range(vectors_ref.shape[0] - 2)]
    half = len(rows) // 2
    return jnp.concatenate(rows[:half], axis=1), jnp.concatenate(rows[half:], axis=1)


def clear_ends(edge_ref):
    tiles, total, _ = edge_ref.shape
    zeros = jnp.zeros((EDGE, LANES), F32)
    for tile in range(tiles):
        edge_ref[tile, 0:EDGE, :] = zeros
        edge_ref[tile, total - EDGE : total, :] = zeros


def taps_at(taps_ref, offset, tile):
    cut = slice(tile * LANES, (tile + 1) * LANES)
    taps = {}
    for step in range(5):
        tap = 8 * step + offset - 1
        if 0 <= tap < KERNEL:
            taps[step] = jnp.broadcast_to(taps_ref[tap : tap + 1, cut], (8, LANES))
    return taps


def block_conv(block, tile, edge_ref, taps_ref):
    rows = block.shape[0]
    edge_ref[tile, EDGE : EDGE + rows, :] = block
    count = (rows + 2 * HALO) // 8
    total = [None] * count
    for offset in range(8):
        taps = taps_at(taps_ref, offset, tile)
        for at in range(count + 4):
            start = 8 * at + offset - 2 * HALO
            if start <= -8 or start >= rows:
                continue
            values = edge_ref[tile, EDGE + start : EDGE + start + 8, :]
            for step, tap in taps.items():
                if 0 <= at - step < count:
                    term = values * tap
                    seen = total[at - step]
                    total[at - step] = term if seen is None else seen + term
    return total


def part_lanes(tile, tiles):
    soon = tiles - tiles // FOLDS
    place = tile if tile < soon else tile - soon
    return int(tile >= soon), slice(place * LANES, (place + 1) * LANES)


def folded(rows):
    wide = rows.shape[1] // FOLDS
    return jnp.concatenate([rows[:, at * wide : (at + 1) * wide] for at in range(FOLDS)])


def first_block_kernel(
    lengths_ref, frames_ref, vectors_ref, taps_ref, weight_ref,
    soon_ref, later_ref, sums_ref, held_ref, pivot_ref, store_ref,
    rows_ref, raw_ref, wide_taps_ref, edge_ref, base_ref, rows_sem, weight_sems, base_sem,
):
    rows = rows_ref.shape[0]
    chans = held_ref.shape[2]
    own = lax.axis_index("tensor")
    rows_copy = pltpu.make_async_copy(frames_ref.at[0], rows_ref, rows_sem)
    rows_copy.start()
    pieces = cuts(chans, WIDE)
    copies = []
    for at, cut in enumerate(pieces):
        for side in range(2):
            place = (side, pl.ds(cut.start, WIDE))
            copy = pltpu.make_async_copy(
                weight_ref.at[place], raw_ref.at[place], weight_sems.at[at, side]
            )
            copy.start()
            copies.append(copy)
    clear_ends(edge_ref)
    keep = valid_rows(own * rows, rows, lengths_ref[0])
    wide_taps_ref[...] = taps_ref[...].astype(F32)
    valid = keep.astype(F32)
    valid_count = jnp.maximum(lengths_ref[0] - own * rows, 1)
    valid_count = jnp.minimum(valid_count, rows).astype(F32)
    gain, bias = affine(vectors_ref)
    rows_copy.wait()
    normed = layer_norm(rows_ref[...], gain, bias)
    tiles = chans // LANES
    for shift, half in enumerate((own, 1 - own)):
        for tile in range(tiles):
            lanes = pl.ds(pl.multiple_of((half * tiles + tile) * LANES, LANES), LANES)
            base_ref[shift, tile] = rows_ref[:, lanes].astype(F32)
    base_copy = pltpu.make_async_copy(base_ref, store_ref.at[pl.ds(HALF, 2)], base_sem)
    base_copy.start()
    for at, cut in enumerate(pieces):
        for side in range(2):
            copies[2 * at + side].wait()
            held_ref[side, :, cut] = raw_ref[side, cut, :].T
        glu = glu_of(normed, held_ref, cut, keep)
        for tile in range(cut.start // LANES, cut.stop // LANES):
            seen = slice(tile * LANES - cut.start, (tile + 1) * LANES - cut.start)
            total = block_conv(glu[:, seen], tile, edge_ref, wide_taps_ref)
            for step, each in enumerate(total):
                sums_ref[tile, 8 * step : 8 * step + 8, :] = each
            lanes = slice(tile * LANES, (tile + 1) * LANES)
            conv = sums_ref[tile, HALO : HALO + rows, :]
            pivot = jnp.sum(conv * valid, axis=0, keepdims=True) / valid_count
            pivot = pivot.astype(BF16).astype(F32)
            pivot_ref[:, lanes] = pivot
            part, there = part_lanes(tile, tiles)
            (soon_ref, later_ref)[part][:, there] = (conv - pivot).astype(BF16)
    base_copy.wait()


def last_block_kernel(
    lengths_ref, rows_ref, vectors_ref, taps_ref, weight_ref, first_sums_ref, pivot_ref, later_ref, _,
    late_ref, tail_ref, spread_ref, store_ref,
    wide_taps_ref, edge_ref, conv_ref, mask_ref, peer_rows_ref, stats_ref, late_sems, conv_sems, stats_sem,
):
    rows, chans = peer_rows_ref.shape
    tiles = chans // LANES
    own = lax.axis_index("tensor")
    peer = 1 - own
    length = lengths_ref[0]
    count = length.astype(F32)
    keep = valid_rows(peer * rows, rows, length)
    for at, place in enumerate((own, peer)):
        valid = valid_rows(place * rows, rows, length).astype(F32)
        mask_ref[at] = jnp.broadcast_to(valid, (rows, LANES))
    first_one = (own == 0).astype(F32)
    last_one = 1.0 - first_one
    clear_ends(edge_ref)
    wide_taps_ref[...] = taps_ref[...].astype(F32)
    last = vectors_ref.shape[0] - 2
    extra = three_parts(vectors_ref[last : last + 1, :])
    extra += three_parts(vectors_ref[last + 1 : last + 2, :])
    extra.append(pivot_ref[...])
    tail_ref[0:rows, :] = later_ref[...]
    means = []
    normed = layer_norm(rows_ref[...], *affine(vectors_ref))
    copies = []
    for cut in cuts(chans, WIDE):
        glu = glu_of(normed, weight_ref, cut, keep)
        for tile in range(cut.start // LANES, cut.stop // LANES):
            seen = slice(tile * LANES - cut.start, (tile + 1) * LANES - cut.start)
            lanes = slice(tile * LANES, (tile + 1) * LANES)
            total = block_conv(glu[:, seen], tile, edge_ref, wide_taps_ref)
            first = [first_sums_ref[tile, 8 * at : 8 * at + 8, :] for at in range(len(total))]
            kept, sent = first[2:-2], total[2:-2]
            for at in range(2):
                kept[at] += total[at - 2] * last_one
                kept[at - 2] += total[at] * first_one
                sent[at] += first[at - 2] * first_one
                sent[at - 2] += first[at] * last_one
            near = jnp.concatenate(kept[:2]) * last_one + jnp.concatenate(kept[-2:]) * first_one
            kept, sent = jnp.concatenate(kept), jnp.concatenate(sent)
            for block, conv in ((KEPT, kept), (SENT, sent)):
                conv_ref[block, tile] = conv
                copies.append(
                    pltpu.make_async_copy(
                        conv_ref.at[block, tile], store_ref.at[block, tile], conv_sems.at[tile, block]
                    )
                )
                copies[-1].start()
            pivot = pivot_ref[:, lanes]
            near = (near - pivot).astype(BF16)
            fold, there = divmod(tile, tiles // FOLDS)
            there = slice(there * LANES, (there + 1) * LANES)
            tail_ref[rows + fold * HALO : rows + (fold + 1) * HALO, there] = near
            mean = jnp.sum(kept * mask_ref[0] + sent * mask_ref[1], axis=0, keepdims=True)
            mean = mean / count
            high = mean.astype(BF16)
            low = (mean - high.astype(F32)).astype(BF16)
            means.append(high.astype(F32))
            peer_rows_ref[:, lanes] = (sent - means[-1]).astype(BF16)
            copies.append(
                pltpu.make_async_copy(
                    peer_rows_ref.at[:, pl.ds(lanes.start, LANES)],
                    late_ref.at[:, pl.ds(lanes.start, LANES)],
                    late_sems.at[tile],
                )
            )
            copies[-1].start()
            mean = means[-1] + low.astype(F32)
            kept, sent = (kept - mean) * mask_ref[0], (sent - mean) * mask_ref[1]
            squares = jnp.sum(kept * kept + sent * sent, axis=0, keepdims=True)
            put_sums(stats_ref, tile, chans, high, low, squares.astype(BF16))
    high = jnp.full((1, LANES), count, F32).astype(BF16)
    low = (jnp.full((1, LANES), count, F32) - high.astype(F32)).astype(BF16)
    stats_ref[0, :, chans + chans // 2 :] = jnp.concatenate([high, low])
    stats = stats_ref[0]
    for at in range(1, stats_ref.shape[0]):
        stats_ref[at] = stats
    copies.append(pltpu.make_async_copy(stats_ref, spread_ref, stats_sem))
    copies[-1].start()
    extra = jnp.concatenate(extra + [jnp.concatenate(means, axis=1)])
    tail_ref[rows + FOLDS * HALO :, :] = folded(extra).astype(BF16)
    for copy in copies:
        copy.wait()


def put_sums(spread_ref, tile, chans, high, low, squares):
    lanes = slice(tile * LANES, (tile + 1) * LANES)
    spread_ref[0, :, lanes] = jnp.concatenate([high, low])
    half = chans // 2
    row, at = divmod(tile * LANES, half)
    spread_ref[0, row : row + 1, chans + at : chans + at + LANES] = squares


def turn_kernel(weight_ref, vectors_ref, store_ref, held_ref, conv_ref, norms_ref, sem):
    parts, chans, _ = held_ref.shape
    copy = pltpu.make_async_copy(store_ref.at[SENT], conv_ref, sem)
    copy.start()
    norms_ref[...] = vectors_ref[vectors_ref.shape[0] - 2 :, :]
    for place in range(parts):
        for cut in cuts(chans, WIDE):
            at = place * chans
            held_ref[place, cut, :] = weight_ref[:, at + cut.start : at + cut.stop].T
    copy.wait()


def peer_vectors(tail_ref):
    first = tail_ref.shape[0] - FOLDS * EXTRA
    parts = tail_ref[first:, :].astype(F32)
    parts = jnp.concatenate([parts[at * EXTRA : (at + 1) * EXTRA] for at in range(FOLDS)], axis=1)
    gain, bias = (parts[at : at + 1] + (parts[at + 1 : at + 2] + parts[at + 2 : at + 3]) for at in (0, 3))
    return gain, bias, parts[6:7], parts[7:8]


def scales(stats_ref, norms_ref, tail_ref, kept):
    chans = norms_ref.shape[1]
    half = chans // 2
    spans = stats_ref.shape[0]
    gain, bias, *pivots = peer_vectors(tail_ref)
    norms = [(norms_ref[0:1, :], norms_ref[1:2, :], 0.0), (gain, bias, pivots[kept])]
    own = lax.axis_index("tensor")
    seen = stats_ref[...].reshape(4 * spans, stats_ref.shape[3])
    picked = lax.broadcasted_iota(jnp.int32, (2 * spans, 4 * spans), 0)
    given = lax.broadcasted_iota(jnp.int32, (2 * spans, 4 * spans), 1)
    place = jnp.where(picked < spans, 1 - own, own)
    first = 4 * lax.rem(picked, spans) + 2 * place
    upper, lower = (given == first).astype(F32), (given == first + 1).astype(F32)

    def pick(rows, lanes):
        return jnp.dot(rows.astype(BF16), seen[:, lanes], preferred_element_type=F32)

    means = pick(upper + lower, slice(0, chans))
    counts = pick(upper + lower, slice(chans + half, chans + half + LANES))[:, 0:1]
    squares = slice(chans, chans + half)
    squares = jnp.concatenate([pick(upper, squares), pick(lower, squares)], axis=1)
    found = []
    for shift, (gain, bias, pivot) in enumerate(norms):
        rows = slice(shift * spans, (shift + 1) * spans)
        weight = counts[rows]
        count = jnp.sum(weight, axis=0, keepdims=True)
        mean = jnp.sum(means[rows] * weight, axis=0, keepdims=True) / count
        off = means[rows] - mean
        var = jnp.sum(squares[rows] + weight * off * off, axis=0, keepdims=True) / count
        found.append((mean - pivot, lax.rsqrt(var + 1e-05) * gain, bias))
    return found


def branch_rows(found, conv_ref, peer_ref, weight_ref):
    own = lax.axis_index("tensor")
    total = None
    for shift in (1, 0):
        mean, scale, bias = found[shift]
        acts = []
        for tile in range(conv_ref.shape[0]):
            lanes = slice(tile * LANES, (tile + 1) * LANES)
            conv = peer_ref[:, lanes].astype(F32) if shift else conv_ref[tile]
            z = (conv - mean[:, lanes]) * scale[:, lanes] + bias[:, lanes]
            acts.append(swish(z).astype(BF16))
        place = 1 - own if shift else own
        term = jnp.dot(jnp.concatenate(acts, axis=1), weight_ref[place], preferred_element_type=F32)
        total = term if total is None else total + term
    return total


def sent_kernel(stats_ref, conv_ref, soon_ref, tail_ref, norms_ref, weight_ref, out_ref, peer_ref):
    rows, wide = soon_ref.shape
    target = pl.multiple_of(jnp.where(lax.axis_index("tensor") == 0, 0, rows - HALO), HALO)
    peer_ref[:, :wide] = soon_ref[...]
    peer_ref[:, wide:] = tail_ref[0:rows, :]
    wide = tail_ref.shape[1]
    for at in range(FOLDS):
        near = tail_ref[rows + at * HALO : rows + (at + 1) * HALO, :]
        peer_ref[pl.ds(target, HALO), at * wide : (at + 1) * wide] = near
    found = scales(stats_ref, norms_ref, tail_ref, 0)
    branch = branch_rows(found, conv_ref, peer_ref, weight_ref)
    out_ref[...] = branch.astype(BF16)


def columns(ref, place, cols):
    return ref.at[:, pl.ds(pl.multiple_of(place * cols, LANES), cols)]


def kept_kernel(
    stats_ref, late_ref, tail_ref, norms_ref, weight_ref, store_ref,
    mine_ref, base_ref, conv_ref, half_ref, sems,
):
    copies = [
        (store_ref.at[KEPT], conv_ref),
        (store_ref.at[HALF], half_ref),
        (store_ref.at[OTHER], base_ref),
    ]
    copies = [pltpu.make_async_copy(*pair, sems.at[at]) for at, pair in enumerate(copies)]
    for copy in copies:
        copy.start()
    found = scales(stats_ref, norms_ref, tail_ref, 1)
    copies[0].wait()
    branch = branch_rows(found, conv_ref, late_ref, weight_ref)
    copies[1].wait()
    for tile in range(conv_ref.shape[0]):
        lanes = slice(tile * LANES, (tile + 1) * LANES)
        mine_ref[:, lanes] = (half_ref[tile] + branch[:, lanes]).astype(BF16)
    copies[2].wait()


def finish_kernel(mine_ref, base_ref, got_ref, out_ref, done_ref, sems):
    own = lax.axis_index("tensor")
    rows, cols = mine_ref.shape
    copies = [pltpu.make_async_copy(mine_ref, columns(out_ref, own, cols), sems.at[0])]
    copies[0].start()
    for tile in range(cols // LANES):
        lanes = slice(tile * LANES, (tile + 1) * LANES)
        done_ref[:, lanes] = (base_ref[tile] + got_ref[:, lanes].astype(F32)).astype(BF16)
    copies.append(pltpu.make_async_copy(done_ref, columns(out_ref, 1 - own, cols), sems.at[1]))
    copies[1].start()
    for copy in copies:
        copy.wait()


def shape(dims, kind):
    return jax.ShapeDtypeStruct(dims, kind)


def call(kernel, outs, in_specs, operands, out_specs=None, scratch=(), name=None, aliases=None, room=32):
    return pl.pallas_call(
        kernel,
        out_shape=tuple(outs),
        in_specs=list(in_specs),
        out_specs=tuple(out_specs or [VMEM] * len(outs)),
        scratch_shapes=list(scratch),
        input_output_aliases=aliases or {},
        compiler_params=pltpu.CompilerParams(vmem_limit_bytes=room * 1024 * 1024),
        name=name,
    )(*operands)


def two_parts(
    devices, frames_in, lengths, ln_gain, ln_bias, glu_weight, conv_kernel, bn_gain, bn_bias, out_weight
):
    _, span, width = frames_in.shape
    chans = glu_weight.shape[1]
    cols = out_weight.shape[0]
    tiles = chans // LANES
    pieces = chans // WIDE

    def swap(value):
        return lax.ppermute(value, "tensor", [(0, 1), (1, 0)])

    frames = swap(frames_in[0])
    vectors = jnp.concatenate([ln_gain, ln_bias, bn_gain, bn_bias]).reshape(-1, chans)
    edge = pltpu.VMEM((tiles, span + 2 * EDGE, LANES), F32)
    wide_taps = pltpu.VMEM((KERNEL, chans), F32)
    dma = pltpu.SemaphoreType.DMA
    reach = shape((tiles, span + 2 * HALO, LANES), F32)
    block = shape((tiles, span, LANES), F32)
    store = shape((BLOCKS,) + block.shape, F32)
    soon, later, first_sums, held, pivot, store_first = call(
        first_block_kernel,
        (
            shape((span, chans - chans // FOLDS), BF16),
            shape((span, chans // FOLDS), BF16),
            reach,
            shape((2, width, chans), BF16),
            shape((1, chans), F32),
            store,
        ),
        [SMEM, HBM, VMEM, VMEM, HBM],
        (lengths, frames_in, vectors, conv_kernel, glu_weight),
        out_specs=(VMEM,) * 5 + (HBM,),
        scratch=(
            pltpu.VMEM((span, width), BF16),
            pltpu.VMEM((2, chans, width), BF16),
            wide_taps,
            edge,
            pltpu.VMEM((2,) + block.shape, F32),
            dma,
            dma((pieces, 2)),
            dma,
        ),
        name="first_block",
        room=48,
    )
    soon = swap(soon)
    late, tail, spread, store_second = call(
        last_block_kernel,
        (
            shape((span, chans), BF16),
            shape((span + FOLDS * (HALO + EXTRA), chans // FOLDS), BF16),
            shape((devices, 2, chans + chans // 2 + LANES), BF16),
            store,
        ),
        [SMEM] + [VMEM] * 7 + [HBM],
        (lengths, frames, vectors, conv_kernel, held, first_sums, pivot, later, store_first),
        out_specs=(HBM, VMEM, HBM, HBM),
        scratch=(
            wide_taps,
            edge,
            pltpu.VMEM((2, tiles, span, LANES), F32),
            pltpu.VMEM((2, span, LANES), F32),
            pltpu.VMEM((span, chans), BF16),
            pltpu.VMEM((devices, 2, chans + chans // 2 + LANES), BF16),
            dma((tiles,)),
            dma((tiles, 2)),
            dma,
        ),
        aliases={8: 3},
        name="last_block",
        room=40,
    )
    spread, soon, out_weight = lax.optimization_barrier((spread, soon, out_weight))
    stats = lax.all_to_all(
        spread, ("dp", "tensor"), split_axis=0, concat_axis=0, tiled=True,
        axis_index_groups=[list(reversed(range(devices)))],
    )
    stats = stats.reshape((devices // 2, 2) + spread.shape[1:])
    tail, late = swap(tail), swap(late)
    weight, sent_conv, norms = call(
        turn_kernel,
        (shape((2, chans, cols), BF16), block, shape((2, chans), F32)),
        [VMEM, VMEM, HBM],
        (out_weight, vectors, store_second),
        scratch=(dma,),
        name="turn",
    )
    (sent,) = call(
        sent_kernel,
        (shape((span, cols), BF16),),
        [VMEM] * 6,
        (stats, sent_conv, soon, tail, norms, weight),
        scratch=(pltpu.VMEM((span, chans), BF16),),
        name="branch_sent",
    )
    got = swap(sent)
    mine, base = call(
        kept_kernel,
        (shape((span, cols), BF16), block),
        [VMEM] * 5 + [HBM],
        (stats, late, tail, norms, weight, store_second),
        scratch=(pltpu.VMEM(block.shape, F32), pltpu.VMEM(block.shape, F32), dma((3,))),
        name="branch_kept",
    )
    (out,) = call(
        finish_kernel,
        (shape((span, width), BF16),),
        [VMEM] * 3,
        (mine, base, got),
        out_specs=(HBM,),
        scratch=(pltpu.VMEM((span, cols), BF16), dma((2,))),
        name="residual",
    )
    return out[None]


def contract_last(left, right):
    return lax.dot_general(
        left, right, (((1,), (1,)), ((), ())), preferred_element_type=F32
    )


def many_parts(
    devices, frames_in, lengths, ln_gain, ln_bias, glu_weight, conv_kernel, bn_gain, bn_bias, out_weight
):
    rows = frames_in[0]
    chans = glu_weight.shape[1]
    normed = layer_norm(rows, ln_gain, ln_bias)
    proj = contract_last(
        lax.all_gather(normed, "tensor", axis=0, tiled=True),
        glu_weight.reshape(2 * chans, rows.shape[1]),
    )
    valid = valid_rows(0, proj.shape[0], lengths[0])
    glu = (proj[:, :chans] * jax.nn.sigmoid(proj[:, chans:])).astype(BF16)
    glu = jnp.where(valid, glu, jnp.zeros_like(glu)).astype(F32)
    padded = jnp.pad(glu, ((15, KERNEL - 16), (0, 0)))
    taps = conv_kernel.astype(F32)
    conv = jnp.zeros_like(glu)
    for tap in range(KERNEL):
        conv = conv + padded[tap : tap + glu.shape[0]] * taps[tap]
    own = lengths[0].astype(F32)
    local = jnp.sum(jnp.where(valid, conv, 0.0), axis=0) / own
    squares = jnp.sum(jnp.where(valid, conv - local, 0.0) ** 2, axis=0)
    count = lax.psum(own, "dp")
    mean = lax.psum(local * own, "dp") / count
    var = lax.psum(squares + own * (local - mean) ** 2, "dp") / count
    z = (conv - mean) * (lax.rsqrt(var + 1e-05) * bn_gain) + bn_bias
    act = lax.all_gather(swish(z).astype(BF16), "tensor", axis=1, tiled=True)
    branch = contract_last(act, out_weight)
    branch = lax.all_to_all(branch, "tensor", split_axis=0, concat_axis=1, tiled=True)
    return (rows.astype(F32) + branch).astype(BF16)[None]


def solution(mesh):
    sizes = dict(mesh.shape)
    body = two_parts if sizes["tensor"] == 2 else many_parts
    body = functools.partial(body, sizes["tensor"] * sizes["dp"])
    return jax.shard_map(
        body,
        mesh=mesh,
        in_specs=(
            P("dp", "tensor", None),
            P("dp"),
            P(),
            P(),
            P(None, "tensor", None),
            P(None, "tensor"),
            P("tensor"),
            P("tensor"),
            P("tensor", None),
        ),
        out_specs=P("dp", "tensor", None),
        check_vma=False,
    )
```

```python
import functools

import jax
import jax.numpy as jnp
from jax import lax
from jax.experimental import pallas as pl
from jax.experimental.pallas import tpu as pltpu
from jax.sharding import PartitionSpec as P

KERNEL = 32
LANES = 128
WIDE = 256
HALO = 16
EDGE = 8
KEPT, SENT, HALF, OTHER, BLOCKS = 0, 1, 2, 3, 72
FOLDS = 3
EXTRA = 8
TAIL = 32
F32 = jnp.float32
BF16 = jnp.bfloat16

VMEM = pl.BlockSpec(memory_space=pltpu.VMEM)
SMEM = pl.BlockSpec(memory_space=pltpu.SMEM)
HBM = pl.BlockSpec(memory_space=pltpu.HBM)


def layer_norm(rows, gain, bias):
    values = rows.astype(F32)
    center = jnp.mean(values, axis=-1, keepdims=True)
    values = values - center
    spread = jnp.mean(values * values, axis=-1, keepdims=True)
    return (values * lax.rsqrt(spread + 1e-05) * gain + bias).astype(BF16)


def swish(z):
    return z * jax.nn.sigmoid(z)


def cuts(width, most):
    return [slice(at, at + most) for at in range(0, width, most)]


def valid_rows(first, rows, length):
    index = first + lax.broadcasted_iota(jnp.int32, (rows, 1), 0)
    return index < length


def glu_of(normed, weight_ref, cut, keep):
    value = jnp.dot(normed, weight_ref[0, :, cut], preferred_element_type=F32)
    gate = jnp.dot(normed, weight_ref[1, :, cut], preferred_element_type=F32)
    glu = (value * jax.nn.sigmoid(gate)).astype(BF16)
    return jnp.where(keep, glu.astype(F32), 0.0)


def three_parts(vector):
    parts = []
    for _ in range(3):
        part = vector.astype(BF16).astype(F32)
        parts.append(part)
        vector = vector - part
    return parts


def affine(vectors_ref):
    rows = [vectors_ref[at : at + 1, :] for at in range(vectors_ref.shape[0] - 2)]
    half = len(rows) // 2
    return jnp.concatenate(rows[:half], axis=1), jnp.concatenate(rows[half:], axis=1)


def clear_ends(edge_ref):
    tiles, total, _ = edge_ref.shape
    zeros = jnp.zeros((EDGE, LANES), F32)
    for tile in range(tiles):
        edge_ref[tile, 0:EDGE, :] = zeros
        edge_ref[tile, total - EDGE : total, :] = zeros


def taps_at(taps_ref, offset, tile):
    cut = slice(tile * LANES, (tile + 1) * LANES)
    taps = {}
    for step in range(5):
        tap = 8 * step + offset - 1
        if 0 <= tap < KERNEL:
            taps[step] = jnp.broadcast_to(taps_ref[tap : tap + 1, cut], (8, LANES))
    return taps


def block_conv(block, tile, edge_ref, taps_ref):
    rows = block.shape[0]
    edge_ref[tile, EDGE : EDGE + rows, :] = block
    count = (rows + 2 * HALO) // 8
    total = [None] * count
    for offset in range(8):
        taps = taps_at(taps_ref, offset, tile)
        for at in range(count + 4):
            start = 8 * at + offset - 2 * HALO
            if start <= -8 or start >= rows:
                continue
            values = edge_ref[tile, EDGE + start : EDGE + start + 8, :]
            for step, tap in taps.items():
                if 0 <= at - step < count:
                    term = values * tap
                    seen = total[at - step]
                    total[at - step] = term if seen is None else seen + term
    return total


def part_lanes(tile, tiles):
    soon = tiles - tiles // FOLDS
    place = tile if tile < soon else tile - soon
    return int(tile >= soon), slice(place * LANES, (place + 1) * LANES)


def folded(rows):
    wide = rows.shape[1] // FOLDS
    return jnp.concatenate([rows[:, at * wide : (at + 1) * wide] for at in range(FOLDS)])


def first_block_kernel(
    lengths_ref, frames_ref, vectors_ref, taps_ref, weight_ref,
    soon_ref, later_ref, sums_ref, held_ref, pivot_ref, store_ref,
    rows_ref, raw_ref, wide_taps_ref, edge_ref, base_ref, rows_sem, weight_sems, base_sem,
):
    rows = rows_ref.shape[0]
    chans = held_ref.shape[2]
    own = lax.axis_index("tensor")
    rows_copy = pltpu.make_async_copy(frames_ref.at[0], rows_ref, rows_sem)
    rows_copy.start()
    pieces = cuts(chans, WIDE)
    copies = []
    for at, cut in enumerate(pieces):
        for side in range(2):
            place = (side, pl.ds(cut.start, WIDE))
            copy = pltpu.make_async_copy(
                weight_ref.at[place], raw_ref.at[place], weight_sems.at[at, side]
            )
            copy.start()
            copies.append(copy)
    clear_ends(edge_ref)
    keep = valid_rows(own * rows, rows, lengths_ref[0])
    wide_taps_ref[...] = taps_ref[...].astype(F32)
    valid = keep.astype(F32)
    valid_count = jnp.maximum(lengths_ref[0] - own * rows, 1)
    valid_count = jnp.minimum(valid_count, rows).astype(F32)
    gain, bias = affine(vectors_ref)
    rows_copy.wait()
    normed = layer_norm(rows_ref[...], gain, bias)
    tiles = chans // LANES
    for shift, half in enumerate((own, 1 - own)):
        for tile in range(tiles):
            lanes = pl.ds(pl.multiple_of((half * tiles + tile) * LANES, LANES), LANES)
            base_ref[shift, tile] = rows_ref[:, lanes].astype(F32)
    base_copy = pltpu.make_async_copy(base_ref, store_ref.at[pl.ds(HALF, 2)], base_sem)
    base_copy.start()
    for at, cut in enumerate(pieces):
        for side in range(2):
            copies[2 * at + side].wait()
            held_ref[side, :, cut] = raw_ref[side, cut, :].T
        glu = glu_of(normed, held_ref, cut, keep)
        for tile in range(cut.start // LANES, cut.stop // LANES):
            seen = slice(tile * LANES - cut.start, (tile + 1) * LANES - cut.start)
            total = block_conv(glu[:, seen], tile, edge_ref, wide_taps_ref)
            for step, each in enumerate(total):
                sums_ref[tile, 8 * step : 8 * step + 8, :] = each
            lanes = slice(tile * LANES, (tile + 1) * LANES)
            conv = sums_ref[tile, HALO : HALO + rows, :]
            pivot = jnp.sum(conv * valid, axis=0, keepdims=True) / valid_count
            pivot = pivot.astype(BF16).astype(F32)
            pivot_ref[:, lanes] = pivot
            part, there = part_lanes(tile, tiles)
            (soon_ref, later_ref)[part][:, there] = (conv - pivot).astype(BF16)
    base_copy.wait()


def last_block_kernel(
    lengths_ref, rows_ref, vectors_ref, taps_ref, weight_ref, first_sums_ref, pivot_ref, later_ref, _,
    late_ref, tail_ref, spread_ref, store_ref,
    wide_taps_ref, edge_ref, conv_ref, mask_ref, peer_rows_ref, stats_ref, late_sems, conv_sems, stats_sem,
):
    rows, chans = peer_rows_ref.shape
    tiles = chans // LANES
    own = lax.axis_index("tensor")
    peer = 1 - own
    length = lengths_ref[0]
    count = length.astype(F32)
    keep = valid_rows(peer * rows, rows, length)
    for at, place in enumerate((own, peer)):
        valid = valid_rows(place * rows, rows, length).astype(F32)
        mask_ref[at] = jnp.broadcast_to(valid, (rows, LANES))
    first_one = (own == 0).astype(F32)
    last_one = 1.0 - first_one
    clear_ends(edge_ref)
    wide_taps_ref[...] = taps_ref[...].astype(F32)
    last = vectors_ref.shape[0] - 2
    extra = three_parts(vectors_ref[last : last + 1, :])
    extra += three_parts(vectors_ref[last + 1 : last + 2, :])
    extra.append(pivot_ref[...])
    tail_ref[0:rows, :] = later_ref[...]
    means = []
    normed = layer_norm(rows_ref[...], *affine(vectors_ref))
    copies = []
    for cut in cuts(chans, WIDE):
        glu = glu_of(normed, weight_ref, cut, keep)
        for tile in range(cut.start // LANES, cut.stop // LANES):
            seen = slice(tile * LANES - cut.start, (tile + 1) * LANES - cut.start)
            lanes = slice(tile * LANES, (tile + 1) * LANES)
            total = block_conv(glu[:, seen], tile, edge_ref, wide_taps_ref)
            first = [first_sums_ref[tile, 8 * at : 8 * at + 8, :] for at in range(len(total))]
            kept, sent = first[2:-2], total[2:-2]
            for at in range(2):
                kept[at] += total[at - 2] * last_one
                kept[at - 2] += total[at] * first_one
                sent[at] += first[at - 2] * first_one
                sent[at - 2] += first[at] * last_one
            near = jnp.concatenate(kept[:2]) * last_one + jnp.concatenate(kept[-2:]) * first_one
            kept, sent = jnp.concatenate(kept), jnp.concatenate(sent)
            for block, conv in ((KEPT, kept), (SENT, sent)):
                conv_ref[block, tile] = conv
                copies.append(
                    pltpu.make_async_copy(
                        conv_ref.at[block, tile], store_ref.at[block, tile], conv_sems.at[tile, block]
                    )
                )
                copies[-1].start()
            pivot = pivot_ref[:, lanes]
            near = (near - pivot).astype(BF16)
            fold, there = divmod(tile, tiles // FOLDS)
            there = slice(there * LANES, (there + 1) * LANES)
            tail_ref[rows + fold * HALO : rows + (fold + 1) * HALO, there] = near
            mean = jnp.sum(kept * mask_ref[0] + sent * mask_ref[1], axis=0, keepdims=True)
            mean = mean / count
            high = mean.astype(BF16)
            low = (mean - high.astype(F32)).astype(BF16)
            means.append(high.astype(F32))
            peer_rows_ref[:, lanes] = (sent - means[-1]).astype(BF16)
            copies.append(
                pltpu.make_async_copy(
                    peer_rows_ref.at[:, pl.ds(lanes.start, LANES)],
                    late_ref.at[:, pl.ds(lanes.start, LANES)],
                    late_sems.at[tile],
                )
            )
            copies[-1].start()
            mean = means[-1] + low.astype(F32)
            kept, sent = (kept - mean) * mask_ref[0], (sent - mean) * mask_ref[1]
            squares = jnp.sum(kept * kept + sent * sent, axis=0, keepdims=True)
            put_sums(stats_ref, tile, chans, high, low, squares.astype(BF16))
    high = jnp.full((1, LANES), count, F32).astype(BF16)
    low = (jnp.full((1, LANES), count, F32) - high.astype(F32)).astype(BF16)
    stats_ref[0, :, chans + chans // 2 :] = jnp.concatenate([high, low])
    stats = stats_ref[0]
    for at in range(1, stats_ref.shape[0]):
        stats_ref[at] = stats
    copies.append(pltpu.make_async_copy(stats_ref, spread_ref, stats_sem))
    copies[-1].start()
    extra = jnp.concatenate(extra + [jnp.concatenate(means, axis=1)])
    extra = folded(extra)
    spare = jnp.zeros((TAIL - extra.shape[0], extra.shape[1]), F32)
    tail_ref[rows + FOLDS * HALO :, :] = jnp.concatenate([extra, spare]).astype(BF16)
    for copy in copies:
        copy.wait()


def put_sums(spread_ref, tile, chans, high, low, squares):
    lanes = slice(tile * LANES, (tile + 1) * LANES)
    spread_ref[0, :, lanes] = jnp.concatenate([high, low])
    half = chans // 2
    row, at = divmod(tile * LANES, half)
    spread_ref[0, row : row + 1, chans + at : chans + at + LANES] = squares


def turn_kernel(weight_ref, vectors_ref, store_ref, held_ref, conv_ref, norms_ref, sem):
    parts, chans, _ = held_ref.shape
    copy = pltpu.make_async_copy(store_ref.at[SENT], conv_ref, sem)
    copy.start()
    norms_ref[...] = vectors_ref[vectors_ref.shape[0] - 2 :, :]
    for place in range(parts):
        for cut in cuts(chans, WIDE):
            at = place * chans
            held_ref[place, cut, :] = weight_ref[:, at + cut.start : at + cut.stop].T
    copy.wait()


def peer_vectors(tail_ref):
    first = tail_ref.shape[0] - TAIL
    parts = tail_ref[first:, :].astype(F32)
    parts = jnp.concatenate([parts[at * EXTRA : (at + 1) * EXTRA] for at in range(FOLDS)], axis=1)
    gain, bias = (parts[at : at + 1] + (parts[at + 1 : at + 2] + parts[at + 2 : at + 3]) for at in (0, 3))
    return gain, bias, parts[6:7], parts[7:8]


def scales(stats_ref, norms_ref, tail_ref, kept):
    chans = norms_ref.shape[1]
    half = chans // 2
    spans = stats_ref.shape[0]
    gain, bias, *pivots = peer_vectors(tail_ref)
    norms = [(norms_ref[0:1, :], norms_ref[1:2, :], 0.0), (gain, bias, pivots[kept])]
    own = lax.axis_index("tensor")
    seen = stats_ref[...].reshape(4 * spans, stats_ref.shape[3])
    picked = lax.broadcasted_iota(jnp.int32, (2 * spans, 4 * spans), 0)
    given = lax.broadcasted_iota(jnp.int32, (2 * spans, 4 * spans), 1)
    place = jnp.where(picked < spans, 1 - own, own)
    first = 4 * lax.rem(picked, spans) + 2 * place
    upper, lower = (given == first).astype(F32), (given == first + 1).astype(F32)

    def pick(rows, lanes):
        return jnp.dot(rows.astype(BF16), seen[:, lanes], preferred_element_type=F32)

    means = pick(upper + lower, slice(0, chans))
    counts = pick(upper + lower, slice(chans + half, chans + half + LANES))[:, 0:1]
    squares = slice(chans, chans + half)
    squares = jnp.concatenate([pick(upper, squares), pick(lower, squares)], axis=1)
    found = []
    for shift, (gain, bias, pivot) in enumerate(norms):
        rows = slice(shift * spans, (shift + 1) * spans)
        weight = counts[rows]
        count = jnp.sum(weight, axis=0, keepdims=True)
        mean = jnp.sum(means[rows] * weight, axis=0, keepdims=True) / count
        off = means[rows] - mean
        var = jnp.sum(squares[rows] + weight * off * off, axis=0, keepdims=True) / count
        found.append((mean - pivot, lax.rsqrt(var + 1e-05) * gain, bias))
    return found


def branch_rows(found, conv_ref, peer_ref, weight_ref):
    own = lax.axis_index("tensor")
    total = None
    for shift in (1, 0):
        mean, scale, bias = found[shift]
        acts = []
        for tile in range(conv_ref.shape[0]):
            lanes = slice(tile * LANES, (tile + 1) * LANES)
            conv = peer_ref[:, lanes].astype(F32) if shift else conv_ref[tile]
            z = (conv - mean[:, lanes]) * scale[:, lanes] + bias[:, lanes]
            acts.append(swish(z).astype(BF16))
        place = 1 - own if shift else own
        term = jnp.dot(jnp.concatenate(acts, axis=1), weight_ref[place], preferred_element_type=F32)
        total = term if total is None else total + term
    return total


def sent_kernel(stats_ref, conv_ref, soon_ref, tail_ref, norms_ref, weight_ref, out_ref, peer_ref):
    rows, wide = soon_ref.shape
    target = pl.multiple_of(jnp.where(lax.axis_index("tensor") == 0, 0, rows - HALO), HALO)
    peer_ref[:, :wide] = soon_ref[...]
    peer_ref[:, wide:] = tail_ref[0:rows, :]
    wide = tail_ref.shape[1]
    for at in range(FOLDS):
        near = tail_ref[rows + at * HALO : rows + (at + 1) * HALO, :]
        peer_ref[pl.ds(target, HALO), at * wide : (at + 1) * wide] = near
    found = scales(stats_ref, norms_ref, tail_ref, 0)
    branch = branch_rows(found, conv_ref, peer_ref, weight_ref)
    out_ref[...] = branch.astype(BF16)


def columns(ref, place, cols):
    return ref.at[:, pl.ds(pl.multiple_of(place * cols, LANES), cols)]


def kept_kernel(
    stats_ref, late_ref, tail_ref, norms_ref, weight_ref, store_ref,
    mine_ref, base_ref, conv_ref, half_ref, sems,
):
    copies = [
        (store_ref.at[KEPT], conv_ref),
        (store_ref.at[HALF], half_ref),
        (store_ref.at[OTHER], base_ref),
    ]
    copies = [pltpu.make_async_copy(*pair, sems.at[at]) for at, pair in enumerate(copies)]
    for copy in copies:
        copy.start()
    found = scales(stats_ref, norms_ref, tail_ref, 1)
    copies[0].wait()
    branch = branch_rows(found, conv_ref, late_ref, weight_ref)
    copies[1].wait()
    for tile in range(conv_ref.shape[0]):
        lanes = slice(tile * LANES, (tile + 1) * LANES)
        mine_ref[:, lanes] = (half_ref[tile] + branch[:, lanes]).astype(BF16)
    copies[2].wait()


def finish_kernel(mine_ref, base_ref, got_ref, out_ref, done_ref, sems):
    own = lax.axis_index("tensor")
    rows, cols = mine_ref.shape
    copies = [pltpu.make_async_copy(mine_ref, columns(out_ref, own, cols), sems.at[0])]
    copies[0].start()
    for tile in range(cols // LANES):
        lanes = slice(tile * LANES, (tile + 1) * LANES)
        done_ref[:, lanes] = (base_ref[tile] + got_ref[:, lanes].astype(F32)).astype(BF16)
    copies.append(pltpu.make_async_copy(done_ref, columns(out_ref, 1 - own, cols), sems.at[1]))
    copies[1].start()
    for copy in copies:
        copy.wait()


def shape(dims, kind):
    return jax.ShapeDtypeStruct(dims, kind)


def call(kernel, outs, in_specs, operands, out_specs=None, scratch=(), name=None, aliases=None, room=32):
    return pl.pallas_call(
        kernel,
        out_shape=tuple(outs),
        in_specs=list(in_specs),
        out_specs=tuple(out_specs or [VMEM] * len(outs)),
        scratch_shapes=list(scratch),
        input_output_aliases=aliases or {},
        compiler_params=pltpu.CompilerParams(vmem_limit_bytes=room * 1024 * 1024),
        name=name,
    )(*operands)


def two_parts(
    devices, frames_in, lengths, ln_gain, ln_bias, glu_weight, conv_kernel, bn_gain, bn_bias, out_weight
):
    _, span, width = frames_in.shape
    chans = glu_weight.shape[1]
    cols = out_weight.shape[0]
    tiles = chans // LANES
    pieces = chans // WIDE

    def swap(value):
        return lax.ppermute(value, "tensor", [(0, 1), (1, 0)])

    frames = swap(frames_in[0])
    vectors = jnp.concatenate([ln_gain, ln_bias, bn_gain, bn_bias]).reshape(-1, chans)
    edge = pltpu.VMEM((tiles, span + 2 * EDGE, LANES), F32)
    wide_taps = pltpu.VMEM((KERNEL, chans), F32)
    dma = pltpu.SemaphoreType.DMA
    reach = shape((tiles, span + 2 * HALO, LANES), F32)
    block = shape((tiles, span, LANES), F32)
    store = shape((BLOCKS,) + block.shape, F32)
    soon, later, first_sums, held, pivot, store_first = call(
        first_block_kernel,
        (
            shape((span, chans - chans // FOLDS), BF16),
            shape((span, chans // FOLDS), BF16),
            reach,
            shape((2, width, chans), BF16),
            shape((1, chans), F32),
            store,
        ),
        [SMEM, HBM, VMEM, VMEM, HBM],
        (lengths, frames_in, vectors, conv_kernel, glu_weight),
        out_specs=(VMEM,) * 5 + (HBM,),
        scratch=(
            pltpu.VMEM((span, width), BF16),
            pltpu.VMEM((2, chans, width), BF16),
            wide_taps,
            edge,
            pltpu.VMEM((2,) + block.shape, F32),
            dma,
            dma((pieces, 2)),
            dma,
        ),
        name="first_block",
        room=48,
    )
    soon = swap(soon)
    late, tail, spread, store_second = call(
        last_block_kernel,
        (
            shape((span, chans), BF16),
            shape((span + FOLDS * HALO + TAIL, chans // FOLDS), BF16),
            shape((devices, 2, chans + chans // 2 + LANES), BF16),
            store,
        ),
        [SMEM] + [VMEM] * 7 + [HBM],
        (lengths, frames, vectors, conv_kernel, held, first_sums, pivot, later, store_first),
        out_specs=(HBM, VMEM, HBM, HBM),
        scratch=(
            wide_taps,
            edge,
            pltpu.VMEM((2, tiles, span, LANES), F32),
            pltpu.VMEM((2, span, LANES), F32),
            pltpu.VMEM((span, chans), BF16),
            pltpu.VMEM((devices, 2, chans + chans // 2 + LANES), BF16),
            dma((tiles,)),
            dma((tiles, 2)),
            dma,
        ),
        aliases={8: 3},
        name="last_block",
        room=40,
    )
    spread, soon, out_weight = lax.optimization_barrier((spread, soon, out_weight))
    stats = lax.all_to_all(
        spread, ("dp", "tensor"), split_axis=0, concat_axis=0, tiled=True,
        axis_index_groups=[list(reversed(range(devices)))],
    )
    stats = stats.reshape((devices // 2, 2) + spread.shape[1:])
    tail, late = swap(tail), swap(late)
    weight, sent_conv, norms = call(
        turn_kernel,
        (shape((2, chans, cols), BF16), block, shape((2, chans), F32)),
        [VMEM, VMEM, HBM],
        (out_weight, vectors, store_second),
        scratch=(dma,),
        name="turn",
    )
    (sent,) = call(
        sent_kernel,
        (shape((span, cols), BF16),),
        [VMEM] * 6,
        (stats, sent_conv, soon, tail, norms, weight),
        scratch=(pltpu.VMEM((span, chans), BF16),),
        name="branch_sent",
    )
    got = swap(sent)
    mine, base = call(
        kept_kernel,
        (shape((span, cols), BF16), block),
        [VMEM] * 5 + [HBM],
        (stats, late, tail, norms, weight, store_second),
        scratch=(pltpu.VMEM(block.shape, F32), pltpu.VMEM(block.shape, F32), dma((3,))),
        name="branch_kept",
    )
    (out,) = call(
        finish_kernel,
        (shape((span, width), BF16),),
        [VMEM] * 3,
        (mine, base, got),
        out_specs=(HBM,),
        scratch=(pltpu.VMEM((span, cols), BF16), dma((2,))),
        name="residual",
    )
    return out[None]


def contract_last(left, right):
    return lax.dot_general(
        left, right, (((1,), (1,)), ((), ())), preferred_element_type=F32
    )


def many_parts(
    devices, frames_in, lengths, ln_gain, ln_bias, glu_weight, conv_kernel, bn_gain, bn_bias, out_weight
):
    rows = frames_in[0]
    chans = glu_weight.shape[1]
    normed = layer_norm(rows, ln_gain, ln_bias)
    proj = contract_last(
        lax.all_gather(normed, "tensor", axis=0, tiled=True),
        glu_weight.reshape(2 * chans, rows.shape[1]),
    )
    valid = valid_rows(0, proj.shape[0], lengths[0])
    glu = (proj[:, :chans] * jax.nn.sigmoid(proj[:, chans:])).astype(BF16)
    glu = jnp.where(valid, glu, jnp.zeros_like(glu)).astype(F32)
    padded = jnp.pad(glu, ((15, KERNEL - 16), (0, 0)))
    taps = conv_kernel.astype(F32)
    conv = jnp.zeros_like(glu)
    for tap in range(KERNEL):
        conv = conv + padded[tap : tap + glu.shape[0]] * taps[tap]
    own = lengths[0].astype(F32)
    local = jnp.sum(jnp.where(valid, conv, 0.0), axis=0) / own
    squares = jnp.sum(jnp.where(valid, conv - local, 0.0) ** 2, axis=0)
    count = lax.psum(own, "dp")
    mean = lax.psum(local * own, "dp") / count
    var = lax.psum(squares + own * (local - mean) ** 2, "dp") / count
    z = (conv - mean) * (lax.rsqrt(var + 1e-05) * bn_gain) + bn_bias
    act = lax.all_gather(swish(z).astype(BF16), "tensor", axis=1, tiled=True)
    branch = contract_last(act, out_weight)
    branch = lax.all_to_all(branch, "tensor", split_axis=0, concat_axis=1, tiled=True)
    return (rows.astype(F32) + branch).astype(BF16)[None]


def solution(mesh):
    sizes = dict(mesh.shape)
    body = two_parts if sizes["tensor"] == 2 else many_parts
    body = functools.partial(body, sizes["tensor"] * sizes["dp"])
    return jax.shard_map(
        body,
        mesh=mesh,
        in_specs=(
            P("dp", "tensor", None),
            P("dp"),
            P(),
            P(),
            P(None, "tensor", None),
            P(None, "tensor"),
            P("tensor"),
            P("tensor"),
            P("tensor", None),
        ),
        out_specs=P("dp", "tensor", None),
        check_vma=False,
    )
```
